256 devices in a mesh: seq: 32 (over y, x, core), exp: 8 (over z).
Axes of the slice: x: 4, y: 4, z: 8, core: 2. Of those that a mesh axis runs over, the one named last changes fastest.
Arguments:
- tokens: bfloat16 [4096, 4096], P('seq'), may hold values from -6 to 6
- cotangent: bfloat16 [4096, 4096], P('seq'), may hold values from -6 to 6
- expert_ids: int32 [4096, 2], P('seq'), may hold values from 0 to 15, all different within a row; in each aligned block of 128 rows (0 to 127, 128 to 255, ...) at most 24 rows name the same one
- ada_shift: float32 [4096], replicated, may hold values from -3 to 3
- ada_scale: float32 [4096], replicated, may hold values from -1.8 to 1.8
- ada_gate: float32 [4096], replicated, may hold values from 0.3 to 1.5
- router_weight: bfloat16 [4096, 16], replicated, may hold values from -0.09375 to 0.09375
- gate_blocks: bfloat16 [256, 4096, 128], P(('seq', 'exp')), may hold values from -0.09375 to 0.09375
- up_blocks: bfloat16 [256, 4096, 128], P(('seq', 'exp')), may hold values from -0.09375 to 0.09375
- down_blocks: bfloat16 [256, 128, 4096], P(('seq', 'exp')), may hold values from -0.125 to 0.125
Outputs:
- grad_input: float32 [4096, 4096], P('seq', 'exp')
- grad_router: float32 [4096, 16], P('exp')
- grad_gate: bfloat16 [256, 4096, 128], P(('seq', 'exp'))
- grad_up: bfloat16 [256, 4096, 128], P(('seq', 'exp'))
- grad_down: bfloat16 [256, 128, 4096], P(('seq', 'exp'))
The draws below stay inside these ranges and needn't reach their ends.
Inputs may be any that keep to these rules, and one draw needn't show every extreme that they name: `expert_ids`: each row names two different experts; among the 128 rows of one index of seq no expert is named more than 24 times, a bound that some block reaches.
All inputs are finite; a program needn't handle non-finite values.
Results may differ from the reference program's by a relative error of at most 0.0082.
Values may be sent and summed in bfloat16 or wider, within the bound.
A program may use at most 128 MiB of HBM per device.

```python
import math
import jax
import jax.numpy as jnp
import numpy as np
from jax import lax

D = 4096
FF = 2048
EXPERTS = 16
TOP = 2
TOK_DEV = 128
TOKENS = 4096
CAP = 24
PIECES = 16
HID_DEV = 128
BLOCKS = 256
N_SEQ = 32


def block_scale(stream_key, shape, split, smallest, largest):
    gain, own = 1.0, jax.random.fold_in(stream_key, 6)
    for axis_at, shards_of in split:
        draws = jnp.exp(jax.random.uniform(jax.random.fold_in(own, axis_at), (shards_of,), jnp.float32, smallest / len(split), largest / len(split)))
        gain = gain * jnp.repeat(draws, shape[axis_at] // shards_of).reshape([-1 if axis == axis_at else 1 for axis in range(len(shape))])
    return gain


def shared_out(stream_key, own, number, rows, number_of, top, reach, skew):
    order = jax.random.permutation(stream_key, number_of)
    crowded, ordinary = portions_of(number_of, rows * top, reach, skew, True), portions_of(number_of, rows * top, reach, skew, False)
    places = jnp.arange(number_of)

    def named(lengths, offset_by):
        used = int((lengths > 0).sum())
        fixed = max(1, used // 4)
        moved = fixed + (places - fixed + offset_by * (used - fixed)) % max(1, number_of - fixed)
        return jnp.zeros((number_of,), jnp.int32).at[order[jnp.where(places < fixed, places, moved)]].set(jnp.asarray(lengths, jnp.int32))

    lengths = jnp.where(number % 4 == 0, named(crowded, number // 4), named(ordinary, number - number // 4 - 1))
    mixed = jax.random.permutation(jax.random.fold_in(own, 3), number_of)
    source_of, sink = mixed[0:number_of // 2 * 2:2], mixed[1:number_of // 2 * 2:2]
    margin = jnp.minimum(lengths[source_of] - 1, reach - lengths[sink]) // 2
    margin = jnp.where((source_of == order[0]) | (sink == order[0]) | (lengths[sink] == 0), 0, jnp.maximum(margin, 0))
    moved = jax.random.randint(jax.random.fold_in(own, 4), (number_of // 2,), 0, 1 << 20) % (margin + 1)
    lengths = lengths.at[source_of].add(-moved).at[sink].add(moved)
    members = jnp.searchsorted(jnp.cumsum(lengths), jnp.arange(rows * top), side="right").astype(jnp.int32)
    table = members.reshape(top, rows).T
    table = table[jax.random.permutation(jax.random.fold_in(own, 1), rows)]
    offset_by = jax.random.randint(jax.random.fold_in(own, 2), (rows, 1), 0, top)
    return jnp.take_along_axis(table, (jnp.arange(top)[None, :] + offset_by) % top, axis=1)


def portions_of(amount, total, bound, skew, full):
    loads = [(1 << 20) // math.isqrt(rank ** skew) + 1 for rank in range(1, amount + 1)]
    largest = bound if full else min(bound, max(-(-total // amount), total * loads[0] // sum(loads)))
    least = 1 if total - largest >= amount - 1 else 0
    holding, spare = [largest] + [least] * (amount - 1), total - largest - least * (amount - 1)
    while spare > 0:
        free = [i for i in range(1, amount) if holding[i] < largest] or [i for i in range(1, amount) if holding[i] < bound]
        mass, budget = sum([loads[i] for i in free]), spare
        for i in free:
            extra = min(bound - holding[i], max(1, budget * loads[i] // mass), spare)
            holding[i] = holding[i] + extra
            spare = spare - extra
    return np.array(holding)


def bell_draw(own_key, shape, spread, limit, shards=(), kind=jnp.bfloat16):
    entries = spread * jax.random.normal(own_key, shape, jnp.float32)
    if shards:
        entries = entries * block_scale(own_key, shape, shards, -0.22, 0.18)
    return jnp.clip(entries, -limit, limit).astype(kind)


def setup_inputs(seed: int = 0) -> dict:
    splits = jax.random.split(jax.random.key(seed), 11)
    tokens = bell_draw(splits[0], (TOKENS, D), 1.0, 6.0, ((0, 32),))
    cotangent = bell_draw(splits[1], (TOKENS, D), 1.0, 6.0, ((0, 32),))
    expert_ids_keys = jax.random.split(jax.random.fold_in(splits[2], 1), TOKENS // TOK_DEV)
    expert_ids_turns = jax.random.permutation(jax.random.fold_in(splits[2], 3), TOKENS // TOK_DEV)
    expert_ids = jax.vmap(lambda own, number: shared_out(jax.random.fold_in(splits[2], 2), own, number, TOK_DEV, EXPERTS, TOP, CAP, 2))(expert_ids_keys, expert_ids_turns).reshape((TOKENS, TOP))
    ada_shift = bell_draw(splits[3], (D,), 0.5, 3.0, (), jnp.float32)
    ada_scale = bell_draw(splits[4], (D,), 0.5, 1.8, (), jnp.float32)
    ada_gate = jnp.clip(jax.random.uniform(splits[5], (D,), jnp.float32, 0.3, 1.5), 0.3, 1.5)
    router_weight = bell_draw(splits[6], (D, EXPERTS), D ** -0.5, 0.09375)
    gate_blocks = bell_draw(splits[7], (BLOCKS, D, HID_DEV), D ** -0.5, 0.09375, ((0, 256),))
    up_blocks = bell_draw(splits[8], (BLOCKS, D, HID_DEV), D ** -0.5, 0.09375, ((0, 256),))
    down_blocks = bell_draw(splits[9], (BLOCKS, HID_DEV, D), FF ** -0.5, 0.125, ((0, 256),))
    return {"tokens": tokens, "cotangent": cotangent, "expert_ids": expert_ids, "ada_shift": ada_shift, "ada_scale": ada_scale, "ada_gate": ada_gate, "router_weight": router_weight, "gate_blocks": gate_blocks, "up_blocks": up_blocks, "down_blocks": down_blocks}


EPSILON = 1e-06

def normalize(tokens, ada_shift, ada_scale):
    values = tokens.astype(jnp.float32)
    center = values - lax.optimization_barrier(jnp.mean(values, axis=-1, keepdims=True))
    inv_std = lax.rsqrt(lax.optimization_barrier(jnp.mean(center * center, axis=-1, keepdims=True)) + EPSILON)
    normed = center * inv_std
    modulated = (normed * (1.0 + ada_scale) + ada_shift).astype(jnp.bfloat16)
    return (normed, inv_std, modulated)

def expert_backward(rows_z, rows_dy, rows_share, gate_w, up_w, down_w):
    gate_pre = jnp.dot(rows_z, gate_w, preferred_element_type=jnp.float32)
    up_pre = jnp.dot(rows_z, up_w, preferred_element_type=jnp.float32)
    gate_sig = jax.nn.sigmoid(gate_pre)
    active = gate_pre * gate_sig
    hidden = active * up_pre
    back_hidden = lax.dot_general(rows_dy, down_w, (((1,), (1,)), ((), ())), preferred_element_type=jnp.float32)
    weight_terms = lax.optimization_barrier(jnp.sum(hidden * back_hidden, axis=-1))
    weight_col = rows_share.astype(jnp.float32)[:, None]
    scaled = weight_col * back_hidden
    grad_up_pre = (scaled * active).astype(jnp.bfloat16)
    grad_gate_pre = (scaled * up_pre * gate_sig * (1.0 + gate_pre * (1.0 - gate_sig))).astype(jnp.bfloat16)
    grad_rows = lax.dot_general(grad_gate_pre, gate_w, (((1,), (1,)), ((), ())), preferred_element_type=jnp.float32)
    grad_rows = grad_rows + lax.dot_general(grad_up_pre, up_w, (((1,), (1,)), ((), ())), preferred_element_type=jnp.float32)
    grad_gate = lax.dot_general(rows_z, grad_gate_pre, (((0,), (0,)), ((), ())), preferred_element_type=jnp.float32)
    grad_up = lax.dot_general(rows_z, grad_up_pre, (((0,), (0,)), ((), ())), preferred_element_type=jnp.float32)
    hidden_b = hidden.astype(jnp.bfloat16)
    weighted_dy = (weight_col * rows_dy.astype(jnp.float32)).astype(jnp.bfloat16)
    grad_down = lax.dot_general(hidden_b, weighted_dy, (((0,), (0,)), ((), ())), preferred_element_type=jnp.float32)
    return (grad_rows, weight_terms, grad_gate, grad_up, grad_down)

def reference(tokens, cotangent, expert_ids, ada_shift, ada_scale, ada_gate, router_weight, gate_blocks, up_blocks, down_blocks):
    normed, inv_std, modulated = normalize(tokens, ada_shift, ada_scale)
    logits = jnp.dot(modulated, router_weight, preferred_element_type=jnp.float32)
    scores = jax.nn.sigmoid(logits)
    chosen = (expert_ids[:, :, None] == jnp.arange(EXPERTS, dtype=jnp.int32)[None, None, :]).astype(jnp.float32)
    picked = jnp.einsum('tke,te->tk', chosen, scores)
    score_sum = lax.optimization_barrier(jnp.sum(picked, axis=-1, keepdims=True))
    shares = picked / score_sum
    share_b = lax.optimization_barrier(shares.astype(jnp.bfloat16))
    expert_share = jnp.einsum('tke,tk->te', chosen, share_b.astype(jnp.float32))
    out_grad = (ada_gate * cotangent.astype(jnp.float32)).astype(jnp.bfloat16)
    gate_full = gate_blocks.reshape(EXPERTS, PIECES, D, HID_DEV).transpose(0, 2, 1, 3).reshape(EXPERTS, D, FF)
    up_full = up_blocks.reshape(EXPERTS, PIECES, D, HID_DEV).transpose(0, 2, 1, 3).reshape(EXPERTS, D, FF)
    down_full = down_blocks.reshape(EXPERTS, FF, D)
    routed = lax.optimization_barrier(jnp.sum(chosen, axis=1))
    row_limit = N_SEQ * CAP

    def one_expert(state_pair, inputs):
        grad_acc, term_acc = state_pair
        expert, gate_w, up_w, down_w = inputs
        hit_col = lax.dynamic_index_in_dim(routed, expert, 1, keepdims=False)
        row_index = jnp.nonzero(hit_col > 0, size=row_limit, fill_value=0)[0].astype(jnp.int32)
        valid = (jnp.arange(row_limit, dtype=jnp.int32).astype(jnp.float32) < jnp.sum(hit_col)).astype(jnp.float32)
        rows_z = modulated[row_index]
        rows_dy = (out_grad[row_index].astype(jnp.float32) * valid[:, None]).astype(jnp.bfloat16)
        share_col = lax.dynamic_index_in_dim(expert_share, expert, 1, keepdims=False)
        rows_share = (share_col[row_index] * valid).astype(jnp.bfloat16)
        grad_rows, weight_terms, grad_g, grad_u, grad_d = expert_backward(rows_z, rows_dy, rows_share, gate_w, up_w, down_w)
        grad_acc = grad_acc.at[row_index].add(grad_rows * valid[:, None])
        expert_hit = (jnp.arange(EXPERTS, dtype=jnp.int32) == expert).astype(jnp.float32)
        term_acc = term_acc.at[row_index].add((weight_terms * valid)[:, None] * expert_hit[None, :])
        return ((grad_acc, term_acc), (grad_g.astype(jnp.bfloat16), grad_u.astype(jnp.bfloat16), grad_d.astype(jnp.bfloat16)))
    start_state = (jnp.zeros((TOKENS, D), jnp.float32), jnp.zeros((TOKENS, EXPERTS), jnp.float32))
    (expert_grad, weight_grad), (gate_grads, up_grads, down_grads) = lax.scan(one_expert, start_state, (jnp.arange(EXPERTS, dtype=jnp.int32), gate_full, up_full, down_full))
    choice_grad = jnp.einsum('tke,te->tk', chosen, weight_grad)
    mean_grad = lax.optimization_barrier(jnp.sum(shares * choice_grad, axis=-1, keepdims=True))
    pick_grad = (choice_grad - mean_grad) / score_sum * picked * (1.0 - picked)
    logit_grad = jnp.einsum('tke,tk->te', chosen, pick_grad)
    router_f = router_weight.astype(jnp.float32)
    mod_grad = expert_grad + jnp.dot(logit_grad, router_f.T, precision=lax.Precision.HIGHEST)
    grad_router = jnp.dot(modulated.astype(jnp.float32).T, logit_grad, precision=lax.Precision.HIGHEST)
    norm_grad = mod_grad * (1.0 + ada_scale)
    grad_total = lax.optimization_barrier(jnp.sum(norm_grad, axis=-1, keepdims=True))
    grad_cross = lax.optimization_barrier(jnp.sum(norm_grad * normed, axis=-1, keepdims=True))
    grad_input = inv_std * (norm_grad - grad_total / D - normed * (grad_cross / D))
    grad_gate = gate_grads.reshape(EXPERTS, D, PIECES, HID_DEV).transpose(0, 2, 1, 3).reshape(BLOCKS, D, HID_DEV)
    grad_up = up_grads.reshape(EXPERTS, D, PIECES, HID_DEV).transpose(0, 2, 1, 3).reshape(BLOCKS, D, HID_DEV)
    grad_down = down_grads.reshape(BLOCKS, HID_DEV, D)
    return (grad_input, grad_router, grad_gate, grad_up, grad_down)
```

```python
import functools
import math

import jax
import jax.numpy as jnp
from jax import lax
from jax.experimental import pallas as pl
from jax.experimental.pallas import tpu as pltpu
from jax.sharding import PartitionSpec as P

CAP = 24
EPSILON = 1e-06
MESH = pl.DeviceIdType.MESH
F32 = jnp.float32
BF16 = jnp.bfloat16
NT = (((1,), (1,)), ((), ()))
TN = (((0,), (0,)), ((), ()))


def dot(a, b, dims=(((1,), (0,)), ((), ()))):
    return lax.dot_general(a, b, dims, preferred_element_type=F32)


def expert_kernel(
    n,
    zn,
    send,
    gate,
    up,
    down,
    back_out,
    terms_out,
    gate_out,
    up_out,
    down_out,
    recv,
    w_gate,
    w_up,
    w_down,
    rows_z,
    rows_wdy,
    d_gu,
    hid,
    hr,
    g_acc,
    u_acc,
    r_acc,
    t_send,
    t_recv,
    b_send,
    b_recv,
    term_own,
    term_z,
    term_sum,
    term_b,
    gu_own,
    gu_send,
    gu_recv,
    dn_own,
    dn_send,
    dn_recv,
    w_local,
    w_ssem,
    w_rsem,
    d_ssem,
    d_rsem,
    t_ssem,
    t_rsem,
    b_ssem,
    b_rsem,
    tz_ssem,
    tz_rsem,
    tb_ssem,
    tb_rsem,
    g_ssem,
    g_rsem,
    h_ssem,
    h_rsem,
):
    slots = n * n
    width = rows_z.shape[1]
    group = n * CAP
    hidden = w_gate.shape[2]
    kb = 512
    nb = width // kb
    cols_z = width // zn
    half = cols_z // 2
    seq = lax.axis_index("seq")
    z = lax.axis_index("exp")
    core = lax.rem(seq, 2)
    chip = seq // 2
    cy, cx = chip // n, lax.rem(chip, n)

    def offset(slot):
        dy = lax.rem(slot, n)
        dx = lax.rem(dy + slot // n, n)
        return dy, dx

    def target(slot):
        dy, dx = offset(slot)
        return (2 * (lax.rem(cy + dy, n) * n + lax.rem(cx + dx, n)) + core, z)

    def source(slot):
        dy, dx = offset(slot)
        return (2 * (lax.rem(cy - dy + n, n) * n + lax.rem(cx - dx + n, n)) + core, z)

    def z_peer(step):
        return (seq, lax.rem(z + step, zn))

    sibling = (seq + 1 - 2 * core, z)

    def remote(src, dst, ssem, rsem, dev):
        return pltpu.make_async_remote_copy(
            src_ref=src, dst_ref=dst, send_sem=ssem, recv_sem=rsem, device_id=dev, device_id_type=MESH
        )

    def send_copy(slot):
        return remote(send.at[slot], recv.at[slot], d_ssem.at[slot], d_rsem.at[slot], target(slot))

    def t_copy(g, step):
        return remote(
            t_send.at[g, step], t_recv.at[g, step], t_ssem.at[g, step], t_rsem.at[g, step], z_peer(step)
        )

    def b_copy(slot):
        return remote(b_send.at[slot], b_recv.at[slot], b_ssem.at[slot], b_rsem.at[slot], source(slot))

    def tz_copy(step):
        return remote(term_own, term_z.at[step], tz_ssem.at[step], tz_rsem.at[step], z_peer(step))

    def tb_copy(slot):
        return remote(term_sum, term_b.at[slot], tb_ssem.at[slot], tb_rsem.at[slot], source(slot))

    def gu_copy(b):
        return remote(gu_send.at[b], gu_recv.at[b], g_ssem.at[b], g_rsem.at[b], sibling)

    def dn_copy(b):
        return remote(dn_send.at[b], dn_recv.at[b], h_ssem.at[b], h_rsem.at[b], sibling)

    weights = ((gate, w_gate), (up, w_up), (down, w_down))

    def w_copy(i):
        hbm, vmem = weights[i]
        return remote(hbm.at[0], vmem.at[1], w_ssem.at[i], w_rsem.at[i], sibling)

    def w_copy_local(i):
        hbm, vmem = weights[i]
        return pltpu.make_async_copy(hbm.at[0], vmem.at[0], w_local.at[i])

    def loop(lo, hi, body):
        def step(i, carry):
            body(i)
            return carry

        lax.fori_loop(lo, hi, step, 0)

    barrier = pltpu.get_barrier_semaphore()
    loop(
        1,
        slots,
        lambda k: pl.semaphore_signal(barrier, inc=1, device_id=target(k), device_id_type=MESH),
    )
    loop(
        1,
        zn,
        lambda j: pl.semaphore_signal(barrier, inc=1, device_id=z_peer(j), device_id_type=MESH),
    )
    pl.semaphore_signal(barrier, inc=1, device_id=sibling, device_id_type=MESH)
    own = pltpu.make_async_copy(send.at[0], recv.at[0], w_local.at[3])
    own.start()
    for i in range(3):
        w_copy_local(i).start()
    pl.semaphore_wait(barrier, slots + zn - 1)

    for i in range(3):
        w_copy(i).start()
    loop(1, slots, lambda k: send_copy(k).start())
    hr[...] = jnp.zeros_like(hr)
    own.wait()
    for i in range(3):
        w_copy_local(i).wait()
        w_copy(i).wait()

    def wait_group(g):
        def one(i):
            slot = g * n + i

            @pl.when(slot > 0)
            def _():
                send_copy(slot).wait_recv()

        loop(0, n, one)

    def reduce_group(g):
        loop(1, zn, lambda j: t_copy(g, j).wait_recv())
        for i in range(n):
            slot = g * n + i
            parts = []
            for lo in (0, half):
                part = t_recv[g, :, :, lo : lo + half].astype(F32)[:, i * CAP : (i + 1) * CAP, :]
                parts.append(jnp.sum(part, axis=0))
            packed = jnp.concatenate(parts, axis=0).astype(BF16)
            if i > 0:
                b_send[slot] = packed
                b_copy(slot).start()
            else:

                @pl.when(slot > 0)
                def _():
                    b_send[slot] = packed
                    b_copy(slot).start()

                @pl.when(slot == 0)
                def _():
                    b_recv[0] = packed

    def compute_group(g):
        wait_group(g)
        rows = pl.ds(pl.multiple_of(g * group, group), group)
        share = jnp.concatenate(
            [recv[g * n + i, :, width : width + 128].astype(F32)[CAP:, :1] for i in range(n)], axis=0
        )
        g_acc[...] = jnp.zeros_like(g_acc)
        u_acc[...] = jnp.zeros_like(u_acc)
        r_acc[...] = jnp.zeros_like(r_acc)

        def forward(b):
            cols = pl.ds(pl.multiple_of(b * kb, kb), kb)
            tiles = [recv[g * n + i, :, cols].astype(F32) for i in range(n)]
            zb = jnp.concatenate([t[:CAP] for t in tiles], axis=0).astype(BF16)
            dyf = jnp.concatenate([t[CAP:] for t in tiles], axis=0)
            rows_z[rows, cols] = zb
            rows_wdy[rows, cols] = (share * dyf).astype(BF16)
            g_acc[...] += dot(zb, jnp.concatenate([w_gate[0, cols, :], w_gate[1, cols, :]], axis=1))
            u_acc[...] += dot(zb, jnp.concatenate([w_up[0, cols, :], w_up[1, cols, :]], axis=1))
            wd = jnp.concatenate([w_down[0, :, cols], w_down[1, :, cols]], axis=0)
            r_acc[...] += dot(dyf.astype(BF16), wd, NT)

        loop(0, nb, forward)
        gv, uv, rv = g_acc[...], u_acc[...], r_acc[...]
        sig = jax.nn.sigmoid(gv)
        act = gv * sig
        hv = act * uv
        prod = hv * rv
        hr[rows, :] = prod[:, :hidden] + prod[:, hidden:]
        scaled = share * rv
        du = (scaled * act).astype(BF16)
        dg = (scaled * uv * sig * (1.0 + gv * (1.0 - sig))).astype(BF16)
        d_gu[rows, :] = jnp.concatenate(
            [dg[:, :hidden], du[:, :hidden], dg[:, hidden:], du[:, hidden:]], axis=1
        )
        hid[rows, :] = hv.astype(BF16)

        def backward(step):
            dest = lax.rem(z + step, zn)
            wrows = pl.ds(pl.multiple_of(dest * cols_z, cols_z), cols_z)
            wg = jnp.concatenate([w_gate[0, wrows, :], w_gate[1, wrows, :]], axis=1)
            wu = jnp.concatenate([w_up[0, wrows, :], w_up[1, wrows, :]], axis=1)
            part = (dot(dg, wg, NT) + dot(du, wu, NT)).astype(BF16)

            @pl.when(step > 0)
            def _():
                t_send[g, step] = part
                t_copy(g, step).start()

            @pl.when(step == 0)
            def _():
                t_recv[g, 0] = part

        loop(0, zn, lambda i: backward(zn - 1 - i))

    def group_step(g):
        compute_group(g)

        @pl.when(g > 0)
        def _():
            reduce_group(g - 1)

    loop(0, n, group_step)

    nt = hr.shape[0] // 128
    term_own[...] = jnp.zeros_like(term_own)
    for i in range(nt):
        tile = hr[128 * i : 128 * (i + 1), :]
        term_own[i : i + 1, :] = jnp.sum(tile.T, axis=0, keepdims=True)
    loop(1, zn, lambda j: tz_copy(j).start())

    def weight_grads(b):
        cols = pl.ds(pl.multiple_of(b * kb, kb), kb)
        gu = dot(rows_z[:, cols], d_gu[...], TN)
        gu_own[b] = gu[:, : 2 * hidden]
        gu_send[b] = gu[:, 2 * hidden :].astype(BF16)
        gu_copy(b).start()
        dn = dot(hid[...], rows_wdy[:, cols], TN)
        dn_own[b] = dn[:hidden]
        dn_send[b] = dn[hidden:].astype(BF16)
        dn_copy(b).start()

    loop(0, nb // 2, weight_grads)
    loop(1, zn, lambda j: tz_copy(j).wait_recv())
    total = term_own[...]
    for j in range(1, zn):
        total = total + term_z[j]
    term_sum[...] = total
    loop(1, slots, lambda k: tb_copy(k).start())
    loop(nb // 2, nb, weight_grads)
    reduce_group(n - 1)

    def finish(b):
        gu_copy(b).wait_recv()
        dn_copy(b).wait_recv()
        cols = pl.ds(pl.multiple_of(b * kb, kb), kb)
        gu = gu_own[b] + gu_recv[b].astype(F32)
        gate_out[0, cols, :] = gu[:, :hidden].astype(BF16)
        up_out[0, cols, :] = gu[:, hidden:].astype(BF16)
        down_out[0, :, cols] = (dn_own[b] + dn_recv[b].astype(F32)).astype(BF16)

    loop(0, nb, finish)

    loop(1, slots, lambda k: tb_copy(k).wait_recv())
    flat = lax.broadcasted_iota(jnp.int32, (8, 128), 0) * 128 + lax.broadcasted_iota(
        jnp.int32, (8, 128), 1
    )
    terms = jnp.where(flat < CAP, term_sum[...], 0.0)
    for k in range(1, slots):
        terms = jnp.where((flat >= k * CAP) & (flat < (k + 1) * CAP), term_b[k], terms)
    terms_out[...] = terms

    loop(1, slots, lambda k: b_copy(k).wait_recv())
    back_out[...] = b_recv[...]

    def drain_slot(k):
        send_copy(k).wait_send()
        b_copy(k).wait_send()
        tb_copy(k).wait_send()

    loop(1, slots, drain_slot)

    def drain_z(j):
        tz_copy(j).wait_send()
        loop(0, n, lambda g: t_copy(g, j).wait_send())

    loop(1, zn, drain_z)

    def drain_b(b):
        gu_copy(b).wait_send()
        dn_copy(b).wait_send()

    loop(0, nb, drain_b)


def run_experts(n, zn, send, gate, up, down):
    slots = n * n
    width, hidden = gate.shape[1], gate.shape[2]
    rows = slots * CAP
    cols_z = width // zn
    nb = width // 512
    nt = -(-rows // 128)
    dma = pltpu.SemaphoreType.DMA
    vm = pltpu.VMEM
    scratch = [
        vm(send.shape, BF16),
        vm((2, width, hidden), BF16),
        vm((2, width, hidden), BF16),
        vm((2, hidden, width), BF16),
        vm((rows, width), BF16),
        vm((rows, width), BF16),
        vm((rows, 4 * hidden), BF16),
        vm((rows, 2 * hidden), BF16),
        vm((nt * 128, hidden), F32),
        vm((n * CAP, 2 * hidden), F32),
        vm((n * CAP, 2 * hidden), F32),
        vm((n * CAP, 2 * hidden), F32),
        vm((n, zn, n * CAP, cols_z), BF16),
        vm((n, zn, n * CAP, cols_z), BF16),
        vm((slots, 2 * CAP, cols_z // 2), BF16),
        vm((slots, 2 * CAP, cols_z // 2), BF16),
        vm((8, 128), F32),
        vm((zn, 8, 128), F32),
        vm((8, 128), F32),
        vm((slots, 8, 128), F32),
        vm((nb, 512, 2 * hidden), F32),
        vm((nb, 512, 2 * hidden), BF16),
        vm((nb, 512, 2 * hidden), BF16),
        vm((nb, hidden, 512), F32),
        vm((nb, hidden, 512), BF16),
        vm((nb, hidden, 512), BF16),
        dma((4,)),
        dma((3,)),
        dma((3,)),
        dma((slots,)),
        dma((slots,)),
        dma((n, zn)),
        dma((n, zn)),
        dma((slots,)),
        dma((slots,)),
        dma((zn,)),
        dma((zn,)),
        dma((slots,)),
        dma((slots,)),
        dma((nb,)),
        dma((nb,)),
        dma((nb,)),
        dma((nb,)),
    ]
    any_spec = pl.BlockSpec(memory_space=pl.ANY)
    vm_spec = pl.BlockSpec(memory_space=pltpu.VMEM)
    return pl.pallas_call(
        functools.partial(expert_kernel, n, zn),
        out_shape=(
            jax.ShapeDtypeStruct((slots, 2 * CAP, cols_z // 2), BF16),
            jax.ShapeDtypeStruct((8, 128), F32),
            jax.ShapeDtypeStruct((1, width, hidden), BF16),
            jax.ShapeDtypeStruct((1, width, hidden), BF16),
            jax.ShapeDtypeStruct((1, hidden, width), BF16),
        ),
        in_specs=[any_spec] * 4,
        out_specs=(vm_spec,) * 5,
        scratch_shapes=scratch,
        compiler_params=pltpu.CompilerParams(
            collective_id=0, has_side_effects=True, vmem_limit_bytes=58 * 1024 * 1024
        ),
        cost_estimate=pl.CostEstimate(
            flops=16 * rows * width * 2 * hidden, bytes_accessed=16 * 1024 * 1024, transcendentals=0
        ),
    )(send, gate, up, down)


def shards(
    tokens,
    cotangent,
    expert_ids,
    ada_shift,
    ada_scale,
    ada_gate,
    router_weight,
    gate_blocks,
    up_blocks,
    down_blocks,
):
    zn = lax.axis_size("exp")
    experts = lax.axis_size("seq") // 2
    n = math.isqrt(experts)
    seq_index = lax.axis_index("seq")
    exp_index = lax.axis_index("exp")
    tok_rows, width = tokens.shape
    cols = width // zn
    slots = n * n
    highest = lax.Precision.HIGHEST
    col_start = exp_index * cols

    values = tokens.astype(F32)
    center = values - jnp.mean(values, axis=-1, keepdims=True)
    inv_std = lax.rsqrt(jnp.mean(center * center, axis=-1, keepdims=True) + EPSILON)
    normed = center * inv_std
    modulated = (normed * (1.0 + ada_scale) + ada_shift).astype(BF16)
    scores = jax.nn.sigmoid(dot(modulated, router_weight))
    expert_iota = jnp.arange(experts, dtype=jnp.int32)
    chosen = (expert_ids[:, :, None] == expert_iota[None, None, :]).astype(F32)
    picked = jnp.sum(chosen * scores[:, None, :], axis=-1)
    score_sum = jnp.sum(picked, axis=-1, keepdims=True)
    shares = picked / score_sum
    share_b = lax.optimization_barrier(shares.astype(BF16))
    out_grad = (ada_gate * cotangent.astype(F32)).astype(BF16)

    routed = jnp.sum(chosen, axis=1)
    tok_iota = jnp.arange(tok_rows, dtype=jnp.int32)
    earlier = (tok_iota[:, None] > tok_iota[None, :]).astype(BF16)
    rank_all = dot(earlier, routed.astype(BF16))
    rank = jnp.sum(chosen * rank_all[:, None, :], axis=-1).astype(jnp.int32)
    chip = seq_index // 2
    dy = lax.rem(expert_ids // n - chip // n + n, n)
    dx = lax.rem(lax.rem(expert_ids, n) - lax.rem(chip, n) + n, n)
    slot = (lax.rem(dx - dy + n, n) * n + dy) * CAP + rank
    slot_iota = jnp.arange(slots * CAP, dtype=jnp.int32)
    hit = slot[:, :, None] == slot_iota[None, None, :]
    place = jnp.any(hit, axis=1).astype(BF16)
    slot_share = jnp.sum(jnp.where(hit, share_b.astype(F32)[:, :, None], 0.0), axis=(0, 1))

    send_z = dot(place, modulated, TN).astype(BF16)
    send_dy = dot(place, out_grad, TN).astype(BF16)
    side = jnp.broadcast_to(slot_share.astype(BF16)[:, None], (slots * CAP, 128))
    send = jnp.concatenate(
        [
            jnp.concatenate([send_z, side], axis=1).reshape(slots, CAP, width + 128),
            jnp.concatenate([send_dy, side], axis=1).reshape(slots, CAP, width + 128),
        ],
        axis=1,
    )
    back, terms, grad_gate, grad_up, grad_down = run_experts(
        n, zn, send, gate_blocks, up_blocks, down_blocks
    )
    rows_back = (
        back.reshape(slots, 2, CAP, cols // 2).transpose(0, 2, 1, 3).reshape(slots * CAP, cols)
    )
    expert_grad = dot(place, rows_back)
    term_row = terms.reshape(-1)[: slots * CAP]
    choice_grad = jnp.sum(jnp.where(hit, term_row[None, None, :], 0.0), axis=-1)
    mean_grad = jnp.sum(shares * choice_grad, axis=-1, keepdims=True)
    pick_grad = (choice_grad - mean_grad) / score_sum * picked * (1.0 - picked)
    logit_grad = jnp.sum(chosen * pick_grad[:, :, None], axis=1)
    router_cols = lax.dynamic_slice_in_dim(router_weight, col_start, cols, 0).astype(F32)
    modulated_cols = lax.dynamic_slice_in_dim(modulated, col_start, cols, 1).astype(F32)
    mod_grad = expert_grad + lax.dot_general(logit_grad, router_cols, NT, precision=highest)
    router_part = lax.dot_general(modulated_cols, logit_grad, TN, precision=highest)
    grad_router = lax.psum(router_part, "seq")
    scale_cols = lax.dynamic_slice_in_dim(ada_scale, col_start, cols, 0)
    normed_cols = lax.dynamic_slice_in_dim(normed, col_start, cols, 1)
    norm_grad = mod_grad * (1.0 + scale_cols)
    grad_total, grad_cross = lax.psum(
        (jnp.sum(norm_grad, axis=-1), jnp.sum(norm_grad * normed_cols, axis=-1)), "exp"
    )
    grad_input = inv_std * (
        norm_grad - grad_total[:, None] / width - normed_cols * (grad_cross[:, None] / width)
    )
    return (grad_input, grad_router, grad_gate, grad_up, grad_down)


def solution(mesh):
    in_specs = (
        P("seq", None),
        P("seq", None),
        P("seq", None),
        P(),
        P(),
        P(),
        P(),
        P(("seq", "exp"), None, None),
        P(("seq", "exp"), None, None),
        P(("seq", "exp"), None, None),
    )
    out_specs = (
        P("seq", "exp"),
        P("exp", None),
        P(("seq", "exp"), None, None),
        P(("seq", "exp"), None, None),
        P(("seq", "exp"), None, None),
    )
    return jax.shard_map(shards, mesh=mesh, in_specs=in_specs, out_specs=out_specs, check_vma=False)
```

```python
import functools
import math

import jax
import jax.numpy as jnp
from jax import lax
from jax.experimental import pallas as pl
from jax.experimental.pallas import tpu as pltpu
from jax.sharding import PartitionSpec as P

CAP = 24
EPSILON = 1e-06
MESH = pl.DeviceIdType.MESH
F32 = jnp.float32
BF16 = jnp.bfloat16
NT = (((1,), (1,)), ((), ()))
TN = (((0,), (0,)), ((), ()))


def dot(a, b, dims=(((1,), (0,)), ((), ()))):
    return lax.dot_general(a, b, dims, preferred_element_type=F32)


def split_refs(refs, counts):
    parts, at = [], 0
    for count in counts:
        parts.append(refs[at : at + count])
        at += count
    return parts


def split3(x):
    hi = x.astype(BF16)
    rest = x - hi.astype(F32)
    mid = rest.astype(BF16)
    return hi, mid, (rest - mid.astype(F32)).astype(BF16)


def expert_kernel(n, zn, *refs):
    (
        (tokens, cotangent, ids, shift, scale, ada_gate, router, gate, up, down),
        (input_out, router_out, gate_out, up_out, down_out),
        (mod, og, place_t, send, recv, w_gate, w_up, w_down, rows_z, rows_wdy, d_gu, hid, hr),
        (g_acc, u_acc, r_acc, t_send, t_recv, b_send, b_recv, term_own, term_z, term_sum, term_b),
        (gu_own, gu_send, gu_recv, dn_own, dn_send, dn_recv),
        (logit_acc, rc_own, rc_sib, rx_sum, rx_buf, ry_sum, ry_buf, ns_own, ns_z),
        (w_local, w_ssem, w_rsem, d_ssem, d_rsem, t_ssem, t_rsem, b_ssem, b_rsem),
        (tz_ssem, tz_rsem, tb_ssem, tb_rsem, g_ssem, g_rsem, h_ssem, h_rsem),
        (rc_ssem, rc_rsem, rx_ssem, rx_rsem, ry_ssem, ry_rsem, ns_ssem, ns_rsem),
    ) = split_refs(refs, (10, 5, 13, 11, 6, 9, 9, 8, 8))
    slots = n * n
    width = rows_z.shape[1]
    group = n * CAP
    hidden = w_gate.shape[2]
    kb = 512
    nb = width // kb
    cols_z = width // zn
    half = cols_z // 2
    toks = tokens.shape[0]
    seq = lax.axis_index("seq")
    z = lax.axis_index("exp")
    core = lax.rem(seq, 2)
    chip = seq // 2
    cy, cx = chip // n, lax.rem(chip, n)

    def offset(slot):
        dy = lax.rem(slot, n)
        dx = lax.rem(dy + slot // n, n)
        return dy, dx

    def target(slot):
        dy, dx = offset(slot)
        return (2 * (lax.rem(cy + dy, n) * n + lax.rem(cx + dx, n)) + core, z)

    def source(slot):
        dy, dx = offset(slot)
        return (2 * (lax.rem(cy - dy + n, n) * n + lax.rem(cx - dx + n, n)) + core, z)

    def z_peer(step):
        return (seq, lax.rem(z + step, zn))

    sibling = (seq + 1 - 2 * core, z)

    def remote(src, dst, ssem, rsem, dev):
        return pltpu.make_async_remote_copy(
            src_ref=src, dst_ref=dst, send_sem=ssem, recv_sem=rsem, device_id=dev, device_id_type=MESH
        )

    def send_copy(slot):
        return remote(send.at[slot], recv.at[slot], d_ssem.at[slot], d_rsem.at[slot], target(slot))

    def t_copy(g, step):
        return remote(
            t_send.at[g, step], t_recv.at[g, step], t_ssem.at[g, step], t_rsem.at[g, step], z_peer(step)
        )

    def b_copy(slot):
        return remote(b_send.at[slot], b_recv.at[slot], b_ssem.at[slot], b_rsem.at[slot], source(slot))

    def tz_copy(step):
        return remote(term_own, term_z.at[step], tz_ssem.at[step], tz_rsem.at[step], z_peer(step))

    def tb_copy(slot):
        return remote(term_sum, term_b.at[slot], tb_ssem.at[slot], tb_rsem.at[slot], source(slot))

    def rc_copy():
        return remote(rc_own, rc_sib, rc_ssem.at[0], rc_rsem.at[0], sibling)

    def rx_copy(step, at):
        to = (2 * (cy * n + lax.rem(cx + step, n)) + core, z)
        return remote(rx_sum, rx_buf.at[at], rx_ssem.at[step], rx_rsem.at[at], to)

    def ry_copy(step, at):
        to = (2 * (lax.rem(cy + step, n) * n + cx) + core, z)
        return remote(ry_sum, ry_buf.at[at], ry_ssem.at[step], ry_rsem.at[at], to)

    def ns_copy(step):
        return remote(ns_own, ns_z.at[step], ns_ssem.at[step], ns_rsem.at[step], z_peer(step))

    def gu_copy(b):
        return remote(gu_send.at[b], gu_recv.at[b], g_ssem.at[b], g_rsem.at[b], sibling)

    def dn_copy(b):
        return remote(dn_send.at[b], dn_recv.at[b], h_ssem.at[b], h_rsem.at[b], sibling)

    weights = ((gate, w_gate), (up, w_up), (down, w_down))

    def w_copy(i):
        hbm, vmem = weights[i]
        return remote(hbm.at[0], vmem.at[1], w_ssem.at[i], w_rsem.at[i], sibling)

    def w_copy_local(i):
        hbm, vmem = weights[i]
        return pltpu.make_async_copy(hbm.at[0], vmem.at[0], w_local.at[i])

    def loop(lo, hi, body):
        def step(i, carry):
            body(i)
            return carry

        lax.fori_loop(lo, hi, step, 0)

    barrier = pltpu.get_barrier_semaphore()
    loop(
        1,
        slots,
        lambda k: pl.semaphore_signal(barrier, inc=1, device_id=target(k), device_id_type=MESH),
    )
    loop(
        1,
        zn,
        lambda j: pl.semaphore_signal(barrier, inc=1, device_id=z_peer(j), device_id_type=MESH),
    )
    pl.semaphore_signal(barrier, inc=1, device_id=sibling, device_id_type=MESH)
    for i in range(3):
        w_copy_local(i).start()

    def moment(center):
        def body(b, acc):
            cols = pl.ds(pl.multiple_of(b * kb, kb), kb)
            x = tokens[:, cols].astype(F32)
            if center is not None:
                x = (x - center) * (x - center)
            return acc + jnp.sum(x, axis=1, keepdims=True)

        return lax.fori_loop(0, nb, body, jnp.zeros((toks, 1), F32)) * (1.0 / width)

    mean = moment(None)
    inv_std = lax.rsqrt(moment(mean) + EPSILON)
    logit_acc[...] = jnp.zeros_like(logit_acc)
    experts = router.shape[1]

    def modulate(b):
        cols = pl.ds(pl.multiple_of(b * kb, kb), kb)
        normed = (tokens[:, cols].astype(F32) - mean) * inv_std
        m = (normed * (1.0 + scale[:, cols]) + shift[:, cols]).astype(BF16)
        mod[:, cols] = m
        og[:, cols] = (ada_gate[:, cols] * cotangent[:, cols].astype(F32)).astype(BF16)
        logit_acc[:, :experts] += dot(m, router[cols, :])

    loop(0, nb, modulate)
    scores = jax.nn.sigmoid(logit_acc[...])
    expert_at = lax.broadcasted_iota(jnp.int32, (toks, 128), 1)
    hits = [expert_at == ids[:, k : k + 1] for k in range(2)]
    picked = [jnp.sum(jnp.where(h, scores, 0.0), axis=1, keepdims=True) for h in hits]
    score_sum = picked[0] + picked[1]
    shares = [p / score_sum for p in picked]
    share_r = [s.astype(BF16).astype(F32) for s in shares]
    routed = jnp.where(hits[0] | hits[1], 1.0, 0.0)
    tok_at = lax.broadcasted_iota(jnp.int32, (toks, toks), 0)
    earlier = jnp.where(tok_at > lax.broadcasted_iota(jnp.int32, (toks, toks), 1), 1.0, 0.0)
    rank = dot(earlier.astype(BF16), routed.astype(BF16))
    bits = n.bit_length() - 1
    e_dy = ((expert_at >> bits) - cy) & (n - 1)
    e_dx = ((expert_at & (n - 1)) - cx) & (n - 1)
    base = ((((e_dx - e_dy) & (n - 1)) * n + e_dy) * CAP).astype(F32) + rank
    slot_at = lax.broadcasted_iota(jnp.int32, (toks, slots * CAP), 1).astype(F32)
    places = [
        jnp.where(slot_at == jnp.sum(jnp.where(h, base, 0.0), axis=1, keepdims=True), 1.0, 0.0)
        for h in hits
    ]
    place_t[...] = (places[0] + places[1]).T.astype(BF16)
    slot_share = jnp.sum(
        (places[0] * share_r[0] + places[1] * share_r[1]).T, axis=1, keepdims=True
    )
    side = jnp.broadcast_to(slot_share, (slots * CAP, 128))
    for k in range(slots):
        part = side[k * CAP : (k + 1) * CAP]
        pair = jnp.concatenate([part, part], axis=0).astype(BF16)
        send[k, :, width : width + 128] = pair
        if k == 0:
            recv[0, :, width : width + 128] = pair

    hr[...] = jnp.zeros_like(hr)
    pl.semaphore_wait(barrier, slots + zn - 1)
    for i in range(3):
        w_copy(i).start()

    def dispatch_group(g):
        rows = pl.ds(pl.multiple_of(g * group, group), group)

        def fill(b):
            cols = pl.ds(pl.multiple_of(b * kb, kb), kb)
            zc = dot(place_t[rows, :], mod[:, cols])
            dc = dot(place_t[rows, :], og[:, cols])
            for i in range(n):
                at = slice(i * CAP, (i + 1) * CAP)
                pair = jnp.concatenate([zc[at], dc[at]], axis=0).astype(BF16)
                send[g * n + i, :, cols] = pair
                if i == 0:

                    @pl.when(g == 0)
                    def _():
                        recv[0, :, cols] = pair

        loop(0, nb, fill)

        def start(i):
            @pl.when(g * n + i > 0)
            def _():
                send_copy(g * n + i).start()

        loop(0, n, start)

    loop(0, n, dispatch_group)
    for i in range(3):
        w_copy_local(i).wait()
        w_copy(i).wait()

    def wait_group(g):
        def one(i):
            slot = g * n + i

            @pl.when(slot > 0)
            def _():
                send_copy(slot).wait_recv()

        loop(0, n, one)

    def reduce_group(g):
        loop(1, zn, lambda j: t_copy(g, j).wait_recv())
        for i in range(n):
            slot = g * n + i
            parts = []
            for lo in (0, half):
                part = t_recv[g, :, :, lo : lo + half].astype(F32)[:, i * CAP : (i + 1) * CAP, :]
                parts.append(jnp.sum(part, axis=0))
            packed = jnp.concatenate(parts, axis=0).astype(BF16)
            if i > 0:
                b_send[slot] = packed
                b_copy(slot).start()
            else:

                @pl.when(slot > 0)
                def _():
                    b_send[slot] = packed
                    b_copy(slot).start()

                @pl.when(slot == 0)
                def _():
                    b_recv[0] = packed

    def compute_group(g):
        wait_group(g)
        rows = pl.ds(pl.multiple_of(g * group, group), group)
        share = jnp.concatenate(
            [recv[g * n + i, :, width : width + 128].astype(F32)[CAP:, :1] for i in range(n)], axis=0
        )
        g_acc[...] = jnp.zeros_like(g_acc)
        u_acc[...] = jnp.zeros_like(u_acc)
        r_acc[...] = jnp.zeros_like(r_acc)

        def forward(b):
            cols = pl.ds(pl.multiple_of(b * kb, kb), kb)
            tiles = [recv[g * n + i, :, cols].astype(F32) for i in range(n)]
            zb = jnp.concatenate([t[:CAP] for t in tiles], axis=0).astype(BF16)
            dyf = jnp.concatenate([t[CAP:] for t in tiles], axis=0)
            rows_z[rows, cols] = zb
            rows_wdy[rows, cols] = (share * dyf).astype(BF16)
            g_acc[...] += dot(zb, jnp.concatenate([w_gate[0, cols, :], w_gate[1, cols, :]], axis=1))
            u_acc[...] += dot(zb, jnp.concatenate([w_up[0, cols, :], w_up[1, cols, :]], axis=1))
            wd = jnp.concatenate([w_down[0, :, cols], w_down[1, :, cols]], axis=0)
            r_acc[...] += dot(dyf.astype(BF16), wd, NT)

        loop(0, nb, forward)
        gv, uv, rv = g_acc[...], u_acc[...], r_acc[...]
        sig = jax.nn.sigmoid(gv)
        act = gv * sig
        hv = act * uv
        prod = hv * rv
        hr[rows, :] = prod[:, :hidden] + prod[:, hidden:]
        scaled = share * rv
        du = (scaled * act).astype(BF16)
        dg = (scaled * uv * sig * (1.0 + gv * (1.0 - sig))).astype(BF16)
        d_gu[rows, :] = jnp.concatenate(
            [dg[:, :hidden], du[:, :hidden], dg[:, hidden:], du[:, hidden:]], axis=1
        )
        hid[rows, :] = hv.astype(BF16)

        def backward(step):
            dest = lax.rem(z + step, zn)
            wrows = pl.ds(pl.multiple_of(dest * cols_z, cols_z), cols_z)
            wg = jnp.concatenate([w_gate[0, wrows, :], w_gate[1, wrows, :]], axis=1)
            wu = jnp.concatenate([w_up[0, wrows, :], w_up[1, wrows, :]], axis=1)
            part = (dot(dg, wg, NT) + dot(du, wu, NT)).astype(BF16)

            @pl.when(step > 0)
            def _():
                t_send[g, step] = part
                t_copy(g, step).start()

            @pl.when(step == 0)
            def _():
                t_recv[g, 0] = part

        loop(0, zn, lambda i: backward(zn - 1 - i))

    def group_step(g):
        compute_group(g)

        @pl.when(g > 0)
        def _():
            reduce_group(g - 1)

    loop(0, n, group_step)

    nt = hr.shape[0] // 128
    term_own[...] = jnp.zeros_like(term_own)
    for i in range(nt):
        tile = hr[128 * i : 128 * (i + 1), :]
        term_own[i : i + 1, :] = jnp.sum(tile.T, axis=0, keepdims=True)
    loop(1, zn, lambda j: tz_copy(j).start())

    def weight_grads(b):
        cols = pl.ds(pl.multiple_of(b * kb, kb), kb)
        gu = dot(rows_z[:, cols], d_gu[...], TN)
        gu_own[b] = gu[:, : 2 * hidden]
        gu_send[b] = gu[:, 2 * hidden :].astype(BF16)
        gu_copy(b).start()
        dn = dot(hid[...], rows_wdy[:, cols], TN)
        dn_own[b] = dn[:hidden]
        dn_send[b] = dn[hidden:].astype(BF16)
        dn_copy(b).start()

    loop(0, nb // 2, weight_grads)
    loop(1, zn, lambda j: tz_copy(j).wait_recv())
    total = term_own[...]
    for j in range(1, zn):
        total = total + term_z[j]
    term_sum[...] = total
    loop(1, slots, lambda k: tb_copy(k).start())
    loop(nb // 2, nb, weight_grads)
    loop(1, slots, lambda k: tb_copy(k).wait_recv())
    flat = lax.broadcasted_iota(jnp.int32, (8, 128), 0) * 128 + lax.broadcasted_iota(
        jnp.int32, (8, 128), 1
    )
    terms = jnp.where(flat < CAP, term_sum[...], 0.0)
    for k in range(1, slots):
        terms = jnp.where((flat >= k * CAP) & (flat < (k + 1) * CAP), term_b[k], terms)
    term_row = jnp.concatenate([terms[i : i + 1] for i in range(nt)], axis=1)[:, : slots * CAP]
    choice = [jnp.sum(p * term_row, axis=1, keepdims=True) for p in places]
    mean_grad = shares[0] * choice[0] + shares[1] * choice[1]
    logit_grad = jnp.zeros((toks, 128), F32)
    for k in range(2):
        pick = (choice[k] - mean_grad) / score_sum * picked[k] * (1.0 - picked[k])
        logit_grad = logit_grad + jnp.where(hits[k], pick, 0.0)
    my_cols = pl.ds(pl.multiple_of(z * cols_z, cols_z), cols_z)
    lg_rows = logit_grad.T[:16]
    parts = [p.astype(F32) for p in split3(lg_rows)]
    prod = dot(jnp.concatenate(parts, axis=0).astype(BF16), mod[:, my_cols])
    rc_own[...] = prod[:16] + prod[16:32] + prod[32:]
    rc_copy().start()
    reduce_group(n - 1)

    def finish(b):
        gu_copy(b).wait_recv()
        dn_copy(b).wait_recv()
        cols = pl.ds(pl.multiple_of(b * kb, kb), kb)
        gu = gu_own[b] + gu_recv[b].astype(F32)
        gate_out[0, cols, :] = gu[:, :hidden].astype(BF16)
        up_out[0, cols, :] = gu[:, hidden:].astype(BF16)
        down_out[0, :, cols] = (dn_own[b] + dn_recv[b].astype(F32)).astype(BF16)

    rc_copy().wait_recv()
    rx_sum[...] = rc_own[...] + rc_sib[...]
    rx_buf[cx] = rx_sum[...]
    loop(1, n, lambda j: rx_copy(j, cx).start())
    loop(0, nb // 2, finish)
    loop(1, n, lambda j: rx_copy(j, lax.rem(cx + j, n)).wait_recv())
    total = rx_buf[0]
    for j in range(1, n):
        total = total + rx_buf[j]
    ry_sum[...] = total
    ry_buf[cy] = total
    loop(1, n, lambda j: ry_copy(j, cy).start())
    loop(nb // 2, nb, finish)

    def mod_part(i):
        return dot(split3(logit_grad)[i][:, :experts], router[my_cols, :], NT)

    mod_grad = mod_part(0) + mod_part(1) + mod_part(2)
    gain = 1.0 + scale[:, my_cols]
    normed = (tokens[:, my_cols].astype(F32) - mean) * inv_std

    loop(1, slots, lambda k: b_copy(k).wait_recv())
    tiles = [b_recv[k].astype(F32) for k in range(slots)]
    rows_back = jnp.concatenate(
        [
            jnp.concatenate([t[:CAP] for t in tiles], axis=0),
            jnp.concatenate([t[CAP:] for t in tiles], axis=0),
        ],
        axis=1,
    ).astype(BF16)
    norm_grad = (mod_grad + dot(place_t[...], rows_back, TN)) * gain
    sums = [
        jnp.sum(norm_grad, axis=1, keepdims=True),
        jnp.sum(norm_grad * normed, axis=1, keepdims=True),
    ]
    lane = lax.broadcasted_iota(jnp.int32, (toks, 128), 1)
    sums_t = jnp.where(lane == 0, sums[0], jnp.where(lane == 1, sums[1], 0.0)).T
    ns_own[...] = sums_t[:8]
    loop(1, zn, lambda j: ns_copy(j).start())

    loop(1, n, lambda j: ry_copy(j, lax.rem(cy + j, n)).wait_recv())
    total = ry_buf[0]
    for j in range(1, n):
        total = total + ry_buf[j]
    router_out[...] = total

    loop(1, zn, lambda j: ns_copy(j).wait_recv())
    total = ns_own[...]
    for j in range(1, zn):
        total = total + ns_z[j]
    total = jnp.concatenate([total, jnp.zeros((120, toks), F32)], axis=0).T * (1.0 / width)
    input_out[...] = inv_std * (norm_grad - total[:, 0:1] - normed * total[:, 1:2])

    def drain_slot(k):
        send_copy(k).wait_send()
        b_copy(k).wait_send()
        tb_copy(k).wait_send()

    loop(1, slots, drain_slot)

    def drain_ring(j):
        rx_copy(j, cx).wait_send()
        ry_copy(j, cy).wait_send()

    rc_copy().wait_send()
    loop(1, n, drain_ring)

    def drain_z(j):
        tz_copy(j).wait_send()
        ns_copy(j).wait_send()
        loop(0, n, lambda g: t_copy(g, j).wait_send())

    loop(1, zn, drain_z)

    def drain_b(b):
        gu_copy(b).wait_send()
        dn_copy(b).wait_send()

    loop(0, nb, drain_b)


def shards(
    tokens,
    cotangent,
    expert_ids,
    ada_shift,
    ada_scale,
    ada_gate,
    router_weight,
    gate_blocks,
    up_blocks,
    down_blocks,
):
    zn = lax.axis_size("exp")
    n = math.isqrt(lax.axis_size("seq") // 2)
    slots = n * n
    toks, width = tokens.shape
    experts = router_weight.shape[1]
    hidden = gate_blocks.shape[2]
    rows = slots * CAP
    cols_z = width // zn
    nb = width // 512
    nt = -(-rows // 128)
    dma = pltpu.SemaphoreType.DMA
    vm = pltpu.VMEM
    scratch = [
        vm((toks, width), BF16),
        vm((toks, width), BF16),
        vm((rows, toks), BF16),
        vm((slots, 2 * CAP, width + 128), BF16),
        vm((slots, 2 * CAP, width + 128), BF16),
        vm((2, width, hidden), BF16),
        vm((2, width, hidden), BF16),
        vm((2, hidden, width), BF16),
        vm((rows, width), BF16),
        vm((rows, width), BF16),
        vm((rows, 4 * hidden), BF16),
        vm((rows, 2 * hidden), BF16),
        vm((nt * 128, hidden), F32),
        vm((n * CAP, 2 * hidden), F32),
        vm((n * CAP, 2 * hidden), F32),
        vm((n * CAP, 2 * hidden), F32),
        vm((n, zn, n * CAP, cols_z), BF16),
        vm((n, zn, n * CAP, cols_z), BF16),
        vm((slots, 2 * CAP, cols_z // 2), BF16),
        vm((slots, 2 * CAP, cols_z // 2), BF16),
        vm((8, 128), F32),
        vm((zn, 8, 128), F32),
        vm((8, 128), F32),
        vm((slots, 8, 128), F32),
        vm((nb, 512, 2 * hidden), F32),
        vm((nb, 512, 2 * hidden), BF16),
        vm((nb, 512, 2 * hidden), BF16),
        vm((nb, hidden, 512), F32),
        vm((nb, hidden, 512), BF16),
        vm((nb, hidden, 512), BF16),
        vm((toks, 128), F32),
        vm((16, cols_z), F32),
        vm((16, cols_z), F32),
        vm((16, cols_z), F32),
        vm((n, 16, cols_z), F32),
        vm((16, cols_z), F32),
        vm((n, 16, cols_z), F32),
        vm((8, toks), F32),
        vm((zn, 8, toks), F32),
    ]
    sems = [3, 3, 3, slots, slots, (n, zn), (n, zn), slots, slots]
    sems += [zn, zn, slots, slots, nb, nb, nb, nb]
    sems += [1, 1, n, n, n, n, zn, zn]
    scratch += [dma(s if isinstance(s, tuple) else (s,)) for s in sems]
    any_spec = pl.BlockSpec(memory_space=pl.ANY)
    vm_spec = pl.BlockSpec(memory_space=pltpu.VMEM)
    row = lambda v: v.reshape(1, width)
    grad_input, router_t, grad_gate, grad_up, grad_down = pl.pallas_call(
        functools.partial(expert_kernel, n, zn),
        out_shape=(
            jax.ShapeDtypeStruct((toks, cols_z), F32),
            jax.ShapeDtypeStruct((16, cols_z), F32),
            jax.ShapeDtypeStruct((1, width, hidden), BF16),
            jax.ShapeDtypeStruct((1, width, hidden), BF16),
            jax.ShapeDtypeStruct((1, hidden, width), BF16),
        ),
        in_specs=[vm_spec] * 7 + [any_spec] * 3,
        out_specs=(vm_spec,) * 5,
        scratch_shapes=scratch,
        compiler_params=pltpu.CompilerParams(
            collective_id=0, has_side_effects=True, vmem_limit_bytes=60 * 1024 * 1024
        ),
        cost_estimate=pl.CostEstimate(
            flops=16 * rows * width * 2 * hidden, bytes_accessed=16 * 1024 * 1024, transcendentals=0
        ),
    )(
        tokens,
        cotangent,
        expert_ids,
        row(ada_shift),
        row(ada_scale),
        row(ada_gate),
        router_weight,
        gate_blocks,
        up_blocks,
        down_blocks,
    )
    return (grad_input, router_t[:experts].T, grad_gate, grad_up, grad_down)


def solution(mesh):
    in_specs = (
        P("seq", None),
        P("seq", None),
        P("seq", None),
        P(),
        P(),
        P(),
        P(),
        P(("seq", "exp"), None, None),
        P(("seq", "exp"), None, None),
        P(("seq", "exp"), None, None),
    )
    out_specs = (
        P("seq", "exp"),
        P("exp", None),
        P(("seq", "exp"), None, None),
        P(("seq", "exp"), None, None),
        P(("seq", "exp"), None, None),
    )
    return jax.shard_map(shards, mesh=mesh, in_specs=in_specs, out_specs=out_specs, check_vma=False)
```

```python
import functools
import math

import jax
import jax.numpy as jnp
from jax import lax
from jax.experimental import pallas as pl
from jax.experimental.pallas import tpu as pltpu
from jax.sharding import PartitionSpec as P

CAP = 24
RELAYED = 2
ROLE = (1, 7, 4, 2, 5)
CLASS = (0, 0, 1, 1, 2)
SIGN = (1, -1, 1, -1, -1)
EPSILON = 1e-06
MESH = pl.DeviceIdType.MESH
F32 = jnp.float32
BF16 = jnp.bfloat16
NT = (((1,), (1,)), ((), ()))
TN = (((0,), (0,)), ((), ()))


def dot(a, b, dims=(((1,), (0,)), ((), ()))):
    return lax.dot_general(a, b, dims, preferred_element_type=F32)


def split_refs(refs, counts):
    parts, at = [], 0
    for count in counts:
        parts.append(refs[at : at + count])
        at += count
    return parts


def split3(x):
    hi = x.astype(BF16)
    rest = x - hi.astype(F32)
    mid = rest.astype(BF16)
    return hi, mid, (rest - mid.astype(F32)).astype(BF16)


def expert_kernel(n, zn, *refs):
    (
        (tokens, cotangent, ids, shift, scale, ada_gate, router, gate, up, down),
        (input_out, router_out, gate_out, up_out, down_out),
        (mod, og, place_t, send, recv, w_gate, w_up, w_down, rows_z, rows_wdy, d_gu, hid, hr),
        (gu_acc, r_acc, t_send, t_in, t_own, m_send, m_in, b_send, b_recv),
        (term_own, term_z, term_sum, term_b, sh_own, sh_recv, sh_col),
        (gu_own, gu_send, gu_recv, dn_own, dn_send, dn_recv),
        (logit_acc, rc_own, rc_sib, rx_sum, rx_buf, ry_sum, ry_buf, ns_own, ns_z),
        (w_local, w_ssem, w_rsem, d_ssem, d_rsem, f_ssem, f_rsem, a_ssem, a_rsem),
        (m_ssem, m_rsem, b_ssem, b_rsem, sh_ssem, sh_rsem),
        (tz_ssem, tz_rsem, tb_ssem, tb_rsem, g_ssem, g_rsem, h_ssem, h_rsem),
        (rc_ssem, rc_rsem, rx_ssem, rx_rsem, ry_ssem, ry_rsem, ns_ssem, ns_rsem),
    ) = split_refs(refs, (10, 5, 13, 9, 7, 6, 9, 9, 6, 8, 8))
    slots = n * n
    width = rows_z.shape[1]
    group = n * CAP
    hidden = w_gate.shape[2]
    kb = cols_z = width // zn
    nb = zn
    half = cols_z // 2
    toks = tokens.shape[0]
    seq = lax.axis_index("seq")
    z = lax.axis_index("exp")
    core = lax.rem(seq, 2)
    chip = seq // 2
    cy, cx = chip // n, lax.rem(chip, n)

    def offset(slot):
        dy = lax.rem(slot, n)
        dx = lax.rem(dy + slot // n, n)
        return dy, dx

    def target(slot):
        dy, dx = offset(slot)
        return (2 * (lax.rem(cy + dy, n) * n + lax.rem(cx + dx, n)) + core, z)

    def source(slot):
        dy, dx = offset(slot)
        return (2 * (lax.rem(cy - dy + n, n) * n + lax.rem(cx - dx + n, n)) + core, z)

    def z_peer(step):
        return (seq, lax.rem(z + step, zn))

    sibling = (seq + 1 - 2 * core, z)

    def remote(src, dst, ssem, rsem, dev):
        return pltpu.make_async_remote_copy(
            src_ref=src, dst_ref=dst, send_sem=ssem, recv_sem=rsem, device_id=dev, device_id_type=MESH
        )

    def plane(step):
        return lax.rem(z + step + 2 * zn, zn)

    def turn(g):
        return 1 - 2 * lax.rem(g, 2)

    def own_class(g, c):
        return plane(-3 * turn(g) * c)

    def direct_copy(slot):
        dst = recv.at[slot // n, :, lax.rem(slot, n)]
        return remote(send.at[slot], dst, d_ssem.at[slot, 0], d_rsem.at[slot, 0], target(slot))

    def part_copy(slot, c):
        g = slot // n
        r = own_class(g, c)
        dst = recv.at[g, r, lax.rem(slot, n)]
        return remote(send.at[slot, r], dst, d_ssem.at[slot, c], d_rsem.at[slot, c], target(slot))

    def relay_copy(g, i, r):
        to = (seq, plane(turn(g) * SIGN[i]))
        return remote(recv.at[g, r], recv.at[g, r], f_ssem.at[g, i], f_rsem.at[g, i], to)

    def near_copy(g, i):
        to = (seq, plane(-turn(g) * SIGN[i]))
        return remote(t_send.at[g, i], t_in.at[g, i], a_ssem.at[g, i], a_rsem.at[g, i], to)

    def far_copy(g, c):
        to = (seq, own_class(g, c))
        return remote(m_send.at[g, c - 1], m_in.at[g, c - 1], m_ssem.at[g, c - 1], m_rsem.at[g, c - 1], to)

    def sh_copy(slot):
        return remote(sh_own, sh_recv.at[slot], sh_ssem.at[slot], sh_rsem.at[slot], target(slot))

    def b_copy(slot):
        return remote(b_send.at[slot], b_recv.at[slot], b_ssem.at[slot], b_rsem.at[slot], source(slot))

    def tz_copy(step):
        return remote(term_own, term_z.at[step], tz_ssem.at[step], tz_rsem.at[step], z_peer(step))

    def tb_copy(slot):
        return remote(term_sum, term_b.at[slot], tb_ssem.at[slot], tb_rsem.at[slot], source(slot))

    def rc_copy():
        return remote(rc_own, rc_sib, rc_ssem.at[0], rc_rsem.at[0], sibling)

    def rx_copy(step, at):
        to = (2 * (cy * n + lax.rem(cx + step, n)) + core, z)
        return remote(rx_sum, rx_buf.at[at], rx_ssem.at[step], rx_rsem.at[at], to)

    def ry_copy(step, at):
        to = (2 * (lax.rem(cy + step, n) * n + cx) + core, z)
        return remote(ry_sum, ry_buf.at[at], ry_ssem.at[step], ry_rsem.at[at], to)

    def ns_copy(step):
        return remote(ns_own, ns_z.at[step], ns_ssem.at[step], ns_rsem.at[step], z_peer(step))

    def gu_copy(b):
        return remote(gu_send.at[b], gu_recv.at[b], g_ssem.at[b], g_rsem.at[b], sibling)

    def dn_copy(b):
        return remote(dn_send.at[b], dn_recv.at[b], h_ssem.at[b], h_rsem.at[b], sibling)

    weights = ((gate, w_gate), (up, w_up), (down, w_down))

    def w_copy(i):
        hbm, vmem = weights[i]
        return remote(hbm.at[0], vmem.at[1], w_ssem.at[i], w_rsem.at[i], sibling)

    def w_copy_local(i):
        hbm, vmem = weights[i]
        return pltpu.make_async_copy(hbm.at[0], vmem.at[0], w_local.at[i])

    def loop(lo, hi, body):
        def step(i, carry):
            body(i)
            return carry

        lax.fori_loop(lo, hi, step, 0)

    barrier = pltpu.get_barrier_semaphore()
    loop(
        1,
        slots,
        lambda k: pl.semaphore_signal(barrier, inc=1, device_id=target(k), device_id_type=MESH),
    )
    loop(
        1,
        zn,
        lambda j: pl.semaphore_signal(barrier, inc=1, device_id=z_peer(j), device_id_type=MESH),
    )
    pl.semaphore_signal(barrier, inc=1, device_id=sibling, device_id_type=MESH)
    for i in range(3):
        w_copy_local(i).start()

    def moment(center):
        def body(b, acc):
            cols = pl.ds(pl.multiple_of(b * kb, kb), kb)
            x = tokens[:, cols].astype(F32)
            if center is not None:
                x = (x - center) * (x - center)
            return acc + jnp.sum(x, axis=1, keepdims=True)

        return lax.fori_loop(0, nb, body, jnp.zeros((toks, 1), F32)) * (1.0 / width)

    mean = moment(None)
    inv_std = lax.rsqrt(moment(mean) + EPSILON)
    logit_acc[...] = jnp.zeros_like(logit_acc)
    experts = router.shape[0]

    def modulate(b):
        cols = pl.ds(pl.multiple_of(b * kb, kb), kb)
        normed = (tokens[:, cols].astype(F32) - mean) * inv_std
        m = (normed * (1.0 + scale[:, cols]) + shift[:, cols]).astype(BF16)
        mod[:, cols] = m
        og[:, cols] = (ada_gate[:, cols] * cotangent[:, cols].astype(F32)).astype(BF16)
        logit_acc[:, :experts] += dot(m, router[:, cols], NT)

    loop(0, nb, modulate)
    scores = jax.nn.sigmoid(logit_acc[...])
    expert_at = lax.broadcasted_iota(jnp.int32, (toks, 128), 1)
    ids_t = jnp.concatenate([ids[...].astype(F32), jnp.zeros((126, toks), F32)], axis=0).T
    hits = [expert_at.astype(F32) == ids_t[:, k : k + 1] for k in range(2)]
    picked = [jnp.sum(jnp.where(h, scores, 0.0), axis=1, keepdims=True) for h in hits]
    score_sum = picked[0] + picked[1]
    shares = [p / score_sum for p in picked]
    share_r = [s.astype(BF16).astype(F32) for s in shares]
    routed = jnp.where(hits[0] | hits[1], 1.0, 0.0)
    tok_at = lax.broadcasted_iota(jnp.int32, (toks, toks), 0)
    earlier = jnp.where(tok_at > lax.broadcasted_iota(jnp.int32, (toks, toks), 1), 1.0, 0.0)
    rank = dot(earlier.astype(BF16), routed.astype(BF16))
    bits = n.bit_length() - 1
    e_dy = ((expert_at >> bits) - cy) & (n - 1)
    e_dx = ((expert_at & (n - 1)) - cx) & (n - 1)
    base = ((((e_dx - e_dy) & (n - 1)) * n + e_dy) * CAP).astype(F32) + rank
    slot_at = lax.broadcasted_iota(jnp.int32, (toks, slots * CAP), 1).astype(F32)
    places = [
        jnp.where(slot_at == jnp.sum(jnp.where(h, base, 0.0), axis=1, keepdims=True), 1.0, 0.0)
        for h in hits
    ]
    place_t[...] = (places[0] + places[1]).T.astype(BF16)
    nt = hr.shape[0] // 128
    flat = lax.broadcasted_iota(jnp.int32, (8, 128), 0) * 128 + lax.broadcasted_iota(
        jnp.int32, (8, 128), 1
    )

    def merge(own, others):
        out = jnp.where(flat < CAP, own, 0.0)
        for k in range(1, slots):
            out = jnp.where((flat >= k * CAP) & (flat < (k + 1) * CAP), others[k], out)
        return out

    share_row = jnp.sum(places[0] * share_r[0] + places[1] * share_r[1], axis=0, keepdims=True)
    if nt * 128 > slots * CAP:
        share_row = jnp.concatenate(
            [share_row, jnp.zeros((1, nt * 128 - slots * CAP), F32)], axis=1
        )
    sh_own[...] = jnp.zeros_like(sh_own)
    for i in range(nt):
        sh_own[i : i + 1, :] = share_row[:, 128 * i : 128 * (i + 1)]

    hr[...] = jnp.zeros_like(hr)
    pl.semaphore_wait(barrier, slots + zn - 1)
    for i in range(3):
        w_copy(i).start()

    loop(1, slots, lambda k: sh_copy(k).start())

    def fill(g, b):
        rows = pl.ds(pl.multiple_of(g * group, group), group)
        cols = pl.ds(pl.multiple_of(b * kb, kb), kb)
        zc = dot(place_t[rows, :], mod[:, cols])
        dc = dot(place_t[rows, :], og[:, cols])
        for i in range(n):
            at = slice(i * CAP, (i + 1) * CAP)
            pair = jnp.concatenate([zc[at], dc[at]], axis=0).astype(BF16)

            @pl.when(g * n + i > 0)
            def _():
                send[g * n + i, b] = pair

            if i == 0:

                @pl.when(g == 0)
                def _():
                    recv[0, b, 0] = pair

    def each_remote(g, body):
        def one(i):
            @pl.when(g * n + i > 0)
            def _():
                body(g * n + i)

        loop(0, n, one)

    def relayed_start(g):
        for c in range(3):
            fill(g, own_class(g, c))
            each_remote(g, lambda slot: part_copy(slot, c).start())

    def relayed_arrive(g):
        for c in range(3):
            each_remote(g, lambda slot: part_copy(slot, c).wait_recv())
            for i in range(5):
                if CLASS[i] == c:
                    relay_copy(g, i, own_class(g, c)).start()

    loop(0, RELAYED, relayed_start)
    loop(RELAYED, n, lambda g: loop(0, nb, lambda b: fill(g, b)))
    for g in range(RELAYED):
        relayed_arrive(g)
        if g == 0:
            loop(RELAYED * n, (RELAYED + 1) * n, lambda k: direct_copy(k).start())
    loop(1, slots, lambda k: sh_copy(k).wait_recv())
    shares_in = merge(sh_own[...], sh_recv)
    shares_in = jnp.concatenate([shares_in, jnp.zeros((120, 128), F32)], axis=0).T
    for i in range(nt):
        sh_col[128 * i : 128 * (i + 1), :] = jnp.broadcast_to(shares_in[:, i : i + 1], (128, 128))
    for i in range(3):
        w_copy_local(i).wait()
        w_copy(i).wait()

    def wait_group(g):
        @pl.when(g < RELAYED)
        def _():
            for i in range(5):
                relay_copy(g, i, plane(-turn(g) * ROLE[i])).wait_recv()

        @pl.when(g >= RELAYED)
        def _():
            loop(0, n, lambda i: direct_copy(g * n + i).wait_recv())

        @pl.when(g == RELAYED - 1)
        def _():
            loop((RELAYED + 1) * n, slots, lambda k: direct_copy(k).start())

    def near_sums(g):
        for i in range(5):
            near_copy(g, i).wait_recv()
        for c in (1, 2, 0):
            total = t_own[g, c]
            for i in range(5):
                if CLASS[i] == c:
                    total = total + t_in[g, i].astype(F32)
            if c > 0:
                m_send[g, c - 1] = total.astype(BF16)
                far_copy(g, c).start()
            else:
                t_own[g, 0] = total

    def far_sums(g):
        for c in (1, 2):
            far_copy(g, c).wait_recv()
        total = t_own[g, 0] + m_in[g, 0].astype(F32) + m_in[g, 1].astype(F32)
        for i in range(n):
            slot = g * n + i
            part = total[i * CAP : (i + 1) * CAP]
            packed = jnp.concatenate([part[:, :half], part[:, half:]], axis=0).astype(BF16)
            if i > 0:
                b_send[slot] = packed
                b_copy(slot).start()
            else:

                @pl.when(slot > 0)
                def _():
                    b_send[slot] = packed
                    b_copy(slot).start()

                @pl.when(slot == 0)
                def _():
                    b_recv[0] = packed

    def compute_group(g):
        wait_group(g)
        rows = pl.ds(pl.multiple_of(g * group, group), group)
        share = sh_col[rows, :1]
        gu_acc[...] = jnp.zeros_like(gu_acc)
        r_acc[...] = jnp.zeros_like(r_acc)

        def forward(b):
            cols = pl.ds(pl.multiple_of(b * kb, kb), kb)
            tiles = [recv[g, b, i].astype(F32) for i in range(n)]
            zb = jnp.concatenate([t[:CAP] for t in tiles], axis=0).astype(BF16)
            dyf = jnp.concatenate([t[CAP:] for t in tiles], axis=0)
            rows_z[rows, cols] = zb
            rows_wdy[rows, cols] = (share * dyf).astype(BF16)
            w_gu = [w_gate[0, cols, :], w_gate[1, cols, :], w_up[0, cols, :], w_up[1, cols, :]]
            gu_acc[...] += dot(zb, jnp.concatenate(w_gu, axis=1))
            wd = jnp.concatenate([w_down[0, :, cols], w_down[1, :, cols]], axis=0)
            r_acc[...] += dot(dyf.astype(BF16), wd, NT)

        loop(0, nb, forward)
        gv, uv, rv = gu_acc[:, : 2 * hidden], gu_acc[:, 2 * hidden :], r_acc[...]
        sig = jax.nn.sigmoid(gv)
        act = gv * sig
        hv = act * uv
        prod = hv * rv
        hr[rows, :] = prod[:, :hidden] + prod[:, hidden:]
        scaled = share * rv
        du = (scaled * act).astype(BF16)
        dg = (scaled * uv * sig * (1.0 + gv * (1.0 - sig))).astype(BF16)
        d_gu[rows, :] = jnp.concatenate(
            [dg[:, :hidden], du[:, :hidden], dg[:, hidden:], du[:, hidden:]], axis=1
        )
        hid[rows, :] = hv.astype(BF16)

        def backward(r):
            wrows = pl.ds(pl.multiple_of(r * kb, kb), kb)
            w_gu = [w_gate[0, wrows, :], w_up[0, wrows, :], w_gate[1, wrows, :], w_up[1, wrows, :]]
            return dot(d_gu[rows, :], jnp.concatenate(w_gu, axis=1), NT)

        for i in range(5):
            t_send[g, i] = backward(plane(-turn(g) * ROLE[i])).astype(BF16)
            near_copy(g, i).start()
        for c in range(3):
            t_own[g, c] = backward(own_class(g, c))

    def group_step(g):
        compute_group(g)

        @pl.when(g > 0)
        def _():
            near_sums(g - 1)

        @pl.when(g > 1)
        def _():
            far_sums(g - 2)

    loop(0, n, group_step)

    term_own[...] = jnp.zeros_like(term_own)
    for i in range(nt):
        tile = hr[128 * i : 128 * (i + 1), :]
        term_own[i : i + 1, :] = jnp.sum(tile.T, axis=0, keepdims=True)
    loop(1, zn, lambda j: tz_copy(j).start())

    def weight_grads(b):
        cols = pl.ds(pl.multiple_of(b * kb, kb), kb)
        gu = dot(rows_z[:, cols], d_gu[...], TN)
        gu_own[b] = gu[:, : 2 * hidden]
        gu_send[b] = gu[:, 2 * hidden :].astype(BF16)
        gu_copy(b).start()
        dn = dot(hid[...], rows_wdy[:, cols], TN)
        dn_own[b] = dn[:hidden]
        dn_send[b] = dn[hidden:].astype(BF16)
        dn_copy(b).start()

    loop(0, nb // 4, weight_grads)
    near_sums(n - 1)
    far_sums(n - 2)
    loop(nb // 4, nb // 2, weight_grads)
    loop(1, zn, lambda j: tz_copy(j).wait_recv())
    total = term_own[...]
    for j in range(1, zn):
        total = total + term_z[j]
    term_sum[...] = total
    loop(1, slots, lambda k: tb_copy(k).start())
    loop(nb // 2, nb, weight_grads)
    loop(1, slots, lambda k: tb_copy(k).wait_recv())
    terms = merge(term_sum[...], term_b)
    term_row = jnp.concatenate([terms[i : i + 1] for i in range(nt)], axis=1)[:, : slots * CAP]
    choice = [jnp.sum(p * term_row, axis=1, keepdims=True) for p in places]
    mean_grad = shares[0] * choice[0] + shares[1] * choice[1]
    logit_grad = jnp.zeros((toks, 128), F32)
    for k in range(2):
        pick = (choice[k] - mean_grad) / score_sum * picked[k] * (1.0 - picked[k])
        logit_grad = logit_grad + jnp.where(hits[k], pick, 0.0)
    my_cols = pl.ds(pl.multiple_of(z * cols_z, cols_z), cols_z)
    lg_rows = logit_grad.T[:16]
    parts = [p.astype(F32) for p in split3(lg_rows)]
    prod = dot(jnp.concatenate(parts, axis=0).astype(BF16), mod[:, my_cols])
    rc_own[...] = prod[:16] + prod[16:32] + prod[32:]
    rc_copy().start()
    far_sums(n - 1)

    def finish(b):
        gu_copy(b).wait_recv()
        dn_copy(b).wait_recv()
        cols = pl.ds(pl.multiple_of(b * kb, kb), kb)
        gu = gu_own[b] + gu_recv[b].astype(F32)
        gate_out[0, cols, :] = gu[:, :hidden].astype(BF16)
        up_out[0, cols, :] = gu[:, hidden:].astype(BF16)
        down_out[0, :, cols] = (dn_own[b] + dn_recv[b].astype(F32)).astype(BF16)

    rc_copy().wait_recv()
    rx_sum[...] = rc_own[...] + rc_sib[...]
    rx_buf[cx] = rx_sum[...]
    loop(1, n, lambda j: rx_copy(j, cx).start())
    loop(0, nb // 2, finish)
    loop(1, n, lambda j: rx_copy(j, lax.rem(cx + j, n)).wait_recv())
    total = rx_buf[0]
    for j in range(1, n):
        total = total + rx_buf[j]
    ry_sum[...] = total
    ry_buf[cy] = total
    loop(1, n, lambda j: ry_copy(j, cy).start())
    loop(nb // 2, nb, finish)

    def mod_part(i):
        return dot(split3(logit_grad)[i][:, :experts], router[:, my_cols])

    mod_grad = mod_part(0) + mod_part(1) + mod_part(2)
    gain = 1.0 + scale[:, my_cols]
    normed = (tokens[:, my_cols].astype(F32) - mean) * inv_std

    loop(1, slots, lambda k: b_copy(k).wait_recv())
    tiles = [b_recv[k].astype(F32) for k in range(slots)]
    rows_back = jnp.concatenate(
        [
            jnp.concatenate([t[:CAP] for t in tiles], axis=0),
            jnp.concatenate([t[CAP:] for t in tiles], axis=0),
        ],
        axis=1,
    ).astype(BF16)
    norm_grad = (mod_grad + dot(place_t[...], rows_back, TN)) * gain
    sums = [
        jnp.sum(norm_grad, axis=1, keepdims=True),
        jnp.sum(norm_grad * normed, axis=1, keepdims=True),
    ]
    lane = lax.broadcasted_iota(jnp.int32, (toks, 128), 1)
    sums_t = jnp.where(lane == 0, sums[0], jnp.where(lane == 1, sums[1], 0.0)).T
    ns_own[...] = sums_t[:8]
    loop(1, zn, lambda j: ns_copy(j).start())

    loop(1, n, lambda j: ry_copy(j, lax.rem(cy + j, n)).wait_recv())
    total = ry_buf[0]
    for j in range(1, n):
        total = total + ry_buf[j]
    router_out[...] = total

    loop(1, zn, lambda j: ns_copy(j).wait_recv())
    total = ns_own[...]
    for j in range(1, zn):
        total = total + ns_z[j]
    total = jnp.concatenate([total, jnp.zeros((120, toks), F32)], axis=0).T * (1.0 / width)
    input_out[...] = inv_std * (norm_grad - total[:, 0:1] - normed * total[:, 1:2])

    def drain_slot(k):
        sh_copy(k).wait_send()
        b_copy(k).wait_send()
        tb_copy(k).wait_send()

        @pl.when(k < RELAYED * n)
        def _():
            for c in range(3):
                part_copy(k, c).wait_send()

        @pl.when(k >= RELAYED * n)
        def _():
            direct_copy(k).wait_send()

    loop(1, slots, drain_slot)

    def drain_group(g):
        for i in range(5):
            near_copy(g, i).wait_send()
        for c in (1, 2):
            far_copy(g, c).wait_send()

        @pl.when(g < RELAYED)
        def _():
            for i in range(5):
                relay_copy(g, i, own_class(g, CLASS[i])).wait_send()

    loop(0, n, drain_group)

    def drain_ring(j):
        rx_copy(j, cx).wait_send()
        ry_copy(j, cy).wait_send()

    rc_copy().wait_send()
    loop(1, n, drain_ring)

    def drain_z(j):
        tz_copy(j).wait_send()
        ns_copy(j).wait_send()

    loop(1, zn, drain_z)

    def drain_b(b):
        gu_copy(b).wait_send()
        dn_copy(b).wait_send()

    loop(0, nb, drain_b)


def copy_kernel(count, *refs):
    sems = refs[-1]
    copies = [
        pltpu.make_async_copy(refs[i], refs[count + i], sems.at[i]) for i in range(count)
    ]
    for copy in copies:
        copy.start()
    for copy in copies:
        copy.wait()


def place_results(arrays):
    count = len(arrays)
    any_spec = pl.BlockSpec(memory_space=pl.ANY)
    return pl.pallas_call(
        functools.partial(copy_kernel, count),
        out_shape=tuple(jax.ShapeDtypeStruct(a.shape, a.dtype) for a in arrays),
        in_specs=[any_spec] * count,
        out_specs=(any_spec,) * count,
        scratch_shapes=[pltpu.SemaphoreType.DMA((count,))],
    )(*arrays)


def shards(
    tokens,
    cotangent,
    expert_ids,
    ada_shift,
    ada_scale,
    ada_gate,
    router_weight,
    gate_blocks,
    up_blocks,
    down_blocks,
):
    zn = lax.axis_size("exp")
    n = math.isqrt(lax.axis_size("seq") // 2)
    slots = n * n
    toks, width = tokens.shape
    experts = router_weight.shape[1]
    hidden = gate_blocks.shape[2]
    rows = slots * CAP
    cols_z = kb = width // zn
    nb = zn
    nt = -(-rows // 128)
    group = n * CAP
    dma = pltpu.SemaphoreType.DMA
    vm = pltpu.VMEM
    scratch = [
        vm((toks, width), BF16),
        vm((toks, width), BF16),
        vm((rows, toks), BF16),
        vm((slots, nb, 2 * CAP, kb), BF16),
        vm((n, nb, n, 2 * CAP, kb), BF16),
        vm((2, width, hidden), BF16),
        vm((2, width, hidden), BF16),
        vm((2, hidden, width), BF16),
        vm((rows, width), BF16),
        vm((rows, width), BF16),
        vm((rows, 4 * hidden), BF16),
        vm((rows, 2 * hidden), BF16),
        vm((nt * 128, hidden), F32),
        vm((group, 4 * hidden), F32),
        vm((group, 2 * hidden), F32),
        vm((n, 5, group, kb), BF16),
        vm((n, 5, group, kb), BF16),
        vm((n, 3, group, kb), F32),
        vm((n, 2, group, kb), BF16),
        vm((n, 2, group, kb), BF16),
        vm((slots, 2 * CAP, kb // 2), BF16),
        vm((slots, 2 * CAP, kb // 2), BF16),
        vm((8, 128), F32),
        vm((zn, 8, 128), F32),
        vm((8, 128), F32),
        vm((slots, 8, 128), F32),
        vm((8, 128), F32),
        vm((slots, 8, 128), F32),
        vm((nt * 128, 128), F32),
        vm((nb, kb, 2 * hidden), F32),
        vm((nb, kb, 2 * hidden), BF16),
        vm((nb, kb, 2 * hidden), BF16),
        vm((nb, hidden, kb), F32),
        vm((nb, hidden, kb), BF16),
        vm((nb, hidden, kb), BF16),
        vm((toks, 128), F32),
        vm((16, cols_z), F32),
        vm((16, cols_z), F32),
        vm((16, cols_z), F32),
        vm((n, 16, cols_z), F32),
        vm((16, cols_z), F32),
        vm((n, 16, cols_z), F32),
        vm((8, toks), F32),
        vm((zn, 8, toks), F32),
    ]
    sems = [3, 3, 3, (slots, 3), (slots, 3), (n, 5), (n, 5), (n, 5), (n, 5)]
    sems += [(n, 2), (n, 2), slots, slots, slots, slots]
    sems += [zn, zn, slots, slots, nb, nb, nb, nb]
    sems += [1, 1, n, n, n, n, zn, zn]
    scratch += [dma(s if isinstance(s, tuple) else (s,)) for s in sems]
    any_spec = pl.BlockSpec(memory_space=pl.ANY)
    vm_spec = pl.BlockSpec(memory_space=pltpu.VMEM)
    row = lambda v: v.reshape(1, width)
    results = pl.pallas_call(
        functools.partial(expert_kernel, n, zn),
        out_shape=(
            jax.ShapeDtypeStruct((toks, cols_z), F32),
            jax.ShapeDtypeStruct((16, cols_z), F32),
            jax.ShapeDtypeStruct((1, width, hidden), BF16),
            jax.ShapeDtypeStruct((1, width, hidden), BF16),
            jax.ShapeDtypeStruct((1, hidden, width), BF16),
        ),
        in_specs=[vm_spec] * 7 + [any_spec] * 3,
        out_specs=(vm_spec,) * 5,
        scratch_shapes=scratch,
        compiler_params=pltpu.CompilerParams(
            collective_id=0, has_side_effects=True, vmem_limit_bytes=60 * 1024 * 1024
        ),
        cost_estimate=pl.CostEstimate(
            flops=16 * rows * width * 2 * hidden, bytes_accessed=16 * 1024 * 1024, transcendentals=0
        ),
    )(
        tokens,
        cotangent,
        expert_ids.T,
        row(ada_shift),
        row(ada_scale),
        row(ada_gate),
        router_weight.T,
        gate_blocks,
        up_blocks,
        down_blocks,
    )
    grad_input, router_t, grad_gate, grad_up, grad_down = place_results(results)
    return (grad_input, router_t[:experts].T, grad_gate, grad_up, grad_down)


def solution(mesh):
    in_specs = (
        P("seq", None),
        P("seq", None),
        P("seq", None),
        P(),
        P(),
        P(),
        P(),
        P(("seq", "exp"), None, None),
        P(("seq", "exp"), None, None),
        P(("seq", "exp"), None, None),
    )
    out_specs = (
        P("seq", "exp"),
        P("exp", None),
        P(("seq", "exp"), None, None),
        P(("seq", "exp"), None, None),
        P(("seq", "exp"), None, None),
    )
    return jax.shard_map(shards, mesh=mesh, in_specs=in_specs, out_specs=out_specs, check_vma=False)
```

```python
import functools
import math

import jax
import jax.numpy as jnp
from jax import lax
from jax.experimental import pallas as pl
from jax.experimental.pallas import tpu as pltpu
from jax.sharding import PartitionSpec as P

CAP = 24
RELAYED = 2
ROLE = (1, 7, 4, 2, 5)
CLASS = (0, 0, 1, 1, 2)
SIGN = (1, -1, 1, -1, -1)
EPSILON = 1e-06
MESH = pl.DeviceIdType.MESH
F32 = jnp.float32
BF16 = jnp.bfloat16
NT = (((1,), (1,)), ((), ()))
TN = (((0,), (0,)), ((), ()))


def dot(a, b, dims=(((1,), (0,)), ((), ()))):
    return lax.dot_general(a, b, dims, preferred_element_type=F32)


def split_refs(refs, counts):
    parts, at = [], 0
    for count in counts:
        parts.append(refs[at : at + count])
        at += count
    return parts


def split3(x):
    hi = x.astype(BF16)
    rest = x - hi.astype(F32)
    mid = rest.astype(BF16)
    return hi, mid, (rest - mid.astype(F32)).astype(BF16)


def expert_kernel(n, zn, *refs):
    (
        (tokens, cotangent, ids, shift, scale, ada_gate, router, gate, up, down),
        (input_out, router_out, gate_out, up_out, down_out),
        (mod, og, place_t, send, recv, w_gate, w_up, w_down, rows_z, rows_wdy, d_gu, hid, hr),
        (gu_acc, r_acc, t_send, t_in, t_own, m_send, m_in, b_send, b_recv),
        (term_own, term_z, term_sum, term_b, sh_own, sh_recv, sh_col),
        (gu_own, gu_send, gu_recv, dn_own, dn_send, dn_recv),
        (logit_acc, rc_own, rc_sib, rx_sum, rx_buf, ry_sum, ry_buf, ns_own, ns_z),
        (w_local, w_ssem, w_rsem, d_ssem, d_rsem, f_ssem, f_rsem, a_ssem, a_rsem),
        (m_ssem, m_rsem, b_ssem, b_rsem, sh_ssem, sh_rsem),
        (tz_ssem, tz_rsem, tb_ssem, tb_rsem, g_ssem, g_rsem, h_ssem, h_rsem),
        (rc_ssem, rc_rsem, rx_ssem, rx_rsem, ry_ssem, ry_rsem, ns_ssem, ns_rsem),
    ) = split_refs(refs, (10, 5, 13, 9, 7, 6, 9, 9, 6, 8, 8))
    slots = n * n
    width = rows_z.shape[1]
    group = n * CAP
    hidden = w_gate.shape[2]
    kb = cols_z = width // zn
    nb = zn
    half = cols_z // 2
    toks = tokens.shape[0]
    seq = lax.axis_index("seq")
    z = lax.axis_index("exp")
    core = lax.rem(seq, 2)
    chip = seq // 2
    cy, cx = chip // n, lax.rem(chip, n)

    def offset(slot):
        dy = lax.rem(slot, n)
        dx = lax.rem(dy + slot // n, n)
        return dy, dx

    def target(slot):
        dy, dx = offset(slot)
        return (2 * (lax.rem(cy + dy, n) * n + lax.rem(cx + dx, n)) + core, z)

    def source(slot):
        dy, dx = offset(slot)
        return (2 * (lax.rem(cy - dy + n, n) * n + lax.rem(cx - dx + n, n)) + core, z)

    def z_peer(step):
        return (seq, lax.rem(z + step, zn))

    sibling = (seq + 1 - 2 * core, z)

    def remote(src, dst, ssem, rsem, dev):
        return pltpu.make_async_remote_copy(
            src_ref=src, dst_ref=dst, send_sem=ssem, recv_sem=rsem, device_id=dev, device_id_type=MESH
        )

    def plane(step):
        return lax.rem(z + step + 2 * zn, zn)

    def turn(g):
        return 1 - 2 * lax.rem(g, 2)

    def own_class(g, c):
        return plane(-3 * turn(g) * c)

    def direct_copy(slot):
        dst = recv.at[slot // n, :, lax.rem(slot, n)]
        return remote(send.at[slot], dst, d_ssem.at[slot, 0], d_rsem.at[slot, 0], target(slot))

    def part_copy(slot, c):
        g = slot // n
        r = own_class(g, c)
        dst = recv.at[g, r, lax.rem(slot, n)]
        return remote(send.at[slot, r], dst, d_ssem.at[slot, c], d_rsem.at[slot, c], target(slot))

    def relay_copy(g, i, r):
        to = (seq, plane(turn(g) * SIGN[i]))
        return remote(recv.at[g, r], recv.at[g, r], f_ssem.at[g, i], f_rsem.at[g, i], to)

    def near_copy(g, i):
        to = (seq, plane(-turn(g) * SIGN[i]))
        return remote(t_send.at[g, i], t_in.at[g, i], a_ssem.at[g, i], a_rsem.at[g, i], to)

    def far_copy(g, c):
        to = (seq, own_class(g, c))
        return remote(m_send.at[g, c - 1], m_in.at[g, c - 1], m_ssem.at[g, c - 1], m_rsem.at[g, c - 1], to)

    def sh_copy(slot):
        return remote(sh_own, sh_recv.at[slot], sh_ssem.at[slot], sh_rsem.at[slot], target(slot))

    def b_copy(slot):
        return remote(b_send.at[slot], b_recv.at[slot], b_ssem.at[slot], b_rsem.at[slot], source(slot))

    def tz_copy(step):
        return remote(term_own, term_z.at[step], tz_ssem.at[step], tz_rsem.at[step], z_peer(step))

    def tb_copy(slot):
        return remote(term_sum, term_b.at[slot], tb_ssem.at[slot], tb_rsem.at[slot], source(slot))

    def rc_copy():
        return remote(rc_own, rc_sib, rc_ssem.at[0], rc_rsem.at[0], sibling)

    def rx_copy(step, at):
        to = (2 * (cy * n + lax.rem(cx + step, n)) + core, z)
        return remote(rx_sum, rx_buf.at[at], rx_ssem.at[step], rx_rsem.at[at], to)

    def ry_copy(step, at):
        to = (2 * (lax.rem(cy + step, n) * n + cx) + core, z)
        return remote(ry_sum, ry_buf.at[at], ry_ssem.at[step], ry_rsem.at[at], to)

    def ns_copy(step):
        return remote(ns_own, ns_z.at[step], ns_ssem.at[step], ns_rsem.at[step], z_peer(step))

    def gu_copy(b):
        return remote(gu_send.at[b], gu_recv.at[b], g_ssem.at[b], g_rsem.at[b], sibling)

    def dn_copy(b):
        return remote(dn_send.at[b], dn_recv.at[b], h_ssem.at[b], h_rsem.at[b], sibling)

    weights = ((gate, w_gate), (up, w_up), (down, w_down))

    def w_copy(i):
        hbm, vmem = weights[i]
        return remote(hbm.at[0], vmem.at[1], w_ssem.at[i], w_rsem.at[i], sibling)

    def w_copy_local(i):
        hbm, vmem = weights[i]
        return pltpu.make_async_copy(hbm.at[0], vmem.at[0], w_local.at[i])

    def loop(lo, hi, body):
        def step(i, carry):
            body(i)
            return carry

        lax.fori_loop(lo, hi, step, 0)

    barrier = pltpu.get_barrier_semaphore()
    loop(
        1,
        slots,
        lambda k: pl.semaphore_signal(barrier, inc=1, device_id=target(k), device_id_type=MESH),
    )
    loop(
        1,
        zn,
        lambda j: pl.semaphore_signal(barrier, inc=1, device_id=z_peer(j), device_id_type=MESH),
    )
    pl.semaphore_signal(barrier, inc=1, device_id=sibling, device_id_type=MESH)
    for i in range(3):
        w_copy_local(i).start()

    def moment(center):
        def body(b, acc):
            cols = pl.ds(pl.multiple_of(b * kb, kb), kb)
            x = tokens[:, cols].astype(F32)
            if center is not None:
                x = (x - center) * (x - center)
            return acc + jnp.sum(x, axis=1, keepdims=True)

        return lax.fori_loop(0, nb, body, jnp.zeros((toks, 1), F32)) * (1.0 / width)

    mean = moment(None)
    inv_std = lax.rsqrt(moment(mean) + EPSILON)
    logit_acc[...] = jnp.zeros_like(logit_acc)
    experts = router.shape[0]

    def modulate(b):
        cols = pl.ds(pl.multiple_of(b * kb, kb), kb)
        normed = (tokens[:, cols].astype(F32) - mean) * inv_std
        m = (normed * (1.0 + scale[:, cols]) + shift[:, cols]).astype(BF16)
        mod[:, cols] = m
        og[:, cols] = (ada_gate[:, cols] * cotangent[:, cols].astype(F32)).astype(BF16)
        logit_acc[:, :experts] += dot(m, router[:, cols], NT)

    loop(0, nb, modulate)
    scores = jax.nn.sigmoid(logit_acc[...])
    expert_at = lax.broadcasted_iota(jnp.int32, (toks, 128), 1)
    ids_t = jnp.concatenate([ids[...].astype(F32), jnp.zeros((126, toks), F32)], axis=0).T
    hits = [expert_at.astype(F32) == ids_t[:, k : k + 1] for k in range(2)]
    picked = [jnp.sum(jnp.where(h, scores, 0.0), axis=1, keepdims=True) for h in hits]
    score_sum = picked[0] + picked[1]
    shares = [p / score_sum for p in picked]
    share_r = [s.astype(BF16).astype(F32) for s in shares]
    routed = jnp.where(hits[0] | hits[1], 1.0, 0.0)
    tok_at = lax.broadcasted_iota(jnp.int32, (toks, toks), 0)
    earlier = jnp.where(tok_at > lax.broadcasted_iota(jnp.int32, (toks, toks), 1), 1.0, 0.0)
    rank = dot(earlier.astype(BF16), routed.astype(BF16))
    bits = n.bit_length() - 1
    e_dy = ((expert_at >> bits) - cy) & (n - 1)
    e_dx = ((expert_at & (n - 1)) - cx) & (n - 1)
    base = ((((e_dx - e_dy) & (n - 1)) * n + e_dy) * CAP).astype(F32) + rank
    slot_at = lax.broadcasted_iota(jnp.int32, (toks, slots * CAP), 1).astype(F32)
    places = [
        jnp.where(slot_at == jnp.sum(jnp.where(h, base, 0.0), axis=1, keepdims=True), 1.0, 0.0)
        for h in hits
    ]
    place_t[...] = (places[0] + places[1]).T.astype(BF16)
    nt = hr.shape[0] // 128
    flat = lax.broadcasted_iota(jnp.int32, (8, 128), 0) * 128 + lax.broadcasted_iota(
        jnp.int32, (8, 128), 1
    )

    def merge(own, others):
        out = jnp.where(flat < CAP, own, 0.0)
        for k in range(1, slots):
            out = jnp.where((flat >= k * CAP) & (flat < (k + 1) * CAP), others[k], out)
        return out

    share_row = jnp.sum(places[0] * share_r[0] + places[1] * share_r[1], axis=0, keepdims=True)
    if nt * 128 > slots * CAP:
        share_row = jnp.concatenate(
            [share_row, jnp.zeros((1, nt * 128 - slots * CAP), F32)], axis=1
        )
    sh_own[...] = jnp.zeros_like(sh_own)
    for i in range(nt):
        sh_own[i : i + 1, :] = share_row[:, 128 * i : 128 * (i + 1)]

    hr[...] = jnp.zeros_like(hr)
    pl.semaphore_wait(barrier, slots + zn - 1)
    for i in range(3):
        w_copy(i).start()

    loop(1, slots, lambda k: sh_copy(k).start())

    def fill(g, b):
        rows = pl.ds(pl.multiple_of(g * group, group), group)
        cols = pl.ds(pl.multiple_of(b * kb, kb), kb)
        zc = dot(place_t[rows, :], mod[:, cols])
        dc = dot(place_t[rows, :], og[:, cols])
        for i in range(n):
            at = slice(i * CAP, (i + 1) * CAP)
            pair = jnp.concatenate([zc[at], dc[at]], axis=0).astype(BF16)

            @pl.when(g * n + i > 0)
            def _():
                send[g * n + i, b] = pair

            if i == 0:

                @pl.when(g == 0)
                def _():
                    recv[0, b, 0] = pair

    def each_remote(g, body):
        def one(i):
            @pl.when(g * n + i > 0)
            def _():
                body(g * n + i)

        loop(0, n, one)

    def relayed_start(g):
        for c in range(3):
            fill(g, own_class(g, c))
            each_remote(g, lambda slot: part_copy(slot, c).start())

    def relayed_arrive(g):
        for c in range(3):
            each_remote(g, lambda slot: part_copy(slot, c).wait_recv())
            for i in range(5):
                if CLASS[i] == c:
                    relay_copy(g, i, own_class(g, c)).start()

    loop(0, RELAYED, relayed_start)
    loop(RELAYED, n, lambda g: loop(0, nb, lambda b: fill(g, b)))
    for g in range(RELAYED):
        relayed_arrive(g)
        if g == 0:
            loop(RELAYED * n, (RELAYED + 1) * n, lambda k: direct_copy(k).start())
    loop(1, slots, lambda k: sh_copy(k).wait_recv())
    shares_in = merge(sh_own[...], sh_recv)
    shares_in = jnp.concatenate([shares_in, jnp.zeros((120, 128), F32)], axis=0).T
    for i in range(nt):
        sh_col[128 * i : 128 * (i + 1), :] = jnp.broadcast_to(shares_in[:, i : i + 1], (128, 128))
    for i in range(3):
        w_copy_local(i).wait()
        w_copy(i).wait()

    def wait_group(g):
        @pl.when(g < RELAYED)
        def _():
            for i in range(5):
                relay_copy(g, i, plane(-turn(g) * ROLE[i])).wait_recv()

        @pl.when(g >= RELAYED)
        def _():
            loop(0, n, lambda i: direct_copy(g * n + i).wait_recv())

        @pl.when(g == RELAYED - 1)
        def _():
            loop((RELAYED + 1) * n, slots, lambda k: direct_copy(k).start())

    def near_sums(g):
        for i in range(5):
            near_copy(g, i).wait_recv()
        for c in (1, 2, 0):
            total = t_own[g, c]
            for i in range(5):
                if CLASS[i] == c:
                    total = total + t_in[g, i].astype(F32)
            if c > 0:
                m_send[g, c - 1] = total.astype(BF16)
                far_copy(g, c).start()
            else:
                t_own[g, 0] = total

    def far_sums(g):
        for c in (1, 2):
            far_copy(g, c).wait_recv()
        total = t_own[g, 0] + m_in[g, 0].astype(F32) + m_in[g, 1].astype(F32)
        for i in range(n):
            slot = g * n + i
            part = total[i * CAP : (i + 1) * CAP]
            packed = jnp.concatenate([part[:, :half], part[:, half:]], axis=0).astype(BF16)
            if i > 0:
                b_send[slot] = packed
                b_copy(slot).start()
            else:

                @pl.when(slot > 0)
                def _():
                    b_send[slot] = packed
                    b_copy(slot).start()

                @pl.when(slot == 0)
                def _():
                    b_recv[0] = packed

    def compute_group(g):
        wait_group(g)
        rows = pl.ds(pl.multiple_of(g * group, group), group)
        share = sh_col[rows, :1]
        gu_acc[...] = jnp.zeros_like(gu_acc)
        r_acc[...] = jnp.zeros_like(r_acc)

        def forward(b):
            cols = pl.ds(pl.multiple_of(b * kb, kb), kb)
            tiles = [recv[g, b, i].astype(F32) for i in range(n)]
            zb = jnp.concatenate([t[:CAP] for t in tiles], axis=0).astype(BF16)
            dyf = jnp.concatenate([t[CAP:] for t in tiles], axis=0)
            rows_z[rows, cols] = zb
            rows_wdy[rows, cols] = (share * dyf).astype(BF16)
            w_gu = [w_gate[0, cols, :], w_gate[1, cols, :], w_up[0, cols, :], w_up[1, cols, :]]
            gu_acc[...] += dot(zb, jnp.concatenate(w_gu, axis=1))
            wd = jnp.concatenate([w_down[0, :, cols], w_down[1, :, cols]], axis=0)
            r_acc[...] += dot(dyf.astype(BF16), wd, NT)

        loop(0, nb, forward)
        gv, uv, rv = gu_acc[:, : 2 * hidden], gu_acc[:, 2 * hidden :], r_acc[...]
        sig = jax.nn.sigmoid(gv)
        act = gv * sig
        hv = act * uv
        prod = hv * rv
        hr[rows, :] = prod[:, :hidden] + prod[:, hidden:]
        scaled = share * rv
        du = (scaled * act).astype(BF16)
        dg = (scaled * uv * sig * (1.0 + gv * (1.0 - sig))).astype(BF16)
        d_gu[rows, :] = jnp.concatenate(
            [dg[:, :hidden], du[:, :hidden], dg[:, hidden:], du[:, hidden:]], axis=1
        )
        hid[rows, :] = hv.astype(BF16)

        def backward(r):
            wrows = pl.ds(pl.multiple_of(r * kb, kb), kb)
            w_gu = [w_gate[0, wrows, :], w_up[0, wrows, :], w_gate[1, wrows, :], w_up[1, wrows, :]]
            return dot(d_gu[rows, :], jnp.concatenate(w_gu, axis=1), NT)

        for i in range(5):
            t_send[g, i] = backward(plane(-turn(g) * ROLE[i])).astype(BF16)
            near_copy(g, i).start()
        for c in range(3):
            t_own[g, c] = backward(own_class(g, c))

    def group_step(g):
        compute_group(g)

        @pl.when(g > 0)
        def _():
            near_sums(g - 1)

        @pl.when(g > 1)
        def _():
            far_sums(g - 2)

    loop(0, n, group_step)

    term_own[...] = jnp.zeros_like(term_own)
    for i in range(nt):
        tile = hr[128 * i : 128 * (i + 1), :]
        term_own[i : i + 1, :] = jnp.sum(tile.T, axis=0, keepdims=True)
    loop(1, zn, lambda j: tz_copy(j).start())

    def weight_grads(b):
        cols = pl.ds(pl.multiple_of(b * kb, kb), kb)
        gu = dot(rows_z[:, cols], d_gu[...], TN)
        gu_own[b] = gu[:, : 2 * hidden]
        gu_send[b] = gu[:, 2 * hidden :].astype(BF16)
        gu_copy(b).start()
        dn = dot(hid[...], rows_wdy[:, cols], TN)
        dn_own[b] = dn[:hidden]
        dn_send[b] = dn[hidden:].astype(BF16)
        dn_copy(b).start()

    loop(0, nb // 4, weight_grads)
    near_sums(n - 1)
    far_sums(n - 2)
    loop(nb // 4, nb // 2, weight_grads)
    loop(1, zn, lambda j: tz_copy(j).wait_recv())
    total = term_own[...]
    for j in range(1, zn):
        total = total + term_z[j]
    term_sum[...] = total
    loop(1, slots, lambda k: tb_copy(k).start())
    loop(nb // 2, nb, weight_grads)
    loop(1, slots, lambda k: tb_copy(k).wait_recv())
    terms = merge(term_sum[...], term_b)
    term_row = jnp.concatenate([terms[i : i + 1] for i in range(nt)], axis=1)[:, : slots * CAP]
    choice = [jnp.sum(p * term_row, axis=1, keepdims=True) for p in places]
    mean_grad = shares[0] * choice[0] + shares[1] * choice[1]
    logit_grad = jnp.zeros((toks, 128), F32)
    for k in range(2):
        pick = (choice[k] - mean_grad) / score_sum * picked[k] * (1.0 - picked[k])
        logit_grad = logit_grad + jnp.where(hits[k], pick, 0.0)
    my_cols = pl.ds(pl.multiple_of(z * cols_z, cols_z), cols_z)
    lg_rows = logit_grad.T[:16]
    parts = [p.astype(F32) for p in split3(lg_rows)]
    prod = dot(jnp.concatenate(parts, axis=0).astype(BF16), mod[:, my_cols])
    rc_own[...] = prod[:16] + prod[16:32] + prod[32:]
    rc_copy().start()
    far_sums(n - 1)

    def finish(b):
        gu_copy(b).wait_recv()
        dn_copy(b).wait_recv()
        cols = pl.ds(pl.multiple_of(b * kb, kb), kb)
        gu = gu_own[b] + gu_recv[b].astype(F32)
        gate_out[0, cols, :] = gu[:, :hidden].astype(BF16)
        up_out[0, cols, :] = gu[:, hidden:].astype(BF16)
        down_out[0, :, cols] = (dn_own[b] + dn_recv[b].astype(F32)).astype(BF16)

    rc_copy().wait_recv()
    rx_sum[...] = rc_own[...] + rc_sib[...]
    rx_buf[cx] = rx_sum[...]
    loop(1, n, lambda j: rx_copy(j, cx).start())
    loop(0, nb // 2, finish)
    loop(1, n, lambda j: rx_copy(j, lax.rem(cx + j, n)).wait_recv())
    total = rx_buf[0]
    for j in range(1, n):
        total = total + rx_buf[j]
    ry_sum[...] = total
    ry_buf[cy] = total
    loop(1, n, lambda j: ry_copy(j, cy).start())
    loop(nb // 2, nb, finish)

    def mod_part(i):
        return dot(split3(logit_grad)[i][:, :experts], router[:, my_cols])

    mod_grad = mod_part(0) + mod_part(1) + mod_part(2)
    gain = 1.0 + scale[:, my_cols]
    normed = (tokens[:, my_cols].astype(F32) - mean) * inv_std

    loop(1, slots, lambda k: b_copy(k).wait_recv())
    tiles = [b_recv[k].astype(F32) for k in range(slots)]
    rows_back = jnp.concatenate(
        [
            jnp.concatenate([t[:CAP] for t in tiles], axis=0),
            jnp.concatenate([t[CAP:] for t in tiles], axis=0),
        ],
        axis=1,
    ).astype(BF16)
    norm_grad = (mod_grad + dot(place_t[...], rows_back, TN)) * gain
    sums = [
        jnp.sum(norm_grad, axis=1, keepdims=True),
        jnp.sum(norm_grad * normed, axis=1, keepdims=True),
    ]
    lane = lax.broadcasted_iota(jnp.int32, (toks, 128), 1)
    sums_t = jnp.where(lane == 0, sums[0], jnp.where(lane == 1, sums[1], 0.0)).T
    ns_own[...] = sums_t[:8]
    loop(1, zn, lambda j: ns_copy(j).start())

    loop(1, n, lambda j: ry_copy(j, lax.rem(cy + j, n)).wait_recv())
    total = ry_buf[0]
    for j in range(1, n):
        total = total + ry_buf[j]
    router_out[...] = total

    loop(1, zn, lambda j: ns_copy(j).wait_recv())
    total = ns_own[...]
    for j in range(1, zn):
        total = total + ns_z[j]
    total = jnp.concatenate([total, jnp.zeros((120, toks), F32)], axis=0).T * (1.0 / width)
    input_out[...] = inv_std * (norm_grad - total[:, 0:1] - normed * total[:, 1:2])

    def drain_slot(k):
        sh_copy(k).wait_send()
        b_copy(k).wait_send()
        tb_copy(k).wait_send()

        @pl.when(k < RELAYED * n)
        def _():
            for c in range(3):
                part_copy(k, c).wait_send()

        @pl.when(k >= RELAYED * n)
        def _():
            direct_copy(k).wait_send()

    loop(1, slots, drain_slot)

    def drain_group(g):
        for i in range(5):
            near_copy(g, i).wait_send()
        for c in (1, 2):
            far_copy(g, c).wait_send()

        @pl.when(g < RELAYED)
        def _():
            for i in range(5):
                relay_copy(g, i, own_class(g, CLASS[i])).wait_send()

    loop(0, n, drain_group)

    def drain_ring(j):
        rx_copy(j, cx).wait_send()
        ry_copy(j, cy).wait_send()

    rc_copy().wait_send()
    loop(1, n, drain_ring)

    def drain_z(j):
        tz_copy(j).wait_send()
        ns_copy(j).wait_send()

    loop(1, zn, drain_z)

    def drain_b(b):
        gu_copy(b).wait_send()
        dn_copy(b).wait_send()

    loop(0, nb, drain_b)


def copy_kernel(count, *refs):
    sems = refs[-1]
    held = refs[2 * count : 3 * count]
    arrive = [pltpu.make_async_copy(refs[i], held[i], sems.at[0, i]) for i in range(count)]
    leave = [
        pltpu.make_async_copy(held[i], refs[count + i], sems.at[1, i]) for i in range(count)
    ]
    for copy in arrive:
        copy.start()
    for i in range(count):
        arrive[i].wait()
        leave[i].start()
    for copy in leave:
        copy.wait()


def place_results(arrays):
    count = len(arrays)
    any_spec = pl.BlockSpec(memory_space=pl.ANY)
    return pl.pallas_call(
        functools.partial(copy_kernel, count),
        out_shape=tuple(jax.ShapeDtypeStruct(a.shape, a.dtype) for a in arrays),
        in_specs=[any_spec] * count,
        out_specs=(any_spec,) * count,
        scratch_shapes=[pltpu.VMEM(a.shape, a.dtype) for a in arrays]
        + [pltpu.SemaphoreType.DMA((2, count))],
        compiler_params=pltpu.CompilerParams(vmem_limit_bytes=16 * 1024 * 1024),
    )(*arrays)


def shards(
    tokens,
    cotangent,
    expert_ids,
    ada_shift,
    ada_scale,
    ada_gate,
    router_weight,
    gate_blocks,
    up_blocks,
    down_blocks,
):
    zn = lax.axis_size("exp")
    n = math.isqrt(lax.axis_size("seq") // 2)
    slots = n * n
    toks, width = tokens.shape
    experts = router_weight.shape[1]
    hidden = gate_blocks.shape[2]
    rows = slots * CAP
    cols_z = kb = width // zn
    nb = zn
    nt = -(-rows // 128)
    group = n * CAP
    dma = pltpu.SemaphoreType.DMA
    vm = pltpu.VMEM
    scratch = [
        vm((toks, width), BF16),
        vm((toks, width), BF16),
        vm((rows, toks), BF16),
        vm((slots, nb, 2 * CAP, kb), BF16),
        vm((n, nb, n, 2 * CAP, kb), BF16),
        vm((2, width, hidden), BF16),
        vm((2, width, hidden), BF16),
        vm((2, hidden, width), BF16),
        vm((rows, width), BF16),
        vm((rows, width), BF16),
        vm((rows, 4 * hidden), BF16),
        vm((rows, 2 * hidden), BF16),
        vm((nt * 128, hidden), F32),
        vm((group, 4 * hidden), F32),
        vm((group, 2 * hidden), F32),
        vm((n, 5, group, kb), BF16),
        vm((n, 5, group, kb), BF16),
        vm((n, 3, group, kb), F32),
        vm((n, 2, group, kb), BF16),
        vm((n, 2, group, kb), BF16),
        vm((slots, 2 * CAP, kb // 2), BF16),
        vm((slots, 2 * CAP, kb // 2), BF16),
        vm((8, 128), F32),
        vm((zn, 8, 128), F32),
        vm((8, 128), F32),
        vm((slots, 8, 128), F32),
        vm((8, 128), F32),
        vm((slots, 8, 128), F32),
        vm((nt * 128, 128), F32),
        vm((nb, kb, 2 * hidden), F32),
        vm((nb, kb, 2 * hidden), BF16),
        vm((nb, kb, 2 * hidden), BF16),
        vm((nb, hidden, kb), F32),
        vm((nb, hidden, kb), BF16),
        vm((nb, hidden, kb), BF16),
        vm((toks, 128), F32),
        vm((16, cols_z), F32),
        vm((16, cols_z), F32),
        vm((16, cols_z), F32),
        vm((n, 16, cols_z), F32),
        vm((16, cols_z), F32),
        vm((n, 16, cols_z), F32),
        vm((8, toks), F32),
        vm((zn, 8, toks), F32),
    ]
    sems = [3, 3, 3, (slots, 3), (slots, 3), (n, 5), (n, 5), (n, 5), (n, 5)]
    sems += [(n, 2), (n, 2), slots, slots, slots, slots]
    sems += [zn, zn, slots, slots, nb, nb, nb, nb]
    sems += [1, 1, n, n, n, n, zn, zn]
    scratch += [dma(s if isinstance(s, tuple) else (s,)) for s in sems]
    any_spec = pl.BlockSpec(memory_space=pl.ANY)
    vm_spec = pl.BlockSpec(memory_space=pltpu.VMEM)
    row = lambda v: v.reshape(1, width)
    results = pl.pallas_call(
        functools.partial(expert_kernel, n, zn),
        out_shape=(
            jax.ShapeDtypeStruct((toks, cols_z), F32),
            jax.ShapeDtypeStruct((16, cols_z), F32),
            jax.ShapeDtypeStruct((1, width, hidden), BF16),
            jax.ShapeDtypeStruct((1, width, hidden), BF16),
            jax.ShapeDtypeStruct((1, hidden, width), BF16),
        ),
        in_specs=[vm_spec] * 7 + [any_spec] * 3,
        out_specs=(vm_spec,) * 5,
        scratch_shapes=scratch,
        compiler_params=pltpu.CompilerParams(
            collective_id=0, has_side_effects=True, vmem_limit_bytes=60 * 1024 * 1024
        ),
        cost_estimate=pl.CostEstimate(
            flops=16 * rows * width * 2 * hidden, bytes_accessed=16 * 1024 * 1024, transcendentals=0
        ),
    )(
        tokens,
        cotangent,
        expert_ids.T,
        row(ada_shift),
        row(ada_scale),
        row(ada_gate),
        router_weight.T,
        gate_blocks,
        up_blocks,
        down_blocks,
    )
    grad_input, router_t, grad_gate, grad_up, grad_down = place_results(results)
    return (grad_input, router_t[:experts].T, grad_gate, grad_up, grad_down)


def solution(mesh):
    in_specs = (
        P("seq", None),
        P("seq", None),
        P("seq", None),
        P(),
        P(),
        P(),
        P(),
        P(("seq", "exp"), None, None),
        P(("seq", "exp"), None, None),
        P(("seq", "exp"), None, None),
    )
    out_specs = (
        P("seq", "exp"),
        P("exp", None),
        P(("seq", "exp"), None, None),
        P(("seq", "exp"), None, None),
        P(("seq", "exp"), None, None),
    )
    return jax.shard_map(shards, mesh=mesh, in_specs=in_specs, out_specs=out_specs, check_vma=False)
```

```python
import functools
import math

import jax
import jax.numpy as jnp
from jax import lax
from jax.experimental import pallas as pl
from jax.experimental.pallas import tpu as pltpu
from jax.sharding import PartitionSpec as P

CAP = 24
RELAYED = 2
ROLE = (1, 7, 4, 2, 5)
CLASS = (0, 0, 1, 1, 2)
SIGN = (1, -1, 1, -1, -1)
EPSILON = 1e-06
MESH = pl.DeviceIdType.MESH
F32 = jnp.float32
BF16 = jnp.bfloat16
NT = (((1,), (1,)), ((), ()))
TN = (((0,), (0,)), ((), ()))


def dot(a, b, dims=(((1,), (0,)), ((), ()))):
    return lax.dot_general(a, b, dims, preferred_element_type=F32)


def split_refs(refs, counts):
    parts, at = [], 0
    for count in counts:
        parts.append(refs[at : at + count])
        at += count
    return parts


def split3(x):
    hi = x.astype(BF16)
    rest = x - hi.astype(F32)
    mid = rest.astype(BF16)
    return hi, mid, (rest - mid.astype(F32)).astype(BF16)


def expert_kernel(n, zn, *refs):
    (
        (tokens, cotangent, ids, shift, scale, ada_gate, router, gate, up, down),
        (input_out, router_out, gate_out, up_out, down_out),
        (mod, og, place_t, send, recv, w_gate, w_up, w_down, rows_z, rows_wdy, d_gu, hid, hr),
        (gu_acc, r_acc, t_send, t_in, t_own, m_send, m_in, b_send, b_recv, e_acc),
        (term_own, term_z, term_sum, term_b, sh_own, sh_recv, sh_col),
        (gu_own, gu_send, gu_recv, dn_own, dn_send, dn_recv),
        (logit_acc, stat, rc_own, rc_sib, rx_sum, rx_buf, ry_sum, ry_buf, ns_own, ns_z),
        (w_local, w_ssem, w_rsem, d_ssem, d_rsem, f_ssem, f_rsem, a_ssem, a_rsem),
        (m_ssem, m_rsem, b_ssem, b_rsem, sh_ssem, sh_rsem),
        (tz_ssem, tz_rsem, tb_ssem, tb_rsem, g_ssem, g_rsem, h_ssem, h_rsem),
        (rc_ssem, rc_rsem, rx_ssem, rx_rsem, ry_ssem, ry_rsem, ns_ssem, ns_rsem),
    ) = split_refs(refs, (10, 5, 13, 10, 7, 6, 10, 9, 6, 8, 8))
    slots = n * n
    width = rows_z.shape[1]
    group = n * CAP
    hidden = w_gate.shape[2]
    kb = cols_z = width // zn
    nb = zn
    half = cols_z // 2
    toks = tokens.shape[0]
    seq = lax.axis_index("seq")
    z = lax.axis_index("exp")
    core = lax.rem(seq, 2)
    chip = seq // 2
    cy, cx = chip // n, lax.rem(chip, n)

    def offset(slot):
        dy = lax.rem(slot, n)
        dx = lax.rem(dy + slot // n, n)
        return dy, dx

    def target(slot):
        dy, dx = offset(slot)
        return (2 * (lax.rem(cy + dy, n) * n + lax.rem(cx + dx, n)) + core, z)

    def source(slot):
        dy, dx = offset(slot)
        return (2 * (lax.rem(cy - dy + n, n) * n + lax.rem(cx - dx + n, n)) + core, z)

    def z_peer(step):
        return (seq, lax.rem(z + step, zn))

    sibling = (seq + 1 - 2 * core, z)

    def remote(src, dst, ssem, rsem, dev):
        return pltpu.make_async_remote_copy(
            src_ref=src, dst_ref=dst, send_sem=ssem, recv_sem=rsem, device_id=dev, device_id_type=MESH
        )

    def plane(step):
        return lax.rem(z + step + 2 * zn, zn)

    turn = 1 - 2 * core

    def own_class(c):
        return plane(-3 * turn * c)

    def direct_copy(slot):
        dst = recv.at[slot // n, :, lax.rem(slot, n)]
        return remote(send.at[slot], dst, d_ssem.at[slot, 0], d_rsem.at[slot, 0], target(slot))

    def part_copy(slot, c):
        g = slot // n
        r = own_class(c)
        dst = recv.at[g, r, lax.rem(slot, n)]
        return remote(send.at[slot, r], dst, d_ssem.at[slot, c], d_rsem.at[slot, c], target(slot))

    def relay_copy(g, i, r):
        to = (seq, plane(turn * SIGN[i]))
        return remote(recv.at[g, r], recv.at[g, r], f_ssem.at[g, i], f_rsem.at[g, i], to)

    def near_copy(g, i):
        to = (seq, plane(-turn * SIGN[i]))
        return remote(t_send.at[g, i], t_in.at[g, i], a_ssem.at[g, i], a_rsem.at[g, i], to)

    def far_copy(c):
        to = (seq, own_class(c))
        return remote(m_send.at[c - 1], m_in.at[c - 1], m_ssem.at[c - 1], m_rsem.at[c - 1], to)

    def sh_copy(slot):
        return remote(sh_own, sh_recv.at[slot], sh_ssem.at[slot], sh_rsem.at[slot], target(slot))

    def b_copy(slot):
        return remote(b_send.at[slot], b_recv.at[slot], b_ssem.at[slot], b_rsem.at[slot], source(slot))

    def tz_copy(step):
        return remote(term_own, term_z.at[step], tz_ssem.at[step], tz_rsem.at[step], z_peer(step))

    def tb_copy(slot):
        return remote(term_sum, term_b.at[slot], tb_ssem.at[slot], tb_rsem.at[slot], source(slot))

    def rc_copy():
        return remote(rc_own, rc_sib, rc_ssem.at[0], rc_rsem.at[0], sibling)

    def rx_copy(step, at):
        to = (2 * (cy * n + lax.rem(cx + step, n)) + core, z)
        return remote(rx_sum, rx_buf.at[at], rx_ssem.at[step], rx_rsem.at[at], to)

    def ry_copy(step, at):
        to = (2 * (lax.rem(cy + step, n) * n + cx) + core, z)
        return remote(ry_sum, ry_buf.at[at], ry_ssem.at[step], ry_rsem.at[at], to)

    def ns_copy(step):
        return remote(ns_own, ns_z.at[step], ns_ssem.at[step], ns_rsem.at[step], z_peer(step))

    def gu_copy(b):
        return remote(gu_send.at[b], gu_recv.at[b], g_ssem.at[b], g_rsem.at[b], sibling)

    def dn_copy(b):
        return remote(dn_send.at[b], dn_recv.at[b], h_ssem.at[b], h_rsem.at[b], sibling)

    weights = ((gate, w_gate), (up, w_up), (down, w_down))

    def w_copy(i):
        hbm, vmem = weights[i]
        return remote(hbm.at[0], vmem.at[1], w_ssem.at[i], w_rsem.at[i], sibling)

    def w_copy_local(i):
        hbm, vmem = weights[i]
        return pltpu.make_async_copy(hbm.at[0], vmem.at[0], w_local.at[i])

    def loop(lo, hi, body):
        def step(i, carry):
            body(i)
            return carry

        lax.fori_loop(lo, hi, step, 0)

    barrier = pltpu.get_barrier_semaphore()
    loop(
        1,
        slots,
        lambda k: pl.semaphore_signal(barrier, inc=1, device_id=target(k), device_id_type=MESH),
    )
    loop(
        1,
        zn,
        lambda j: pl.semaphore_signal(barrier, inc=1, device_id=z_peer(j), device_id_type=MESH),
    )
    pl.semaphore_signal(barrier, inc=1, device_id=sibling, device_id_type=MESH)
    for i in range(3):
        w_copy_local(i).start()

    experts = router.shape[0]
    expert_at = lax.broadcasted_iota(jnp.int32, (toks, 128), 1)
    ids_t = jnp.concatenate([ids[...].astype(F32), jnp.zeros((126, toks), F32)], axis=0).T
    hits = [expert_at.astype(F32) == ids_t[:, k : k + 1] for k in range(2)]
    routed = jnp.where(hits[0] | hits[1], 1.0, 0.0)
    tok_at = lax.broadcasted_iota(jnp.int32, (toks, toks), 0)
    earlier = jnp.where(tok_at > lax.broadcasted_iota(jnp.int32, (toks, toks), 1), 1.0, 0.0)
    rank = dot(earlier.astype(BF16), routed.astype(BF16))
    bits = n.bit_length() - 1
    e_dy = ((expert_at >> bits) - cy) & (n - 1)
    e_dx = ((expert_at & (n - 1)) - cx) & (n - 1)
    base = ((((e_dx - e_dy) & (n - 1)) * n + e_dy) * CAP).astype(F32) + rank
    slot_at = lax.broadcasted_iota(jnp.int32, (toks, slots * CAP), 1).astype(F32)
    places = [
        jnp.where(slot_at == jnp.sum(jnp.where(h, base, 0.0), axis=1, keepdims=True), 1.0, 0.0)
        for h in hits
    ]
    place_t[...] = (places[0] + places[1]).T.astype(BF16)
    nt = hr.shape[0] // 128
    flat = lax.broadcasted_iota(jnp.int32, (8, 128), 0) * 128 + lax.broadcasted_iota(
        jnp.int32, (8, 128), 1
    )

    def merge(own, others):
        out = jnp.where(flat < CAP, own, 0.0)
        for k in range(1, slots):
            out = jnp.where((flat >= k * CAP) & (flat < (k + 1) * CAP), others[k], out)
        return out

    def modulate(i):
        rows = pl.ds(pl.multiple_of(i * 16, 16), 16)
        x = tokens[rows, :].astype(F32)
        center = jnp.sum(x, axis=1, keepdims=True) * (1.0 / width)
        x = x - center
        inv = lax.rsqrt(jnp.sum(x * x, axis=1, keepdims=True) * (1.0 / width) + EPSILON)
        mod[rows, :] = (x * inv * (1.0 + scale[...]) + shift[...]).astype(BF16)
        og[rows, :] = (ada_gate[...] * cotangent[rows, :].astype(F32)).astype(BF16)
        stat[rows, :] = jnp.where(lax.broadcasted_iota(jnp.int32, (16, 128), 1) == 0, center, inv)

    loop(0, toks // 16, modulate)
    mean, inv_std = stat[:, 0:1], stat[:, 1:2]
    hr[...] = jnp.zeros_like(hr)
    pl.semaphore_wait(barrier, slots + zn - 1)
    for i in range(3):
        w_copy(i).start()

    def fill(g, b):
        rows = pl.ds(pl.multiple_of(g * group, group), group)
        cols = pl.ds(pl.multiple_of(b * kb, kb), kb)
        zc = dot(place_t[rows, :], mod[:, cols])
        dc = dot(place_t[rows, :], og[:, cols])
        for i in range(n):
            at = slice(i * CAP, (i + 1) * CAP)
            pair = jnp.concatenate([zc[at], dc[at]], axis=0).astype(BF16)

            @pl.when(g * n + i > 0)
            def _():
                send[g * n + i, b] = pair

            if i == 0:

                @pl.when(g == 0)
                def _():
                    recv[0, b, 0] = pair

    def each_remote(g, body):
        def one(i):
            @pl.when(g * n + i > 0)
            def _():
                body(g * n + i)

        loop(0, n, one)

    def relayed_start(g):
        for c in range(3):
            fill(g, own_class(c))
            each_remote(g, lambda slot: part_copy(slot, c).start())

    def relayed_arrive(g):
        for c in range(3):
            each_remote(g, lambda slot: part_copy(slot, c).wait_recv())
            for i in range(5):
                if CLASS[i] == c:
                    relay_copy(g, i, own_class(c)).start()

    relayed_start(0)
    logit_acc[...] = jnp.zeros_like(logit_acc)

    def add_logits(b):
        cols = pl.ds(pl.multiple_of(b * kb, kb), kb)
        logit_acc[:, :experts] += dot(mod[:, cols], router[:, cols], NT)

    loop(0, nb, add_logits)
    scores = jax.nn.sigmoid(logit_acc[...])
    picked = [jnp.sum(jnp.where(h, scores, 0.0), axis=1, keepdims=True) for h in hits]
    score_sum = picked[0] + picked[1]
    shares = [p / score_sum for p in picked]
    share_r = [s.astype(BF16).astype(F32) for s in shares]
    share_row = jnp.sum(places[0] * share_r[0] + places[1] * share_r[1], axis=0, keepdims=True)
    if nt * 128 > slots * CAP:
        share_row = jnp.concatenate(
            [share_row, jnp.zeros((1, nt * 128 - slots * CAP), F32)], axis=1
        )
    sh_own[...] = jnp.zeros_like(sh_own)
    for i in range(nt):
        sh_own[i : i + 1, :] = share_row[:, 128 * i : 128 * (i + 1)]
    loop(1, slots, lambda k: sh_copy(k).start())
    loop(1, RELAYED, relayed_start)
    loop(RELAYED, n, lambda g: loop(0, nb, lambda b: fill(g, b)))
    for g in range(RELAYED):
        relayed_arrive(g)
        if g == 0:
            loop(RELAYED * n, (RELAYED + 1) * n, lambda k: direct_copy(k).start())
    loop(1, slots, lambda k: sh_copy(k).wait_recv())
    shares_in = merge(sh_own[...], sh_recv)
    shares_in = jnp.concatenate([shares_in, jnp.zeros((120, 128), F32)], axis=0).T
    for i in range(nt):
        sh_col[128 * i : 128 * (i + 1), :] = jnp.broadcast_to(shares_in[:, i : i + 1], (128, 128))
    for i in range(3):
        w_copy_local(i).wait()
        w_copy(i).wait()

    def wait_group(g):
        @pl.when(g < RELAYED)
        def _():
            for i in range(5):
                relay_copy(g, i, plane(-turn * ROLE[i])).wait_recv()

        @pl.when(g >= RELAYED)
        def _():
            loop(0, n, lambda i: direct_copy(g * n + i).wait_recv())

        @pl.when(g == RELAYED - 1)
        def _():
            loop((RELAYED + 1) * n, slots, lambda k: direct_copy(k).start())

    def near_sums(g):
        for i in range(5):
            near_copy(g, i).wait_recv()
        packed = []
        for c in range(3):
            total = t_own[g, c]
            for i in range(5):
                if CLASS[i] == c:
                    total = total + t_in[g, i].astype(F32)
            packed.append(total)
        for i in range(n):
            slot = g * n + i
            at = slice(i * CAP, (i + 1) * CAP)
            folded = [
                jnp.concatenate([t[at, :half], t[at, half:]], axis=0).astype(BF16) for t in packed
            ]

            @pl.when(slot > 0)
            def _():
                for c in range(3):
                    b_send[slot, c] = folded[c]
                b_copy(slot).start()

            if i == 0:

                @pl.when(slot == 0)
                def _():
                    for c in range(3):
                        b_recv[0, c] = folded[c]

    def combine(g):
        loop(
            0,
            n,
            lambda i: pl.when(g * n + i > 0)(lambda: b_copy(g * n + i).wait_recv()),
        )
        rows = pl.ds(pl.multiple_of(g * group, group), group)
        for c in range(3):
            tiles = [b_recv[g * n + i, c].astype(F32) for i in range(n)]
            low = jnp.concatenate([t[:CAP] for t in tiles], axis=0)
            high = jnp.concatenate([t[CAP:] for t in tiles], axis=0)
            back = jnp.concatenate([low, high], axis=1).astype(BF16)
            e_acc[c] += dot(place_t[rows, :], back, TN)

    def compute_group(g):
        wait_group(g)
        rows = pl.ds(pl.multiple_of(g * group, group), group)
        share = sh_col[rows, :1]
        gu_acc[...] = jnp.zeros_like(gu_acc)
        r_acc[...] = jnp.zeros_like(r_acc)

        def forward(b):
            cols = pl.ds(pl.multiple_of(b * kb, kb), kb)
            tiles = [recv[g, b, i].astype(F32) for i in range(n)]
            zb = jnp.concatenate([t[:CAP] for t in tiles], axis=0).astype(BF16)
            dyf = jnp.concatenate([t[CAP:] for t in tiles], axis=0)
            rows_z[rows, cols] = zb
            rows_wdy[rows, cols] = (share * dyf).astype(BF16)
            w_gu = [w_gate[0, cols, :], w_gate[1, cols, :], w_up[0, cols, :], w_up[1, cols, :]]
            gu_acc[...] += dot(zb, jnp.concatenate(w_gu, axis=1))
            wd = jnp.concatenate([w_down[0, :, cols], w_down[1, :, cols]], axis=0)
            r_acc[...] += dot(dyf.astype(BF16), wd, NT)

        loop(0, nb, forward)
        gv, uv, rv = gu_acc[:, : 2 * hidden], gu_acc[:, 2 * hidden :], r_acc[...]
        sig = jax.nn.sigmoid(gv)
        act = gv * sig
        hv = act * uv
        prod = hv * rv
        hr[rows, :] = prod[:, :hidden] + prod[:, hidden:]
        scaled = share * rv
        du = (scaled * act).astype(BF16)
        dg = (scaled * uv * sig * (1.0 + gv * (1.0 - sig))).astype(BF16)
        d_gu[rows, :] = jnp.concatenate(
            [dg[:, :hidden], du[:, :hidden], dg[:, hidden:], du[:, hidden:]], axis=1
        )
        hid[rows, :] = hv.astype(BF16)

        def backward(r):
            wrows = pl.ds(pl.multiple_of(r * kb, kb), kb)
            w_gu = [w_gate[0, wrows, :], w_up[0, wrows, :], w_gate[1, wrows, :], w_up[1, wrows, :]]
            return dot(d_gu[rows, :], jnp.concatenate(w_gu, axis=1), NT)

        for i in range(5):
            t_send[g, i] = backward(plane(-turn * ROLE[i])).astype(BF16)
            near_copy(g, i).start()
        for c in range(3):
            t_own[g, c] = backward(own_class(c))

    def group_step(g):
        compute_group(g)

        @pl.when(g > 0)
        def _():
            near_sums(g - 1)

    loop(0, n, group_step)

    term_own[...] = jnp.zeros_like(term_own)
    for i in range(nt):
        tile = hr[128 * i : 128 * (i + 1), :]
        term_own[i : i + 1, :] = jnp.sum(tile.T, axis=0, keepdims=True)
    loop(1, zn, lambda j: tz_copy(j).start())

    def weight_grads(b):
        cols = pl.ds(pl.multiple_of(b * kb, kb), kb)
        gu = dot(rows_z[:, cols], d_gu[...], TN)
        gu_own[b] = gu[:, : 2 * hidden]
        gu_send[b] = gu[:, 2 * hidden :].astype(BF16)
        gu_copy(b).start()
        dn = dot(hid[...], rows_wdy[:, cols], TN)
        dn_own[b] = dn[:hidden]
        dn_send[b] = dn[hidden:].astype(BF16)
        dn_copy(b).start()

    loop(0, nb // 2, weight_grads)
    loop(1, zn, lambda j: tz_copy(j).wait_recv())
    total = term_own[...]
    for j in range(1, zn):
        total = total + term_z[j]
    term_sum[...] = total
    loop(1, slots, lambda k: tb_copy(k).start())
    near_sums(n - 1)
    loop(nb // 2, nb, weight_grads)
    e_acc[...] = jnp.zeros_like(e_acc)
    loop(0, n - 1, combine)
    loop(1, slots, lambda k: tb_copy(k).wait_recv())
    terms = merge(term_sum[...], term_b)
    term_row = jnp.concatenate([terms[i : i + 1] for i in range(nt)], axis=1)[:, : slots * CAP]
    choice = [jnp.sum(p * term_row, axis=1, keepdims=True) for p in places]
    mean_grad = shares[0] * choice[0] + shares[1] * choice[1]
    logit_grad = jnp.zeros((toks, 128), F32)
    for k in range(2):
        pick = (choice[k] - mean_grad) / score_sum * picked[k] * (1.0 - picked[k])
        logit_grad = logit_grad + jnp.where(hits[k], pick, 0.0)
    my_cols = pl.ds(pl.multiple_of(z * cols_z, cols_z), cols_z)
    lg_rows = logit_grad.T[:16]
    parts = [p.astype(F32) for p in split3(lg_rows)]
    prod = dot(jnp.concatenate(parts, axis=0).astype(BF16), mod[:, my_cols])
    rc_own[...] = prod[:16] + prod[16:32] + prod[32:]
    rc_copy().start()
    lg_parts = split3(logit_grad)
    mod_grad = sum(dot(p[:, :experts], router[:, my_cols]) for p in lg_parts)
    combine(n - 1)
    for c in (1, 2):
        m_send[c - 1] = e_acc[c].astype(BF16)
        far_copy(c).start()

    def gain_normed(r):
        cols = pl.ds(pl.multiple_of(r * kb, kb), kb)
        return 1.0 + scale[:, cols], (tokens[:, cols].astype(F32) - mean) * inv_std

    gain, normed = gain_normed(z)
    sums = [jnp.zeros((toks, 1), F32)] * 2
    for c in range(3):
        gain_c, normed_c = gain_normed(own_class(c))
        part = e_acc[c] if c > 0 else e_acc[0] + mod_grad
        part = part * gain_c
        sums[0] = sums[0] + jnp.sum(part, axis=1, keepdims=True)
        sums[1] = sums[1] + jnp.sum(part * normed_c, axis=1, keepdims=True)
    lane = lax.broadcasted_iota(jnp.int32, (toks, 128), 1)
    sums_t = jnp.where(lane == 0, sums[0], jnp.where(lane == 1, sums[1], 0.0)).T
    ns_own[...] = sums_t[:8]
    loop(1, zn, lambda j: ns_copy(j).start())

    def finish(b):
        gu_copy(b).wait_recv()
        dn_copy(b).wait_recv()
        cols = pl.ds(pl.multiple_of(b * kb, kb), kb)
        gu = gu_own[b] + gu_recv[b].astype(F32)
        gate_out[0, cols, :] = gu[:, :hidden].astype(BF16)
        up_out[0, cols, :] = gu[:, hidden:].astype(BF16)
        down_out[0, :, cols] = (dn_own[b] + dn_recv[b].astype(F32)).astype(BF16)

    rc_copy().wait_recv()
    rx_sum[...] = rc_own[...] + rc_sib[...]
    rx_buf[cx] = rx_sum[...]
    loop(1, n, lambda j: rx_copy(j, cx).start())
    loop(0, nb // 2, finish)
    loop(1, n, lambda j: rx_copy(j, lax.rem(cx + j, n)).wait_recv())
    total = rx_buf[0]
    for j in range(1, n):
        total = total + rx_buf[j]
    ry_sum[...] = total
    ry_buf[cy] = total
    loop(1, n, lambda j: ry_copy(j, cy).start())
    loop(nb // 2, nb, finish)

    for c in (1, 2):
        far_copy(c).wait_recv()
    expert_grad = e_acc[0] + m_in[0].astype(F32) + m_in[1].astype(F32)
    norm_grad = (mod_grad + expert_grad) * gain
    loop(1, n, lambda j: ry_copy(j, lax.rem(cy + j, n)).wait_recv())
    total = ry_buf[0]
    for j in range(1, n):
        total = total + ry_buf[j]
    router_out[...] = total

    loop(1, zn, lambda j: ns_copy(j).wait_recv())
    total = ns_own[...]
    for j in range(1, zn):
        total = total + ns_z[j]
    total = jnp.concatenate([total, jnp.zeros((120, toks), F32)], axis=0).T * (1.0 / width)
    input_out[...] = inv_std * (norm_grad - total[:, 0:1] - normed * total[:, 1:2])

    def drain_slot(k):
        sh_copy(k).wait_send()
        b_copy(k).wait_send()
        tb_copy(k).wait_send()

        @pl.when(k < RELAYED * n)
        def _():
            for c in range(3):
                part_copy(k, c).wait_send()

        @pl.when(k >= RELAYED * n)
        def _():
            direct_copy(k).wait_send()

    loop(1, slots, drain_slot)

    def drain_group(g):
        for i in range(5):
            near_copy(g, i).wait_send()

        @pl.when(g < RELAYED)
        def _():
            for i in range(5):
                relay_copy(g, i, own_class(CLASS[i])).wait_send()

    loop(0, n, drain_group)
    for c in (1, 2):
        far_copy(c).wait_send()

    def drain_ring(j):
        rx_copy(j, cx).wait_send()
        ry_copy(j, cy).wait_send()

    rc_copy().wait_send()
    loop(1, n, drain_ring)

    def drain_z(j):
        tz_copy(j).wait_send()
        ns_copy(j).wait_send()

    loop(1, zn, drain_z)

    def drain_b(b):
        gu_copy(b).wait_send()
        dn_copy(b).wait_send()

    loop(0, nb, drain_b)


def copy_kernel(count, *refs):
    sems = refs[-1]
    held = refs[2 * count : 3 * count]
    arrive = [pltpu.make_async_copy(refs[i], held[i], sems.at[0, i]) for i in range(count)]
    leave = [
        pltpu.make_async_copy(held[i], refs[count + i], sems.at[1, i]) for i in range(count)
    ]
    for copy in arrive:
        copy.start()
    for i in range(count):
        arrive[i].wait()
        leave[i].start()
    for copy in leave:
        copy.wait()


def place_results(arrays):
    count = len(arrays)
    any_spec = pl.BlockSpec(memory_space=pl.ANY)
    return pl.pallas_call(
        functools.partial(copy_kernel, count),
        out_shape=tuple(jax.ShapeDtypeStruct(a.shape, a.dtype) for a in arrays),
        in_specs=[any_spec] * count,
        out_specs=(any_spec,) * count,
        scratch_shapes=[pltpu.VMEM(a.shape, a.dtype) for a in arrays]
        + [pltpu.SemaphoreType.DMA((2, count))],
        compiler_params=pltpu.CompilerParams(vmem_limit_bytes=60 * 1024 * 1024),
    )(*arrays)


def shards(
    tokens,
    cotangent,
    expert_ids,
    ada_shift,
    ada_scale,
    ada_gate,
    router_weight,
    gate_blocks,
    up_blocks,
    down_blocks,
):
    zn = lax.axis_size("exp")
    n = math.isqrt(lax.axis_size("seq") // 2)
    slots = n * n
    toks, width = tokens.shape
    experts = router_weight.shape[1]
    hidden = gate_blocks.shape[2]
    rows = slots * CAP
    cols_z = kb = width // zn
    nb = zn
    nt = -(-rows // 128)
    group = n * CAP
    dma = pltpu.SemaphoreType.DMA
    vm = pltpu.VMEM
    scratch = [
        vm((toks, width), BF16),
        vm((toks, width), BF16),
        vm((rows, toks), BF16),
        vm((slots, nb, 2 * CAP, kb), BF16),
        vm((n, nb, n, 2 * CAP, kb), BF16),
        vm((2, width, hidden), BF16),
        vm((2, width, hidden), BF16),
        vm((2, hidden, width), BF16),
        vm((rows, width), BF16),
        vm((rows, width), BF16),
        vm((rows, 4 * hidden), BF16),
        vm((rows, 2 * hidden), BF16),
        vm((nt * 128, hidden), F32),
        vm((group, 4 * hidden), F32),
        vm((group, 2 * hidden), F32),
        vm((n, 5, group, kb), BF16),
        vm((n, 5, group, kb), BF16),
        vm((n, 3, group, kb), F32),
        vm((2, toks, kb), BF16),
        vm((2, toks, kb), BF16),
        vm((slots, 3, 2 * CAP, kb // 2), BF16),
        vm((slots, 3, 2 * CAP, kb // 2), BF16),
        vm((3, toks, kb), F32),
        vm((8, 128), F32),
        vm((zn, 8, 128), F32),
        vm((8, 128), F32),
        vm((slots, 8, 128), F32),
        vm((8, 128), F32),
        vm((slots, 8, 128), F32),
        vm((nt * 128, 128), F32),
        vm((nb, kb, 2 * hidden), F32),
        vm((nb, kb, 2 * hidden), BF16),
        vm((nb, kb, 2 * hidden), BF16),
        vm((nb, hidden, kb), F32),
        vm((nb, hidden, kb), BF16),
        vm((nb, hidden, kb), BF16),
        vm((toks, 128), F32),
        vm((toks, 128), F32),
        vm((16, cols_z), F32),
        vm((16, cols_z), F32),
        vm((16, cols_z), F32),
        vm((n, 16, cols_z), F32),
        vm((16, cols_z), F32),
        vm((n, 16, cols_z), F32),
        vm((8, toks), F32),
        vm((zn, 8, toks), F32),
    ]
    sems = [3, 3, 3, (slots, 3), (slots, 3), (n, 5), (n, 5), (n, 5), (n, 5)]
    sems += [2, 2, slots, slots, slots, slots]
    sems += [zn, zn, slots, slots, nb, nb, nb, nb]
    sems += [1, 1, n, n, n, n, zn, zn]
    scratch += [dma(s if isinstance(s, tuple) else (s,)) for s in sems]
    any_spec = pl.BlockSpec(memory_space=pl.ANY)
    vm_spec = pl.BlockSpec(memory_space=pltpu.VMEM)
    row = lambda v: v.reshape(1, width)
    results = pl.pallas_call(
        functools.partial(expert_kernel, n, zn),
        out_shape=(
            jax.ShapeDtypeStruct((toks, cols_z), F32),
            jax.ShapeDtypeStruct((16, cols_z), F32),
            jax.ShapeDtypeStruct((1, width, hidden), BF16),
            jax.ShapeDtypeStruct((1, width, hidden), BF16),
            jax.ShapeDtypeStruct((1, hidden, width), BF16),
        ),
        in_specs=[vm_spec] * 7 + [any_spec] * 3,
        out_specs=(vm_spec,) * 5,
        scratch_shapes=scratch,
        compiler_params=pltpu.CompilerParams(
            collective_id=0, has_side_effects=True, vmem_limit_bytes=60 * 1024 * 1024
        ),
        cost_estimate=pl.CostEstimate(
            flops=16 * rows * width * 2 * hidden, bytes_accessed=16 * 1024 * 1024, transcendentals=0
        ),
    )(
        tokens,
        cotangent,
        expert_ids.T,
        row(ada_shift),
        row(ada_scale),
        row(ada_gate),
        router_weight.T,
        gate_blocks,
        up_blocks,
        down_blocks,
    )
    grad_input, router_t, grad_gate, grad_up, grad_down = place_results(results)
    return (grad_input, router_t[:experts].T, grad_gate, grad_up, grad_down)


def solution(mesh):
    in_specs = (
        P("seq", None),
        P("seq", None),
        P("seq", None),
        P(),
        P(),
        P(),
        P(),
        P(("seq", "exp"), None, None),
        P(("seq", "exp"), None, None),
        P(("seq", "exp"), None, None),
    )
    out_specs = (
        P("seq", "exp"),
        P("exp", None),
        P(("seq", "exp"), None, None),
        P(("seq", "exp"), None, None),
        P(("seq", "exp"), None, None),
    )
    return jax.shard_map(shards, mesh=mesh, in_specs=in_specs, out_specs=out_specs, check_vma=False)
```

```python
import functools
import math

import jax
import jax.numpy as jnp
from jax import lax
from jax.experimental import pallas as pl
from jax.experimental.pallas import tpu as pltpu
from jax.sharding import PartitionSpec as P

CAP = 24
RELAYED = 3
ROLE = (1, 7, 4, 2, 5)
CLASS = (0, 0, 1, 1, 2)
SIGN = (1, -1, 1, -1, -1)
EPSILON = 1e-06
MESH = pl.DeviceIdType.MESH
F32 = jnp.float32
BF16 = jnp.bfloat16
NT = (((1,), (1,)), ((), ()))
TN = (((0,), (0,)), ((), ()))


def dot(a, b, dims=(((1,), (0,)), ((), ()))):
    return lax.dot_general(a, b, dims, preferred_element_type=F32)


def split_refs(refs, counts):
    parts, at = [], 0
    for count in counts:
        parts.append(refs[at : at + count])
        at += count
    return parts


def split3(x):
    hi = x.astype(BF16)
    rest = x - hi.astype(F32)
    mid = rest.astype(BF16)
    return hi, mid, (rest - mid.astype(F32)).astype(BF16)


def expert_kernel(n, zn, *refs):
    (
        (tokens, cotangent, ids, shift, scale, ada_gate, router, gate, up, down),
        (input_out, router_out, gate_out, up_out, down_out),
        (mod, og, place_t, send, recv, w_gate, w_up, w_down, rows_z, rows_wdy, d_gu, hid, hr),
        (gu_acc, r_acc, t_send, t_in, t_own, m_send, m_in, b_send, b_recv, e_acc),
        (term_own, term_z, term_sum, term_b, sh_own, sh_recv, sh_col),
        (gu_own, gu_send, gu_recv, dn_own, dn_send, dn_recv),
        (logit_acc, stat, rc_own, rc_sib, rx_sum, rx_buf, ry_sum, ry_buf, ns_own, ns_z),
        (w_local, w_ssem, w_rsem, d_ssem, d_rsem, f_ssem, f_rsem, a_ssem, a_rsem),
        (m_ssem, m_rsem, b_ssem, b_rsem, sh_ssem, sh_rsem),
        (tz_ssem, tz_rsem, tb_ssem, tb_rsem, g_ssem, g_rsem, h_ssem, h_rsem),
        (rc_ssem, rc_rsem, rx_ssem, rx_rsem, ry_ssem, ry_rsem, ns_ssem, ns_rsem),
    ) = split_refs(refs, (10, 5, 13, 10, 7, 6, 10, 9, 6, 8, 8))
    slots = n * n
    width = rows_z.shape[1]
    group = n * CAP
    hidden = w_gate.shape[2]
    kb = cols_z = width // zn
    nb = zn
    half = cols_z // 2
    toks = tokens.shape[0]
    seq = lax.axis_index("seq")
    z = lax.axis_index("exp")
    core = lax.rem(seq, 2)
    chip = seq // 2
    cy, cx = chip // n, lax.rem(chip, n)

    def offset(slot):
        dy = lax.rem(slot, n)
        dx = lax.rem(dy + slot // n, n)
        return dy, dx

    def target(slot):
        dy, dx = offset(slot)
        return (2 * (lax.rem(cy + dy, n) * n + lax.rem(cx + dx, n)) + core, z)

    def source(slot):
        dy, dx = offset(slot)
        return (2 * (lax.rem(cy - dy + n, n) * n + lax.rem(cx - dx + n, n)) + core, z)

    def z_peer(step):
        return (seq, lax.rem(z + step, zn))

    sibling = (seq + 1 - 2 * core, z)

    def remote(src, dst, ssem, rsem, dev):
        return pltpu.make_async_remote_copy(
            src_ref=src, dst_ref=dst, send_sem=ssem, recv_sem=rsem, device_id=dev, device_id_type=MESH
        )

    def plane(step):
        return lax.rem(z + step + 2 * zn, zn)

    turn = 1 - 2 * core

    def own_class(c):
        return plane(-3 * turn * c)

    def direct_copy(slot):
        dst = recv.at[slot // n, :, lax.rem(slot, n)]
        return remote(send.at[slot], dst, d_ssem.at[slot, 0], d_rsem.at[slot, 0], target(slot))

    def part_copy(slot, c):
        g = slot // n
        r = own_class(c)
        dst = recv.at[g, r, lax.rem(slot, n)]
        return remote(send.at[slot, r], dst, d_ssem.at[slot, c], d_rsem.at[slot, c], target(slot))

    def relay_copy(g, i, r):
        to = (seq, plane(turn * SIGN[i]))
        return remote(recv.at[g, r], recv.at[g, r], f_ssem.at[g, i], f_rsem.at[g, i], to)

    def near_copy(g, i):
        to = (seq, plane(-turn * SIGN[i]))
        return remote(t_send.at[g, i], t_in.at[g, i], a_ssem.at[g, i], a_rsem.at[g, i], to)

    def far_copy(c):
        to = (seq, own_class(c))
        return remote(m_send.at[c - 1], m_in.at[c - 1], m_ssem.at[c - 1], m_rsem.at[c - 1], to)

    def sh_copy(slot):
        return remote(sh_own, sh_recv.at[slot], sh_ssem.at[slot], sh_rsem.at[slot], target(slot))

    def b_copy(slot, c):
        src, dst = b_send.at[slot, c], b_recv.at[slot, c]
        return remote(src, dst, b_ssem.at[slot, c], b_rsem.at[slot, c], source(slot))

    def tz_copy(step):
        return remote(term_own, term_z.at[step], tz_ssem.at[step], tz_rsem.at[step], z_peer(step))

    def tb_copy(slot):
        return remote(term_sum, term_b.at[slot], tb_ssem.at[slot], tb_rsem.at[slot], source(slot))

    def rc_copy():
        return remote(rc_own, rc_sib, rc_ssem.at[0], rc_rsem.at[0], sibling)

    def rx_copy(step, at):
        to = (2 * (cy * n + lax.rem(cx + step, n)) + core, z)
        return remote(rx_sum, rx_buf.at[at], rx_ssem.at[step], rx_rsem.at[at], to)

    def ry_copy(step, at):
        to = (2 * (lax.rem(cy + step, n) * n + cx) + core, z)
        return remote(ry_sum, ry_buf.at[at], ry_ssem.at[step], ry_rsem.at[at], to)

    def ns_copy(step):
        return remote(ns_own, ns_z.at[step], ns_ssem.at[step], ns_rsem.at[step], z_peer(step))

    def gu_copy(b):
        return remote(gu_send.at[b], gu_recv.at[b], g_ssem.at[b], g_rsem.at[b], sibling)

    def dn_copy(b):
        return remote(dn_send.at[b], dn_recv.at[b], h_ssem.at[b], h_rsem.at[b], sibling)

    weights = ((gate, w_gate), (up, w_up), (down, w_down))

    def w_copy(i):
        hbm, vmem = weights[i]
        return remote(hbm.at[0], vmem.at[1], w_ssem.at[i], w_rsem.at[i], sibling)

    def w_copy_local(i):
        hbm, vmem = weights[i]
        return pltpu.make_async_copy(hbm.at[0], vmem.at[0], w_local.at[i])

    def loop(lo, hi, body):
        def step(i, carry):
            body(i)
            return carry

        lax.fori_loop(lo, hi, step, 0)

    barrier = pltpu.get_barrier_semaphore()
    loop(
        1,
        slots,
        lambda k: pl.semaphore_signal(barrier, inc=1, device_id=target(k), device_id_type=MESH),
    )
    loop(
        1,
        zn,
        lambda j: pl.semaphore_signal(barrier, inc=1, device_id=z_peer(j), device_id_type=MESH),
    )
    pl.semaphore_signal(barrier, inc=1, device_id=sibling, device_id_type=MESH)
    for i in range(3):
        w_copy_local(i).start()

    experts = router.shape[0]
    expert_at = lax.broadcasted_iota(jnp.int32, (toks, 128), 1)
    ids_t = jnp.concatenate([ids[...].astype(F32), jnp.zeros((126, toks), F32)], axis=0).T
    hits = [expert_at.astype(F32) == ids_t[:, k : k + 1] for k in range(2)]
    routed = jnp.where(hits[0] | hits[1], 1.0, 0.0)
    tok_at = lax.broadcasted_iota(jnp.int32, (toks, toks), 0)
    earlier = jnp.where(tok_at > lax.broadcasted_iota(jnp.int32, (toks, toks), 1), 1.0, 0.0)
    rank = dot(earlier.astype(BF16), routed.astype(BF16))
    bits = n.bit_length() - 1
    e_dy = ((expert_at >> bits) - cy) & (n - 1)
    e_dx = ((expert_at & (n - 1)) - cx) & (n - 1)
    base = ((((e_dx - e_dy) & (n - 1)) * n + e_dy) * CAP).astype(F32) + rank
    slot_at = lax.broadcasted_iota(jnp.int32, (toks, slots * CAP), 1).astype(F32)
    places = [
        jnp.where(slot_at == jnp.sum(jnp.where(h, base, 0.0), axis=1, keepdims=True), 1.0, 0.0)
        for h in hits
    ]
    place_t[...] = (places[0] + places[1]).T.astype(BF16)
    nt = hr.shape[0] // 128
    flat = lax.broadcasted_iota(jnp.int32, (8, 128), 0) * 128 + lax.broadcasted_iota(
        jnp.int32, (8, 128), 1
    )

    def merge(own, others):
        out = jnp.where(flat < CAP, own, 0.0)
        for k in range(1, slots):
            out = jnp.where((flat >= k * CAP) & (flat < (k + 1) * CAP), others[k], out)
        return out

    def modulate(i):
        rows = pl.ds(pl.multiple_of(i * 16, 16), 16)
        x = tokens[rows, :].astype(F32)
        center = jnp.sum(x, axis=1, keepdims=True) * (1.0 / width)
        x = x - center
        inv = lax.rsqrt(jnp.sum(x * x, axis=1, keepdims=True) * (1.0 / width) + EPSILON)
        mod[rows, :] = (x * inv * (1.0 + scale[...]) + shift[...]).astype(BF16)
        og[rows, :] = (ada_gate[...] * cotangent[rows, :].astype(F32)).astype(BF16)
        stat[rows, :] = jnp.where(lax.broadcasted_iota(jnp.int32, (16, 128), 1) == 0, center, inv)

    loop(0, toks // 16, modulate)
    mean, inv_std = stat[:, 0:1], stat[:, 1:2]
    hr[...] = jnp.zeros_like(hr)
    pl.semaphore_wait(barrier, slots + zn - 1)
    for i in range(3):
        w_copy(i).start()

    def fill(g, b):
        rows = pl.ds(pl.multiple_of(g * group, group), group)
        cols = pl.ds(pl.multiple_of(b * kb, kb), kb)
        zc = dot(place_t[rows, :], mod[:, cols])
        dc = dot(place_t[rows, :], og[:, cols])
        for i in range(n):
            at = slice(i * CAP, (i + 1) * CAP)
            pair = jnp.concatenate([zc[at], dc[at]], axis=0).astype(BF16)

            @pl.when(g * n + i > 0)
            def _():
                send[g * n + i, b] = pair

            if i == 0:

                @pl.when(g == 0)
                def _():
                    recv[0, b, 0] = pair

    def each_remote(g, body):
        def one(i):
            @pl.when(g * n + i > 0)
            def _():
                body(g * n + i)

        loop(0, n, one)

    def relayed_start(g):
        for c in range(3):
            fill(g, own_class(c))
            each_remote(g, lambda slot: part_copy(slot, c).start())

    def relayed_arrive(g):
        for c in range(3):
            each_remote(g, lambda slot: part_copy(slot, c).wait_recv())
            for i in range(5):
                if CLASS[i] == c:
                    relay_copy(g, i, own_class(c)).start()

    relayed_start(0)
    logit_acc[...] = jnp.zeros_like(logit_acc)

    def add_logits(b):
        cols = pl.ds(pl.multiple_of(b * kb, kb), kb)
        logit_acc[:, :experts] += dot(mod[:, cols], router[:, cols], NT)

    loop(0, nb, add_logits)
    scores = jax.nn.sigmoid(logit_acc[...])
    picked = [jnp.sum(jnp.where(h, scores, 0.0), axis=1, keepdims=True) for h in hits]
    score_sum = picked[0] + picked[1]
    shares = [p / score_sum for p in picked]
    share_r = [s.astype(BF16).astype(F32) for s in shares]
    share_row = jnp.sum(places[0] * share_r[0] + places[1] * share_r[1], axis=0, keepdims=True)
    if nt * 128 > slots * CAP:
        share_row = jnp.concatenate(
            [share_row, jnp.zeros((1, nt * 128 - slots * CAP), F32)], axis=1
        )
    sh_own[...] = jnp.zeros_like(sh_own)
    for i in range(nt):
        sh_own[i : i + 1, :] = share_row[:, 128 * i : 128 * (i + 1)]
    loop(1, slots, lambda k: sh_copy(k).start())
    loop(1, RELAYED, relayed_start)
    loop(RELAYED, n, lambda g: loop(0, nb, lambda b: fill(g, b)))
    for g in range(RELAYED):
        relayed_arrive(g)
        if g == 0:
            loop(RELAYED * n, (RELAYED + 1) * n, lambda k: direct_copy(k).start())
    loop(1, slots, lambda k: sh_copy(k).wait_recv())
    shares_in = merge(sh_own[...], sh_recv)
    shares_in = jnp.concatenate([shares_in, jnp.zeros((120, 128), F32)], axis=0).T
    for i in range(nt):
        sh_col[128 * i : 128 * (i + 1), :] = jnp.broadcast_to(shares_in[:, i : i + 1], (128, 128))
    for i in range(3):
        w_copy_local(i).wait()
        w_copy(i).wait()

    def wait_group(g):
        @pl.when(g < RELAYED)
        def _():
            for i in range(5):
                relay_copy(g, i, plane(-turn * ROLE[i])).wait_recv()

        @pl.when(g >= RELAYED)
        def _():
            loop(0, n, lambda i: direct_copy(g * n + i).wait_recv())

        @pl.when(g == RELAYED - 1)
        def _():
            loop((RELAYED + 1) * n, slots, lambda k: direct_copy(k).start())

    def near_sums(g):
        for c in (1, 2, 0):
            total = t_own[g, c]
            for i in range(5):
                if CLASS[i] == c:
                    near_copy(g, i).wait_recv()
                    total = total + t_in[g, i].astype(F32)
            for i in range(n):
                slot = g * n + i
                at = slice(i * CAP, (i + 1) * CAP)
                folded = jnp.concatenate([total[at, :half], total[at, half:]], axis=0)
                folded = folded.astype(BF16)

                @pl.when(slot > 0)
                def _():
                    b_send[slot, c] = folded
                    b_copy(slot, c).start()

                if i == 0:

                    @pl.when(slot == 0)
                    def _():
                        b_recv[0, c] = folded

    def combine(g, c):
        loop(
            0,
            n,
            lambda i: pl.when(g * n + i > 0)(lambda: b_copy(g * n + i, c).wait_recv()),
        )
        rows = pl.ds(pl.multiple_of(g * group, group), group)
        tiles = [b_recv[g * n + i, c].astype(F32) for i in range(n)]
        low = jnp.concatenate([t[:CAP] for t in tiles], axis=0)
        high = jnp.concatenate([t[CAP:] for t in tiles], axis=0)
        back = jnp.concatenate([low, high], axis=1).astype(BF16)
        e_acc[c] += dot(place_t[rows, :], back, TN)

    def send_terms():
        term_own[...] = jnp.zeros_like(term_own)
        for i in range(nt):
            tile = hr[128 * i : 128 * (i + 1), :]
            term_own[i : i + 1, :] = jnp.sum(tile.T, axis=0, keepdims=True)
        loop(1, zn, lambda j: tz_copy(j).start())

    def compute_group(g):
        wait_group(g)
        rows = pl.ds(pl.multiple_of(g * group, group), group)
        share = sh_col[rows, :1]
        gu_acc[...] = jnp.zeros_like(gu_acc)
        r_acc[...] = jnp.zeros_like(r_acc)

        def forward(b):
            cols = pl.ds(pl.multiple_of(b * kb, kb), kb)
            tiles = [recv[g, b, i].astype(F32) for i in range(n)]
            zb = jnp.concatenate([t[:CAP] for t in tiles], axis=0).astype(BF16)
            dyf = jnp.concatenate([t[CAP:] for t in tiles], axis=0)
            rows_z[rows, cols] = zb
            rows_wdy[rows, cols] = (share * dyf).astype(BF16)
            w_gu = [w_gate[0, cols, :], w_gate[1, cols, :], w_up[0, cols, :], w_up[1, cols, :]]
            gu_acc[...] += dot(zb, jnp.concatenate(w_gu, axis=1))
            wd = jnp.concatenate([w_down[0, :, cols], w_down[1, :, cols]], axis=0)
            r_acc[...] += dot(dyf.astype(BF16), wd, NT)

        loop(0, nb, forward)
        gv, uv, rv = gu_acc[:, : 2 * hidden], gu_acc[:, 2 * hidden :], r_acc[...]
        sig = jax.nn.sigmoid(gv)
        act = gv * sig
        hv = act * uv
        prod = hv * rv
        hr[rows, :] = prod[:, :hidden] + prod[:, hidden:]
        scaled = share * rv
        du = (scaled * act).astype(BF16)
        dg = (scaled * uv * sig * (1.0 + gv * (1.0 - sig))).astype(BF16)
        d_gu[rows, :] = jnp.concatenate(
            [dg[:, :hidden], du[:, :hidden], dg[:, hidden:], du[:, hidden:]], axis=1
        )
        hid[rows, :] = hv.astype(BF16)

        @pl.when(g == n - 1)
        def _():
            send_terms()

        def backward(r):
            wrows = pl.ds(pl.multiple_of(r * kb, kb), kb)
            w_gu = [w_gate[0, wrows, :], w_up[0, wrows, :], w_gate[1, wrows, :], w_up[1, wrows, :]]
            return dot(d_gu[rows, :], jnp.concatenate(w_gu, axis=1), NT)

        for i in (2, 3, 4, 0, 1):
            t_send[g, i] = backward(plane(-turn * ROLE[i])).astype(BF16)
            near_copy(g, i).start()
        for c in (1, 2, 0):
            t_own[g, c] = backward(own_class(c))

    def group_step(g):
        compute_group(g)

        @pl.when(g > 0)
        def _():
            near_sums(g - 1)

    loop(0, n, group_step)

    def weight_grads(b):
        cols = pl.ds(pl.multiple_of(b * kb, kb), kb)
        gu = dot(rows_z[:, cols], d_gu[...], TN)
        gu_own[b] = gu[:, : 2 * hidden]
        gu_send[b] = gu[:, 2 * hidden :].astype(BF16)
        gu_copy(b).start()
        dn = dot(hid[...], rows_wdy[:, cols], TN)
        dn_own[b] = dn[:hidden]
        dn_send[b] = dn[hidden:].astype(BF16)
        dn_copy(b).start()

    first, last = nb // 4, nb * 5 // 8
    loop(0, first, weight_grads)
    near_sums(n - 1)
    loop(1, zn, lambda j: tz_copy(j).wait_recv())
    total = term_own[...]
    for j in range(1, zn):
        total = total + term_z[j]
    term_sum[...] = total
    loop(1, slots, lambda k: tb_copy(k).start())
    e_acc[...] = jnp.zeros_like(e_acc)

    def combine_all(g):
        for c in range(3):
            combine(g, c)

    loop(0, n - 1, combine_all)
    loop(first, last, weight_grads)
    for c in (1, 2):
        combine(n - 1, c)
        m_send[c - 1] = e_acc[c].astype(BF16)
        far_copy(c).start()
    combine(n - 1, 0)
    loop(1, slots, lambda k: tb_copy(k).wait_recv())
    terms = merge(term_sum[...], term_b)
    term_row = jnp.concatenate([terms[i : i + 1] for i in range(nt)], axis=1)[:, : slots * CAP]
    choice = [jnp.sum(p * term_row, axis=1, keepdims=True) for p in places]
    mean_grad = shares[0] * choice[0] + shares[1] * choice[1]
    logit_grad = jnp.zeros((toks, 128), F32)
    for k in range(2):
        pick = (choice[k] - mean_grad) / score_sum * picked[k] * (1.0 - picked[k])
        logit_grad = logit_grad + jnp.where(hits[k], pick, 0.0)
    my_cols = pl.ds(pl.multiple_of(z * cols_z, cols_z), cols_z)
    lg_rows = logit_grad.T[:16]
    parts = [p.astype(F32) for p in split3(lg_rows)]
    prod = dot(jnp.concatenate(parts, axis=0).astype(BF16), mod[:, my_cols])
    rc_own[...] = prod[:16] + prod[16:32] + prod[32:]
    rc_copy().start()
    lg_parts = split3(logit_grad)
    mod_grad = sum(dot(p[:, :experts], router[:, my_cols]) for p in lg_parts)
    def gain_normed(r):
        cols = pl.ds(pl.multiple_of(r * kb, kb), kb)
        return 1.0 + scale[:, cols], (tokens[:, cols].astype(F32) - mean) * inv_std

    gain, normed = gain_normed(z)
    sums = [jnp.zeros((toks, 1), F32)] * 2
    for c in range(3):
        gain_c, normed_c = gain_normed(own_class(c))
        part = e_acc[c] if c > 0 else e_acc[0] + mod_grad
        part = part * gain_c
        sums[0] = sums[0] + jnp.sum(part, axis=1, keepdims=True)
        sums[1] = sums[1] + jnp.sum(part * normed_c, axis=1, keepdims=True)
    lane = lax.broadcasted_iota(jnp.int32, (toks, 128), 1)
    sums_t = jnp.where(lane == 0, sums[0], jnp.where(lane == 1, sums[1], 0.0)).T
    ns_own[...] = sums_t[:8]
    loop(1, zn, lambda j: ns_copy(j).start())
    loop(last, nb, weight_grads)

    def finish(b):
        gu_copy(b).wait_recv()
        dn_copy(b).wait_recv()
        cols = pl.ds(pl.multiple_of(b * kb, kb), kb)
        gu = gu_own[b] + gu_recv[b].astype(F32)
        gate_out[0, cols, :] = gu[:, :hidden].astype(BF16)
        up_out[0, cols, :] = gu[:, hidden:].astype(BF16)
        down_out[0, :, cols] = (dn_own[b] + dn_recv[b].astype(F32)).astype(BF16)

    rc_copy().wait_recv()
    rx_sum[...] = rc_own[...] + rc_sib[...]
    rx_buf[cx] = rx_sum[...]
    loop(1, n, lambda j: rx_copy(j, cx).start())
    loop(0, nb // 2, finish)
    loop(1, n, lambda j: rx_copy(j, lax.rem(cx + j, n)).wait_recv())
    total = rx_buf[0]
    for j in range(1, n):
        total = total + rx_buf[j]
    ry_sum[...] = total
    ry_buf[cy] = total
    loop(1, n, lambda j: ry_copy(j, cy).start())
    loop(nb // 2, nb, finish)

    for c in (1, 2):
        far_copy(c).wait_recv()
    expert_grad = e_acc[0] + m_in[0].astype(F32) + m_in[1].astype(F32)
    norm_grad = (mod_grad + expert_grad) * gain
    loop(1, n, lambda j: ry_copy(j, lax.rem(cy + j, n)).wait_recv())
    total = ry_buf[0]
    for j in range(1, n):
        total = total + ry_buf[j]
    router_out[...] = total

    loop(1, zn, lambda j: ns_copy(j).wait_recv())
    total = ns_own[...]
    for j in range(1, zn):
        total = total + ns_z[j]
    total = jnp.concatenate([total, jnp.zeros((120, toks), F32)], axis=0).T * (1.0 / width)
    input_out[...] = inv_std * (norm_grad - total[:, 0:1] - normed * total[:, 1:2])

    def drain_slot(k):
        sh_copy(k).wait_send()
        for c in range(3):
            b_copy(k, c).wait_send()
        tb_copy(k).wait_send()

        @pl.when(k < RELAYED * n)
        def _():
            for c in range(3):
                part_copy(k, c).wait_send()

        @pl.when(k >= RELAYED * n)
        def _():
            direct_copy(k).wait_send()

    loop(1, slots, drain_slot)

    def drain_group(g):
        for i in range(5):
            near_copy(g, i).wait_send()

        @pl.when(g < RELAYED)
        def _():
            for i in range(5):
                relay_copy(g, i, own_class(CLASS[i])).wait_send()

    loop(0, n, drain_group)
    for c in (1, 2):
        far_copy(c).wait_send()

    def drain_ring(j):
        rx_copy(j, cx).wait_send()
        ry_copy(j, cy).wait_send()

    rc_copy().wait_send()
    loop(1, n, drain_ring)

    def drain_z(j):
        tz_copy(j).wait_send()
        ns_copy(j).wait_send()

    loop(1, zn, drain_z)

    def drain_b(b):
        gu_copy(b).wait_send()
        dn_copy(b).wait_send()

    loop(0, nb, drain_b)


def copy_kernel(count, *refs):
    sems = refs[-1]
    held = refs[2 * count : 3 * count]
    arrive = [pltpu.make_async_copy(refs[i], held[i], sems.at[0, i]) for i in range(count)]
    leave = [
        pltpu.make_async_copy(held[i], refs[count + i], sems.at[1, i]) for i in range(count)
    ]
    for copy in arrive:
        copy.start()
    for i in range(count):
        arrive[i].wait()
        leave[i].start()
    for copy in leave:
        copy.wait()


def place_results(arrays):
    count = len(arrays)
    any_spec = pl.BlockSpec(memory_space=pl.ANY)
    return pl.pallas_call(
        functools.partial(copy_kernel, count),
        out_shape=tuple(jax.ShapeDtypeStruct(a.shape, a.dtype) for a in arrays),
        in_specs=[any_spec] * count,
        out_specs=(any_spec,) * count,
        scratch_shapes=[pltpu.VMEM(a.shape, a.dtype) for a in arrays]
        + [pltpu.SemaphoreType.DMA((2, count))],
        compiler_params=pltpu.CompilerParams(vmem_limit_bytes=60 * 1024 * 1024),
    )(*arrays)


def shards(
    tokens,
    cotangent,
    expert_ids,
    ada_shift,
    ada_scale,
    ada_gate,
    router_weight,
    gate_blocks,
    up_blocks,
    down_blocks,
):
    zn = lax.axis_size("exp")
    n = math.isqrt(lax.axis_size("seq") // 2)
    slots = n * n
    toks, width = tokens.shape
    experts = router_weight.shape[1]
    hidden = gate_blocks.shape[2]
    rows = slots * CAP
    cols_z = kb = width // zn
    nb = zn
    nt = -(-rows // 128)
    group = n * CAP
    dma = pltpu.SemaphoreType.DMA
    vm = pltpu.VMEM
    scratch = [
        vm((toks, width), BF16),
        vm((toks, width), BF16),
        vm((rows, toks), BF16),
        vm((slots, nb, 2 * CAP, kb), BF16),
        vm((n, nb, n, 2 * CAP, kb), BF16),
        vm((2, width, hidden), BF16),
        vm((2, width, hidden), BF16),
        vm((2, hidden, width), BF16),
        vm((rows, width), BF16),
        vm((rows, width), BF16),
        vm((rows, 4 * hidden), BF16),
        vm((rows, 2 * hidden), BF16),
        vm((nt * 128, hidden), F32),
        vm((group, 4 * hidden), F32),
        vm((group, 2 * hidden), F32),
        vm((n, 5, group, kb), BF16),
        vm((n, 5, group, kb), BF16),
        vm((n, 3, group, kb), F32),
        vm((2, toks, kb), BF16),
        vm((2, toks, kb), BF16),
        vm((slots, 3, 2 * CAP, kb // 2), BF16),
        vm((slots, 3, 2 * CAP, kb // 2), BF16),
        vm((3, toks, kb), F32),
        vm((8, 128), F32),
        vm((zn, 8, 128), F32),
        vm((8, 128), F32),
        vm((slots, 8, 128), F32),
        vm((8, 128), F32),
        vm((slots, 8, 128), F32),
        vm((nt * 128, 128), F32),
        vm((nb, kb, 2 * hidden), F32),
        vm((nb, kb, 2 * hidden), BF16),
        vm((nb, kb, 2 * hidden), BF16),
        vm((nb, hidden, kb), F32),
        vm((nb, hidden, kb), BF16),
        vm((nb, hidden, kb), BF16),
        vm((toks, 128), F32),
        vm((toks, 128), F32),
        vm((16, cols_z), F32),
        vm((16, cols_z), F32),
        vm((16, cols_z), F32),
        vm((n, 16, cols_z), F32),
        vm((16, cols_z), F32),
        vm((n, 16, cols_z), F32),
        vm((8, toks), F32),
        vm((zn, 8, toks), F32),
    ]
    sems = [3, 3, 3, (slots, 3), (slots, 3), (n, 5), (n, 5), (n, 5), (n, 5)]
    sems += [2, 2, (slots, 3), (slots, 3), slots, slots]
    sems += [zn, zn, slots, slots, nb, nb, nb, nb]
    sems += [1, 1, n, n, n, n, zn, zn]
    scratch += [dma(s if isinstance(s, tuple) else (s,)) for s in sems]
    any_spec = pl.BlockSpec(memory_space=pl.ANY)
    vm_spec = pl.BlockSpec(memory_space=pltpu.VMEM)
    row = lambda v: v.reshape(1, width)
    results = pl.pallas_call(
        functools.partial(expert_kernel, n, zn),
        out_shape=(
            jax.ShapeDtypeStruct((toks, cols_z), F32),
            jax.ShapeDtypeStruct((16, cols_z), F32),
            jax.ShapeDtypeStruct((1, width, hidden), BF16),
            jax.ShapeDtypeStruct((1, width, hidden), BF16),
            jax.ShapeDtypeStruct((1, hidden, width), BF16),
        ),
        in_specs=[vm_spec] * 7 + [any_spec] * 3,
        out_specs=(vm_spec,) * 5,
        scratch_shapes=scratch,
        compiler_params=pltpu.CompilerParams(
            collective_id=0, has_side_effects=True, vmem_limit_bytes=60 * 1024 * 1024
        ),
        cost_estimate=pl.CostEstimate(
            flops=16 * rows * width * 2 * hidden, bytes_accessed=16 * 1024 * 1024, transcendentals=0
        ),
    )(
        tokens,
        cotangent,
        expert_ids.T,
        row(ada_shift),
        row(ada_scale),
        row(ada_gate),
        router_weight.T,
        gate_blocks,
        up_blocks,
        down_blocks,
    )
    grad_input, router_t, grad_gate, grad_up, grad_down = place_results(results)
    return (grad_input, router_t[:experts].T, grad_gate, grad_up, grad_down)


def solution(mesh):
    in_specs = (
        P("seq", None),
        P("seq", None),
        P("seq", None),
        P(),
        P(),
        P(),
        P(),
        P(("seq", "exp"), None, None),
        P(("seq", "exp"), None, None),
        P(("seq", "exp"), None, None),
    )
    out_specs = (
        P("seq", "exp"),
        P("exp", None),
        P(("seq", "exp"), None, None),
        P(("seq", "exp"), None, None),
        P(("seq", "exp"), None, None),
    )
    return jax.shard_map(shards, mesh=mesh, in_specs=in_specs, out_specs=out_specs, check_vma=False)
```

```python
import functools
import math

import jax
import jax.numpy as jnp
from jax import lax
from jax.experimental import pallas as pl
from jax.experimental.pallas import tpu as pltpu
from jax.sharding import PartitionSpec as P

CAP = 24
RELAYED = 3
ROLE = (1, 7, 4, 2, 5)
CLASS = (0, 0, 1, 1, 2)
SIGN = (1, -1, 1, -1, -1)
EPSILON = 1e-06
MESH = pl.DeviceIdType.MESH
F32 = jnp.float32
BF16 = jnp.bfloat16
NT = (((1,), (1,)), ((), ()))
TN = (((0,), (0,)), ((), ()))


def dot(a, b, dims=(((1,), (0,)), ((), ()))):
    return lax.dot_general(a, b, dims, preferred_element_type=F32)


def split_refs(refs, counts):
    parts, at = [], 0
    for count in counts:
        parts.append(refs[at : at + count])
        at += count
    return parts


def split3(x):
    hi = x.astype(BF16)
    rest = x - hi.astype(F32)
    mid = rest.astype(BF16)
    return hi, mid, (rest - mid.astype(F32)).astype(BF16)


def expert_kernel(n, zn, *refs):
    (
        (tokens, cotangent, ids, shift, scale, ada_gate, router, gate, up, down),
        (input_out, router_out, gate_out, up_out, down_out),
        (mod, og, place_t, send, recv, w_gate, w_up, w_down, rows_z, rows_wdy, d_gu, hid, hr),
        (gu_acc, r_acc, t_send, t_in, t_own, m_send, m_in, b_send, b_recv, e_acc),
        (term_own, term_z, term_sum, term_b, sh_own, sh_recv, sh_col),
        (gu_own, gu_send, gu_recv, dn_own, dn_send, dn_recv, gate_st, up_st, down_st, out_sem),
        (logit_acc, stat, rc_own, rc_sib, rx_sum, rx_buf, ry_sum, ry_buf, ns_own, ns_z),
        (w_local, w_ssem, w_rsem, d_ssem, d_rsem, f_ssem, f_rsem, a_ssem, a_rsem),
        (m_ssem, m_rsem, b_ssem, b_rsem, sh_ssem, sh_rsem),
        (tz_ssem, tz_rsem, tb_ssem, tb_rsem, g_ssem, g_rsem, h_ssem, h_rsem),
        (rc_ssem, rc_rsem, rx_ssem, rx_rsem, ry_ssem, ry_rsem, ns_ssem, ns_rsem),
    ) = split_refs(refs, (10, 5, 13, 10, 7, 10, 10, 9, 6, 8, 8))
    slots = n * n
    width = rows_z.shape[1]
    group = n * CAP
    hidden = w_gate.shape[2]
    kb = cols_z = width // zn
    nb = zn
    half = cols_z // 2
    toks = tokens.shape[0]
    seq = lax.axis_index("seq")
    z = lax.axis_index("exp")
    core = lax.rem(seq, 2)
    chip = seq // 2
    cy, cx = chip // n, lax.rem(chip, n)

    def offset(slot):
        dy = lax.rem(slot, n)
        dx = lax.rem(dy + slot // n, n)
        return dy, dx

    def target(slot):
        dy, dx = offset(slot)
        return (2 * (lax.rem(cy + dy, n) * n + lax.rem(cx + dx, n)) + core, z)

    def source(slot):
        dy, dx = offset(slot)
        return (2 * (lax.rem(cy - dy + n, n) * n + lax.rem(cx - dx + n, n)) + core, z)

    def z_peer(step):
        return (seq, lax.rem(z + step, zn))

    sibling = (seq + 1 - 2 * core, z)

    def remote(src, dst, ssem, rsem, dev):
        return pltpu.make_async_remote_copy(
            src_ref=src, dst_ref=dst, send_sem=ssem, recv_sem=rsem, device_id=dev, device_id_type=MESH
        )

    def plane(step):
        return lax.rem(z + step + 2 * zn, zn)

    turn = 1 - 2 * core

    def own_class(c):
        return plane(-3 * turn * c)

    def direct_copy(slot):
        dst = recv.at[slot // n, :, lax.rem(slot, n)]
        return remote(send.at[slot], dst, d_ssem.at[slot, 0], d_rsem.at[slot, 0], target(slot))

    def part_copy(slot, c):
        g = slot // n
        r = own_class(c)
        dst = recv.at[g, r, lax.rem(slot, n)]
        return remote(send.at[slot, r], dst, d_ssem.at[slot, c], d_rsem.at[slot, c], target(slot))

    def relay_copy(g, i, r):
        to = (seq, plane(turn * SIGN[i]))
        return remote(recv.at[g, r], recv.at[g, r], f_ssem.at[g, i], f_rsem.at[g, i], to)

    def near_copy(g, i):
        to = (seq, plane(-turn * SIGN[i]))
        return remote(t_send.at[g, i], t_in.at[g, i], a_ssem.at[g, i], a_rsem.at[g, i], to)

    def far_copy(c):
        to = (seq, own_class(c))
        return remote(m_send.at[c - 1], m_in.at[c - 1], m_ssem.at[c - 1], m_rsem.at[c - 1], to)

    def sh_copy(slot):
        return remote(sh_own, sh_recv.at[slot], sh_ssem.at[slot], sh_rsem.at[slot], target(slot))

    def b_copy(slot, c):
        src, dst = b_send.at[slot, c], b_recv.at[slot, c]
        return remote(src, dst, b_ssem.at[slot, c], b_rsem.at[slot, c], source(slot))

    def tz_copy(step):
        return remote(term_own, term_z.at[step], tz_ssem.at[step], tz_rsem.at[step], z_peer(step))

    def tb_copy(slot):
        return remote(term_sum, term_b.at[slot], tb_ssem.at[slot], tb_rsem.at[slot], source(slot))

    def rc_copy():
        return remote(rc_own, rc_sib, rc_ssem.at[0], rc_rsem.at[0], sibling)

    def rx_copy(step, at):
        to = (2 * (cy * n + lax.rem(cx + step, n)) + core, z)
        return remote(rx_sum, rx_buf.at[at], rx_ssem.at[step], rx_rsem.at[at], to)

    def ry_copy(step, at):
        to = (2 * (lax.rem(cy + step, n) * n + cx) + core, z)
        return remote(ry_sum, ry_buf.at[at], ry_ssem.at[step], ry_rsem.at[at], to)

    def ns_copy(step):
        return remote(ns_own, ns_z.at[step], ns_ssem.at[step], ns_rsem.at[step], z_peer(step))

    def gu_copy(b):
        return remote(gu_send.at[b], gu_recv.at[b], g_ssem.at[b], g_rsem.at[b], sibling)

    def dn_copy(b):
        return remote(dn_send.at[b], dn_recv.at[b], h_ssem.at[b], h_rsem.at[b], sibling)

    weights = ((gate, w_gate), (up, w_up), (down, w_down))

    def w_copy(i):
        hbm, vmem = weights[i]
        return remote(hbm.at[0], vmem.at[1], w_ssem.at[i], w_rsem.at[i], sibling)

    def w_copy_local(i):
        hbm, vmem = weights[i]
        return pltpu.make_async_copy(hbm.at[0], vmem.at[0], w_local.at[i])

    def loop(lo, hi, body):
        def step(i, carry):
            body(i)
            return carry

        lax.fori_loop(lo, hi, step, 0)

    barrier = pltpu.get_barrier_semaphore()
    loop(
        1,
        slots,
        lambda k: pl.semaphore_signal(barrier, inc=1, device_id=target(k), device_id_type=MESH),
    )
    loop(
        1,
        zn,
        lambda j: pl.semaphore_signal(barrier, inc=1, device_id=z_peer(j), device_id_type=MESH),
    )
    pl.semaphore_signal(barrier, inc=1, device_id=sibling, device_id_type=MESH)
    for i in range(3):
        w_copy_local(i).start()

    experts = router.shape[0]
    expert_at = lax.broadcasted_iota(jnp.int32, (toks, 128), 1)
    ids_t = jnp.concatenate([ids[...].astype(F32), jnp.zeros((126, toks), F32)], axis=0).T
    hits = [expert_at.astype(F32) == ids_t[:, k : k + 1] for k in range(2)]
    routed = jnp.where(hits[0] | hits[1], 1.0, 0.0)
    tok_at = lax.broadcasted_iota(jnp.int32, (toks, toks), 0)
    earlier = jnp.where(tok_at > lax.broadcasted_iota(jnp.int32, (toks, toks), 1), 1.0, 0.0)
    rank = dot(earlier.astype(BF16), routed.astype(BF16))
    bits = n.bit_length() - 1
    e_dy = ((expert_at >> bits) - cy) & (n - 1)
    e_dx = ((expert_at & (n - 1)) - cx) & (n - 1)
    base = ((((e_dx - e_dy) & (n - 1)) * n + e_dy) * CAP).astype(F32) + rank
    slot_at = lax.broadcasted_iota(jnp.int32, (toks, slots * CAP), 1).astype(F32)
    places = [
        jnp.where(slot_at == jnp.sum(jnp.where(h, base, 0.0), axis=1, keepdims=True), 1.0, 0.0)
        for h in hits
    ]
    place_t[...] = (places[0] + places[1]).T.astype(BF16)
    nt = hr.shape[0] // 128
    flat = lax.broadcasted_iota(jnp.int32, (8, 128), 0) * 128 + lax.broadcasted_iota(
        jnp.int32, (8, 128), 1
    )

    def merge(own, others):
        out = jnp.where(flat < CAP, own, 0.0)
        for k in range(1, slots):
            out = jnp.where((flat >= k * CAP) & (flat < (k + 1) * CAP), others[k], out)
        return out

    def modulate(i):
        rows = pl.ds(pl.multiple_of(i * 16, 16), 16)
        x = tokens[rows, :].astype(F32)
        center = jnp.sum(x, axis=1, keepdims=True) * (1.0 / width)
        x = x - center
        inv = lax.rsqrt(jnp.sum(x * x, axis=1, keepdims=True) * (1.0 / width) + EPSILON)
        mod[rows, :] = (x * inv * (1.0 + scale[...]) + shift[...]).astype(BF16)
        og[rows, :] = (ada_gate[...] * cotangent[rows, :].astype(F32)).astype(BF16)
        stat[rows, :] = jnp.where(lax.broadcasted_iota(jnp.int32, (16, 128), 1) == 0, center, inv)

    loop(0, toks // 16, modulate)
    mean, inv_std = stat[:, 0:1], stat[:, 1:2]
    hr[...] = jnp.zeros_like(hr)
    pl.semaphore_wait(barrier, slots + zn - 1)
    for i in range(3):
        w_copy(i).start()

    def fill(g, b):
        rows = pl.ds(pl.multiple_of(g * group, group), group)
        cols = pl.ds(pl.multiple_of(b * kb, kb), kb)
        zc = dot(place_t[rows, :], mod[:, cols])
        dc = dot(place_t[rows, :], og[:, cols])
        for i in range(n):
            at = slice(i * CAP, (i + 1) * CAP)
            pair = jnp.concatenate([zc[at], dc[at]], axis=0).astype(BF16)

            @pl.when(g * n + i > 0)
            def _():
                send[g * n + i, b] = pair

            if i == 0:

                @pl.when(g == 0)
                def _():
                    recv[0, b, 0] = pair

    def each_remote(g, body):
        def one(i):
            @pl.when(g * n + i > 0)
            def _():
                body(g * n + i)

        loop(0, n, one)

    def relayed_start(g):
        for c in range(3):
            fill(g, own_class(c))
            each_remote(g, lambda slot: part_copy(slot, c).start())

    def relayed_arrive(g):
        for c in range(3):
            each_remote(g, lambda slot: part_copy(slot, c).wait_recv())
            for i in range(5):
                if CLASS[i] == c:
                    relay_copy(g, i, own_class(c)).start()

    loop(0, RELAYED, relayed_start)
    logit_acc[...] = jnp.zeros_like(logit_acc)

    def add_logits(b):
        cols = pl.ds(pl.multiple_of(b * kb, kb), kb)
        logit_acc[:, :experts] += dot(mod[:, cols], router[:, cols], NT)

    loop(0, nb, add_logits)
    scores = jax.nn.sigmoid(logit_acc[...])
    picked = [jnp.sum(jnp.where(h, scores, 0.0), axis=1, keepdims=True) for h in hits]
    score_sum = picked[0] + picked[1]
    shares = [p / score_sum for p in picked]
    share_r = [s.astype(BF16).astype(F32) for s in shares]
    share_row = jnp.sum(places[0] * share_r[0] + places[1] * share_r[1], axis=0, keepdims=True)
    if nt * 128 > slots * CAP:
        share_row = jnp.concatenate(
            [share_row, jnp.zeros((1, nt * 128 - slots * CAP), F32)], axis=1
        )
    sh_own[...] = jnp.zeros_like(sh_own)
    for i in range(nt):
        sh_own[i : i + 1, :] = share_row[:, 128 * i : 128 * (i + 1)]
    loop(1, slots, lambda k: sh_copy(k).start())
    loop(RELAYED, n, lambda g: loop(0, nb, lambda b: fill(g, b)))
    for g in range(RELAYED):
        relayed_arrive(g)
        if g == 0:
            loop(RELAYED * n, (RELAYED + 1) * n, lambda k: direct_copy(k).start())
    loop(1, slots, lambda k: sh_copy(k).wait_recv())
    shares_in = merge(sh_own[...], sh_recv)
    shares_in = jnp.concatenate([shares_in, jnp.zeros((120, 128), F32)], axis=0).T
    for i in range(nt):
        sh_col[128 * i : 128 * (i + 1), :] = jnp.broadcast_to(shares_in[:, i : i + 1], (128, 128))
    for i in range(3):
        w_copy_local(i).wait()
        w_copy(i).wait()

    def wait_group(g):
        @pl.when(g < RELAYED)
        def _():
            for i in range(5):
                relay_copy(g, i, plane(-turn * ROLE[i])).wait_recv()

        @pl.when(g >= RELAYED)
        def _():
            loop(0, n, lambda i: direct_copy(g * n + i).wait_recv())

        @pl.when(g == RELAYED - 1)
        def _():
            loop((RELAYED + 1) * n, slots, lambda k: direct_copy(k).start())

    def near_sums(g):
        for c in (1, 2, 0):
            total = t_own[g, c]
            for i in range(5):
                if CLASS[i] == c:
                    near_copy(g, i).wait_recv()
                    total = total + t_in[g, i].astype(F32)
            for i in range(n):
                slot = g * n + i
                at = slice(i * CAP, (i + 1) * CAP)
                folded = jnp.concatenate([total[at, :half], total[at, half:]], axis=0)
                folded = folded.astype(BF16)

                @pl.when(slot > 0)
                def _():
                    b_send[slot, c] = folded
                    b_copy(slot, c).start()

                if i == 0:

                    @pl.when(slot == 0)
                    def _():
                        b_recv[0, c] = folded

    def combine(g, c):
        loop(
            0,
            n,
            lambda i: pl.when(g * n + i > 0)(lambda: b_copy(g * n + i, c).wait_recv()),
        )
        rows = pl.ds(pl.multiple_of(g * group, group), group)
        tiles = [b_recv[g * n + i, c].astype(F32) for i in range(n)]
        low = jnp.concatenate([t[:CAP] for t in tiles], axis=0)
        high = jnp.concatenate([t[CAP:] for t in tiles], axis=0)
        back = jnp.concatenate([low, high], axis=1).astype(BF16)
        e_acc[c] += dot(place_t[rows, :], back, TN)

    def send_terms():
        term_own[...] = jnp.zeros_like(term_own)
        for i in range(nt):
            tile = hr[128 * i : 128 * (i + 1), :]
            term_own[i : i + 1, :] = jnp.sum(tile.T, axis=0, keepdims=True)
        loop(1, zn, lambda j: tz_copy(j).start())

    def compute_group(g):
        wait_group(g)
        rows = pl.ds(pl.multiple_of(g * group, group), group)
        share = sh_col[rows, :1]
        gu_acc[...] = jnp.zeros_like(gu_acc)
        r_acc[...] = jnp.zeros_like(r_acc)

        def forward(b):
            cols = pl.ds(pl.multiple_of(b * kb, kb), kb)
            tiles = [recv[g, b, i].astype(F32) for i in range(n)]
            zb = jnp.concatenate([t[:CAP] for t in tiles], axis=0).astype(BF16)
            dyf = jnp.concatenate([t[CAP:] for t in tiles], axis=0)
            rows_z[rows, cols] = zb
            rows_wdy[rows, cols] = (share * dyf).astype(BF16)
            w_gu = [w_gate[0, cols, :], w_gate[1, cols, :], w_up[0, cols, :], w_up[1, cols, :]]
            gu_acc[...] += dot(zb, jnp.concatenate(w_gu, axis=1))
            wd = jnp.concatenate([w_down[0, :, cols], w_down[1, :, cols]], axis=0)
            r_acc[...] += dot(dyf.astype(BF16), wd, NT)

        loop(0, nb, forward)
        gv, uv, rv = gu_acc[:, : 2 * hidden], gu_acc[:, 2 * hidden :], r_acc[...]
        sig = jax.nn.sigmoid(gv)
        act = gv * sig
        hv = act * uv
        prod = hv * rv
        hr[rows, :] = prod[:, :hidden] + prod[:, hidden:]
        scaled = share * rv
        du = (scaled * act).astype(BF16)
        dg = (scaled * uv * sig * (1.0 + gv * (1.0 - sig))).astype(BF16)
        d_gu[rows, :] = jnp.concatenate(
            [dg[:, :hidden], du[:, :hidden], dg[:, hidden:], du[:, hidden:]], axis=1
        )
        hid[rows, :] = hv.astype(BF16)

        @pl.when(g == n - 1)
        def _():
            send_terms()

        def backward(r):
            wrows = pl.ds(pl.multiple_of(r * kb, kb), kb)
            w_gu = [w_gate[0, wrows, :], w_up[0, wrows, :], w_gate[1, wrows, :], w_up[1, wrows, :]]
            return dot(d_gu[rows, :], jnp.concatenate(w_gu, axis=1), NT)

        for i in (2, 3, 4, 0, 1):
            t_send[g, i] = backward(plane(-turn * ROLE[i])).astype(BF16)
            near_copy(g, i).start()
        for c in (1, 2, 0):
            t_own[g, c] = backward(own_class(c))

    def group_step(g):
        compute_group(g)

        @pl.when(g > 0)
        def _():
            near_sums(g - 1)

    loop(0, n, group_step)

    def weight_grads(b):
        cols = pl.ds(pl.multiple_of(b * kb, kb), kb)
        gu = dot(rows_z[:, cols], d_gu[...], TN)
        gu_own[b] = gu[:, : 2 * hidden]
        gu_send[b] = gu[:, 2 * hidden :].astype(BF16)
        gu_copy(b).start()
        dn = dot(hid[...], rows_wdy[:, cols], TN)
        dn_own[b] = dn[:hidden]
        dn_send[b] = dn[hidden:].astype(BF16)
        dn_copy(b).start()

    first, last = nb // 4, nb * 5 // 8
    loop(0, first, weight_grads)
    near_sums(n - 1)
    loop(1, zn, lambda j: tz_copy(j).wait_recv())
    total = term_own[...]
    for j in range(1, zn):
        total = total + term_z[j]
    term_sum[...] = total
    loop(1, slots, lambda k: tb_copy(k).start())
    e_acc[...] = jnp.zeros_like(e_acc)

    def combine_all(g):
        for c in range(3):
            combine(g, c)

    loop(0, n - 1, combine_all)
    loop(first, last, weight_grads)
    for c in (1, 2):
        combine(n - 1, c)
        m_send[c - 1] = e_acc[c].astype(BF16)
        far_copy(c).start()
    combine(n - 1, 0)
    loop(1, slots, lambda k: tb_copy(k).wait_recv())
    terms = merge(term_sum[...], term_b)
    term_row = jnp.concatenate([terms[i : i + 1] for i in range(nt)], axis=1)[:, : slots * CAP]
    choice = [jnp.sum(p * term_row, axis=1, keepdims=True) for p in places]
    mean_grad = shares[0] * choice[0] + shares[1] * choice[1]
    logit_grad = jnp.zeros((toks, 128), F32)
    for k in range(2):
        pick = (choice[k] - mean_grad) / score_sum * picked[k] * (1.0 - picked[k])
        logit_grad = logit_grad + jnp.where(hits[k], pick, 0.0)
    my_cols = pl.ds(pl.multiple_of(z * cols_z, cols_z), cols_z)
    lg_rows = logit_grad.T[:16]
    parts = [p.astype(F32) for p in split3(lg_rows)]
    prod = dot(jnp.concatenate(parts, axis=0).astype(BF16), mod[:, my_cols])
    rc_own[...] = prod[:16] + prod[16:32] + prod[32:]
    rc_copy().start()
    lg_parts = split3(logit_grad)
    mod_grad = sum(dot(p[:, :experts], router[:, my_cols]) for p in lg_parts)
    def gain_normed(r):
        cols = pl.ds(pl.multiple_of(r * kb, kb), kb)
        return 1.0 + scale[:, cols], (tokens[:, cols].astype(F32) - mean) * inv_std

    gain, normed = gain_normed(z)
    sums = [jnp.zeros((toks, 1), F32)] * 2
    for c in range(3):
        gain_c, normed_c = gain_normed(own_class(c))
        part = e_acc[c] if c > 0 else e_acc[0] + mod_grad
        part = part * gain_c
        sums[0] = sums[0] + jnp.sum(part, axis=1, keepdims=True)
        sums[1] = sums[1] + jnp.sum(part * normed_c, axis=1, keepdims=True)
    lane = lax.broadcasted_iota(jnp.int32, (toks, 128), 1)
    sums_t = jnp.where(lane == 0, sums[0], jnp.where(lane == 1, sums[1], 0.0)).T
    ns_own[...] = sums_t[:8]
    loop(1, zn, lambda j: ns_copy(j).start())
    loop(last, nb, weight_grads)

    def finish(b):
        gu_copy(b).wait_recv()
        dn_copy(b).wait_recv()
        cols = pl.ds(pl.multiple_of(b * kb, kb), kb)
        gu = gu_own[b] + gu_recv[b].astype(F32)
        gate_st[cols, :] = gu[:, :hidden].astype(BF16)
        up_st[cols, :] = gu[:, hidden:].astype(BF16)
        down_st[:, cols] = (dn_own[b] + dn_recv[b].astype(F32)).astype(BF16)

    rc_copy().wait_recv()
    rx_sum[...] = rc_own[...] + rc_sib[...]
    rx_buf[cx] = rx_sum[...]
    loop(1, n, lambda j: rx_copy(j, cx).start())
    loop(0, nb // 2, finish)
    loop(1, n, lambda j: rx_copy(j, lax.rem(cx + j, n)).wait_recv())
    total = rx_buf[0]
    for j in range(1, n):
        total = total + rx_buf[j]
    ry_sum[...] = total
    ry_buf[cy] = total
    loop(1, n, lambda j: ry_copy(j, cy).start())
    loop(nb // 2, nb, finish)
    staged = ((gate_st, gate_out), (up_st, up_out), (down_st, down_out))
    stores = [
        pltpu.make_async_copy(src, dst.at[0], out_sem.at[i]) for i, (src, dst) in enumerate(staged)
    ]
    for store in stores:
        store.start()

    for c in (1, 2):
        far_copy(c).wait_recv()
    expert_grad = e_acc[0] + m_in[0].astype(F32) + m_in[1].astype(F32)
    norm_grad = (mod_grad + expert_grad) * gain
    loop(1, n, lambda j: ry_copy(j, lax.rem(cy + j, n)).wait_recv())
    total = ry_buf[0]
    for j in range(1, n):
        total = total + ry_buf[j]
    router_out[...] = total

    loop(1, zn, lambda j: ns_copy(j).wait_recv())
    total = ns_own[...]
    for j in range(1, zn):
        total = total + ns_z[j]
    total = jnp.concatenate([total, jnp.zeros((120, toks), F32)], axis=0).T * (1.0 / width)
    input_out[...] = inv_std * (norm_grad - total[:, 0:1] - normed * total[:, 1:2])

    def drain_slot(k):
        sh_copy(k).wait_send()
        for c in range(3):
            b_copy(k, c).wait_send()
        tb_copy(k).wait_send()

        @pl.when(k < RELAYED * n)
        def _():
            for c in range(3):
                part_copy(k, c).wait_send()

        @pl.when(k >= RELAYED * n)
        def _():
            direct_copy(k).wait_send()

    for store in stores:
        store.wait()
    loop(1, slots, drain_slot)

    def drain_group(g):
        for i in range(5):
            near_copy(g, i).wait_send()

        @pl.when(g < RELAYED)
        def _():
            for i in range(5):
                relay_copy(g, i, own_class(CLASS[i])).wait_send()

    loop(0, n, drain_group)
    for c in (1, 2):
        far_copy(c).wait_send()

    def drain_ring(j):
        rx_copy(j, cx).wait_send()
        ry_copy(j, cy).wait_send()

    rc_copy().wait_send()
    loop(1, n, drain_ring)

    def drain_z(j):
        tz_copy(j).wait_send()
        ns_copy(j).wait_send()

    loop(1, zn, drain_z)

    def drain_b(b):
        gu_copy(b).wait_send()
        dn_copy(b).wait_send()

    loop(0, nb, drain_b)


def copy_kernel(count, *refs):
    sems = refs[-1]
    held = refs[2 * count : 3 * count]
    arrive = [pltpu.make_async_copy(refs[i], held[i], sems.at[0, i]) for i in range(count)]
    leave = [
        pltpu.make_async_copy(held[i], refs[count + i], sems.at[1, i]) for i in range(count)
    ]
    for copy in arrive:
        copy.start()
    for i in range(count):
        arrive[i].wait()
        leave[i].start()
    for copy in leave:
        copy.wait()


def place_results(arrays):
    count = len(arrays)
    any_spec = pl.BlockSpec(memory_space=pl.ANY)
    return pl.pallas_call(
        functools.partial(copy_kernel, count),
        out_shape=tuple(jax.ShapeDtypeStruct(a.shape, a.dtype) for a in arrays),
        in_specs=[any_spec] * count,
        out_specs=(any_spec,) * count,
        scratch_shapes=[pltpu.VMEM(a.shape, a.dtype) for a in arrays]
        + [pltpu.SemaphoreType.DMA((2, count))],
        compiler_params=pltpu.CompilerParams(vmem_limit_bytes=60 * 1024 * 1024),
    )(*arrays)


def shards(
    tokens,
    cotangent,
    expert_ids,
    ada_shift,
    ada_scale,
    ada_gate,
    router_weight,
    gate_blocks,
    up_blocks,
    down_blocks,
):
    zn = lax.axis_size("exp")
    n = math.isqrt(lax.axis_size("seq") // 2)
    slots = n * n
    toks, width = tokens.shape
    experts = router_weight.shape[1]
    hidden = gate_blocks.shape[2]
    rows = slots * CAP
    cols_z = kb = width // zn
    nb = zn
    nt = -(-rows // 128)
    group = n * CAP
    dma = pltpu.SemaphoreType.DMA
    vm = pltpu.VMEM
    scratch = [
        vm((toks, width), BF16),
        vm((toks, width), BF16),
        vm((rows, toks), BF16),
        vm((slots, nb, 2 * CAP, kb), BF16),
        vm((n, nb, n, 2 * CAP, kb), BF16),
        vm((2, width, hidden), BF16),
        vm((2, width, hidden), BF16),
        vm((2, hidden, width), BF16),
        vm((rows, width), BF16),
        vm((rows, width), BF16),
        vm((rows, 4 * hidden), BF16),
        vm((rows, 2 * hidden), BF16),
        vm((nt * 128, hidden), F32),
        vm((group, 4 * hidden), F32),
        vm((group, 2 * hidden), F32),
        vm((n, 5, group, kb), BF16),
        vm((n, 5, group, kb), BF16),
        vm((n, 3, group, kb), F32),
        vm((2, toks, kb), BF16),
        vm((2, toks, kb), BF16),
        vm((slots, 3, 2 * CAP, kb // 2), BF16),
        vm((slots, 3, 2 * CAP, kb // 2), BF16),
        vm((3, toks, kb), F32),
        vm((8, 128), F32),
        vm((zn, 8, 128), F32),
        vm((8, 128), F32),
        vm((slots, 8, 128), F32),
        vm((8, 128), F32),
        vm((slots, 8, 128), F32),
        vm((nt * 128, 128), F32),
        vm((nb, kb, 2 * hidden), F32),
        vm((nb, kb, 2 * hidden), BF16),
        vm((nb, kb, 2 * hidden), BF16),
        vm((nb, hidden, kb), F32),
        vm((nb, hidden, kb), BF16),
        vm((nb, hidden, kb), BF16),
        vm((width, hidden), BF16),
        vm((width, hidden), BF16),
        vm((hidden, width), BF16),
        dma((3,)),
        vm((toks, 128), F32),
        vm((toks, 128), F32),
        vm((16, cols_z), F32),
        vm((16, cols_z), F32),
        vm((16, cols_z), F32),
        vm((n, 16, cols_z), F32),
        vm((16, cols_z), F32),
        vm((n, 16, cols_z), F32),
        vm((8, toks), F32),
        vm((zn, 8, toks), F32),
    ]
    sems = [3, 3, 3, (slots, 3), (slots, 3), (n, 5), (n, 5), (n, 5), (n, 5)]
    sems += [2, 2, (slots, 3), (slots, 3), slots, slots]
    sems += [zn, zn, slots, slots, nb, nb, nb, nb]
    sems += [1, 1, n, n, n, n, zn, zn]
    scratch += [dma(s if isinstance(s, tuple) else (s,)) for s in sems]
    any_spec = pl.BlockSpec(memory_space=pl.ANY)
    vm_spec = pl.BlockSpec(memory_space=pltpu.VMEM)
    row = lambda v: v.reshape(1, width)
    results = pl.pallas_call(
        functools.partial(expert_kernel, n, zn),
        out_shape=(
            jax.ShapeDtypeStruct((toks, cols_z), F32),
            jax.ShapeDtypeStruct((16, cols_z), F32),
            jax.ShapeDtypeStruct((1, width, hidden), BF16),
            jax.ShapeDtypeStruct((1, width, hidden), BF16),
            jax.ShapeDtypeStruct((1, hidden, width), BF16),
        ),
        in_specs=[vm_spec] * 7 + [any_spec] * 3,
        out_specs=(vm_spec,) * 2 + (any_spec,) * 3,
        scratch_shapes=scratch,
        compiler_params=pltpu.CompilerParams(
            collective_id=0, has_side_effects=True, vmem_limit_bytes=60 * 1024 * 1024
        ),
        cost_estimate=pl.CostEstimate(
            flops=16 * rows * width * 2 * hidden, bytes_accessed=16 * 1024 * 1024, transcendentals=0
        ),
    )(
        tokens,
        cotangent,
        expert_ids.T,
        row(ada_shift),
        row(ada_scale),
        row(ada_gate),
        router_weight.T,
        gate_blocks,
        up_blocks,
        down_blocks,
    )
    grad_input, router_t, grad_gate, grad_up, grad_down = place_results(results)
    return (grad_input, router_t[:experts].T, grad_gate, grad_up, grad_down)


def solution(mesh):
    in_specs = (
        P("seq", None),
        P("seq", None),
        P("seq", None),
        P(),
        P(),
        P(),
        P(),
        P(("seq", "exp"), None, None),
        P(("seq", "exp"), None, None),
        P(("seq", "exp"), None, None),
    )
    out_specs = (
        P("seq", "exp"),
        P("exp", None),
        P(("seq", "exp"), None, None),
        P(("seq", "exp"), None, None),
        P(("seq", "exp"), None, None),
    )
    return jax.shard_map(shards, mesh=mesh, in_specs=in_specs, out_specs=out_specs, check_vma=False)
```

```python
import functools
import math

import jax
import jax.numpy as jnp
from jax import lax
from jax.experimental import pallas as pl
from jax.experimental.pallas import tpu as pltpu
from jax.sharding import PartitionSpec as P

CAP = 24
RELAYED = 3
PARTS = 4
ROLE = (1, 7, 4, 2, 5)
CLASS = (0, 0, 1, 1, 2)
SIGN = (1, -1, 1, -1, -1)
EPSILON = 1e-06
MESH = pl.DeviceIdType.MESH
F32 = jnp.float32
BF16 = jnp.bfloat16
NT = (((1,), (1,)), ((), ()))
TN = (((0,), (0,)), ((), ()))


def dot(a, b, dims=(((1,), (0,)), ((), ()))):
    return lax.dot_general(a, b, dims, preferred_element_type=F32)


def split_refs(refs, counts):
    parts, at = [], 0
    for count in counts:
        parts.append(refs[at : at + count])
        at += count
    return parts


def split3(x):
    hi = x.astype(BF16)
    rest = x - hi.astype(F32)
    mid = rest.astype(BF16)
    return hi, mid, (rest - mid.astype(F32)).astype(BF16)


def expert_kernel(n, zn, *refs):
    (
        (tokens, cotangent, ids, shift, scale, ada_gate, router, gate, up, down),
        (input_out, router_out, gate_out, up_out, down_out),
        (mod, og, place_t, send, recv, w_gate, w_up, w_down, rows_z, rows_wdy, d_gu, hid, hr),
        (gu_acc, r_acc, t_send, t_in, t_own, m_send, m_in, b_send, b_recv, e_acc),
        (term_own, term_z, term_sum, term_b, sh_own, sh_recv, sh_col),
        (gu_own, gu_send, gu_recv, dn_own, dn_send, dn_recv, gate_st, up_st, down_st, out_sem),
        (logit_acc, stat, rc_own, rc_sib, rx_sum, rx_buf, ry_sum, ry_buf, ns_own, ns_z),
        (w_local, w_ssem, w_rsem, d_ssem, d_rsem, f_ssem, f_rsem, a_ssem, a_rsem),
        (m_ssem, m_rsem, b_ssem, b_rsem, sh_ssem, sh_rsem),
        (tz_ssem, tz_rsem, tb_ssem, tb_rsem, g_ssem, g_rsem, h_ssem, h_rsem),
        (rc_ssem, rc_rsem, rx_ssem, rx_rsem, ry_ssem, ry_rsem, ns_ssem, ns_rsem),
    ) = split_refs(refs, (10, 5, 13, 10, 7, 10, 10, 9, 6, 8, 8))
    slots = n * n
    width = rows_z.shape[1]
    group = n * CAP
    hidden = w_gate.shape[2]
    kb = cols_z = width // zn
    nb = zn
    half = cols_z // 2
    toks = tokens.shape[0]
    seq = lax.axis_index("seq")
    z = lax.axis_index("exp")
    core = lax.rem(seq, 2)
    chip = seq // 2
    cy, cx = chip // n, lax.rem(chip, n)

    def offset(slot):
        dy = lax.rem(slot, n)
        dx = lax.rem(dy + slot // n, n)
        return dy, dx

    def target(slot):
        dy, dx = offset(slot)
        return (2 * (lax.rem(cy + dy, n) * n + lax.rem(cx + dx, n)) + core, z)

    def source(slot):
        dy, dx = offset(slot)
        return (2 * (lax.rem(cy - dy + n, n) * n + lax.rem(cx - dx + n, n)) + core, z)

    def z_peer(step):
        return (seq, lax.rem(z + step, zn))

    sibling = (seq + 1 - 2 * core, z)

    def remote(src, dst, ssem, rsem, dev):
        return pltpu.make_async_remote_copy(
            src_ref=src, dst_ref=dst, send_sem=ssem, recv_sem=rsem, device_id=dev, device_id_type=MESH
        )

    def plane(step):
        return lax.rem(z + step + 2 * zn, zn)

    turn = 1 - 2 * core

    def own_class(c):
        return plane(-3 * turn * c)

    def direct_copy(slot):
        dst = recv.at[slot // n, :, lax.rem(slot, n)]
        return remote(send.at[slot], dst, d_ssem.at[slot, 0], d_rsem.at[slot, 0], target(slot))

    def part_copy(slot, c):
        g = slot // n
        r = own_class(c)
        dst = recv.at[g, r, lax.rem(slot, n)]
        return remote(send.at[slot, r], dst, d_ssem.at[slot, c], d_rsem.at[slot, c], target(slot))

    def relay_copy(g, i, r):
        to = (seq, plane(turn * SIGN[i]))
        return remote(recv.at[g, r], recv.at[g, r], f_ssem.at[g, i], f_rsem.at[g, i], to)

    def near_copy(g, i):
        to = (seq, plane(-turn * SIGN[i]))
        return remote(t_send.at[g, i], t_in.at[g, i], a_ssem.at[g, i], a_rsem.at[g, i], to)

    def far_copy(c):
        to = (seq, own_class(c))
        return remote(m_send.at[c - 1], m_in.at[c - 1], m_ssem.at[c - 1], m_rsem.at[c - 1], to)

    def sh_copy(slot):
        return remote(sh_own, sh_recv.at[slot], sh_ssem.at[slot], sh_rsem.at[slot], target(slot))

    def b_copy(slot, c):
        src, dst = b_send.at[slot, c], b_recv.at[slot, c]
        return remote(src, dst, b_ssem.at[slot, c], b_rsem.at[slot, c], source(slot))

    def tz_copy(step):
        return remote(term_own, term_z.at[step], tz_ssem.at[step], tz_rsem.at[step], z_peer(step))

    def tb_copy(slot):
        return remote(term_sum, term_b.at[slot], tb_ssem.at[slot], tb_rsem.at[slot], source(slot))

    def rc_copy():
        return remote(rc_own, rc_sib, rc_ssem.at[0], rc_rsem.at[0], sibling)

    def rx_copy(step, at):
        to = (2 * (cy * n + lax.rem(cx + step, n)) + core, z)
        return remote(rx_sum, rx_buf.at[at], rx_ssem.at[step], rx_rsem.at[at], to)

    def ry_copy(step, at):
        to = (2 * (lax.rem(cy + step, n) * n + cx) + core, z)
        return remote(ry_sum, ry_buf.at[at], ry_ssem.at[step], ry_rsem.at[at], to)

    def ns_copy(step):
        return remote(ns_own, ns_z.at[step], ns_ssem.at[step], ns_rsem.at[step], z_peer(step))

    def gu_copy(b):
        return remote(gu_send.at[b], gu_recv.at[b], g_ssem.at[b], g_rsem.at[b], sibling)

    def dn_copy(b):
        return remote(dn_send.at[b], dn_recv.at[b], h_ssem.at[b], h_rsem.at[b], sibling)

    weights = ((gate, w_gate), (up, w_up), (down, w_down))

    def w_copy(i):
        hbm, vmem = weights[i]
        return remote(hbm.at[0], vmem.at[1], w_ssem.at[i], w_rsem.at[i], sibling)

    def w_copy_local(i):
        hbm, vmem = weights[i]
        return pltpu.make_async_copy(hbm.at[0], vmem.at[0], w_local.at[i])

    def loop(lo, hi, body):
        def step(i, carry):
            body(i)
            return carry

        lax.fori_loop(lo, hi, step, 0)

    barrier = pltpu.get_barrier_semaphore()
    loop(
        1,
        slots,
        lambda k: pl.semaphore_signal(barrier, inc=1, device_id=target(k), device_id_type=MESH),
    )
    loop(
        1,
        zn,
        lambda j: pl.semaphore_signal(barrier, inc=1, device_id=z_peer(j), device_id_type=MESH),
    )
    pl.semaphore_signal(barrier, inc=1, device_id=sibling, device_id_type=MESH)
    for i in range(3):
        w_copy_local(i).start()

    experts = router.shape[0]
    expert_at = lax.broadcasted_iota(jnp.int32, (toks, 128), 1)
    ids_t = jnp.concatenate([ids[...].astype(F32), jnp.zeros((126, toks), F32)], axis=0).T
    hits = [expert_at.astype(F32) == ids_t[:, k : k + 1] for k in range(2)]
    routed = jnp.where(hits[0] | hits[1], 1.0, 0.0)
    tok_at = lax.broadcasted_iota(jnp.int32, (toks, toks), 0)
    earlier = jnp.where(tok_at > lax.broadcasted_iota(jnp.int32, (toks, toks), 1), 1.0, 0.0)
    rank = dot(earlier.astype(BF16), routed.astype(BF16))
    bits = n.bit_length() - 1
    e_dy = ((expert_at >> bits) - cy) & (n - 1)
    e_dx = ((expert_at & (n - 1)) - cx) & (n - 1)
    base = ((((e_dx - e_dy) & (n - 1)) * n + e_dy) * CAP).astype(F32) + rank
    slot_at = lax.broadcasted_iota(jnp.int32, (toks, slots * CAP), 1).astype(F32)
    places = [
        jnp.where(slot_at == jnp.sum(jnp.where(h, base, 0.0), axis=1, keepdims=True), 1.0, 0.0)
        for h in hits
    ]
    place_t[...] = (places[0] + places[1]).T.astype(BF16)
    nt = hr.shape[0] // 128
    flat = lax.broadcasted_iota(jnp.int32, (8, 128), 0) * 128 + lax.broadcasted_iota(
        jnp.int32, (8, 128), 1
    )

    def merge(own, others):
        out = jnp.where(flat < CAP, own, 0.0)
        for k in range(1, slots):
            out = jnp.where((flat >= k * CAP) & (flat < (k + 1) * CAP), others[k], out)
        return out

    def modulate(i):
        rows = pl.ds(pl.multiple_of(i * 16, 16), 16)
        x = tokens[rows, :].astype(F32)
        center = jnp.sum(x, axis=1, keepdims=True) * (1.0 / width)
        x = x - center
        inv = lax.rsqrt(jnp.sum(x * x, axis=1, keepdims=True) * (1.0 / width) + EPSILON)
        mod[rows, :] = (x * inv * (1.0 + scale[...]) + shift[...]).astype(BF16)
        og[rows, :] = (ada_gate[...] * cotangent[rows, :].astype(F32)).astype(BF16)
        stat[rows, :] = jnp.where(lax.broadcasted_iota(jnp.int32, (16, 128), 1) == 0, center, inv)

    loop(0, toks // 16, modulate)
    mean, inv_std = stat[:, 0:1], stat[:, 1:2]
    hr[...] = jnp.zeros_like(hr)
    pl.semaphore_wait(barrier, slots + zn - 1)
    for i in range(3):
        w_copy(i).start()

    def fill(g, b):
        rows = pl.ds(pl.multiple_of(g * group, group), group)
        cols = pl.ds(pl.multiple_of(b * kb, kb), kb)
        zc = dot(place_t[rows, :], mod[:, cols])
        dc = dot(place_t[rows, :], og[:, cols])
        for i in range(n):
            at = slice(i * CAP, (i + 1) * CAP)
            pair = jnp.concatenate([zc[at], dc[at]], axis=0).astype(BF16)

            @pl.when(g * n + i > 0)
            def _():
                send[g * n + i, b] = pair

            if i == 0:

                @pl.when(g == 0)
                def _():
                    recv[0, b, 0] = pair

    def each_remote(g, body):
        def one(i):
            @pl.when(g * n + i > 0)
            def _():
                body(g * n + i)

        loop(0, n, one)

    def relayed_start(g):
        for c in range(3):
            fill(g, own_class(c))
            each_remote(g, lambda slot: part_copy(slot, c).start())

    def relayed_arrive(g):
        for c in range(3):
            each_remote(g, lambda slot: part_copy(slot, c).wait_recv())
            for i in range(5):
                if CLASS[i] == c:
                    relay_copy(g, i, own_class(c)).start()

    loop(0, RELAYED, relayed_start)
    logit_acc[...] = jnp.zeros_like(logit_acc)

    def add_logits(b):
        cols = pl.ds(pl.multiple_of(b * kb, kb), kb)
        logit_acc[:, :experts] += dot(mod[:, cols], router[:, cols], NT)

    loop(0, nb, add_logits)
    scores = jax.nn.sigmoid(logit_acc[...])
    picked = [jnp.sum(jnp.where(h, scores, 0.0), axis=1, keepdims=True) for h in hits]
    score_sum = picked[0] + picked[1]
    shares = [p / score_sum for p in picked]
    share_r = [s.astype(BF16).astype(F32) for s in shares]
    share_row = jnp.sum(places[0] * share_r[0] + places[1] * share_r[1], axis=0, keepdims=True)
    if nt * 128 > slots * CAP:
        share_row = jnp.concatenate(
            [share_row, jnp.zeros((1, nt * 128 - slots * CAP), F32)], axis=1
        )
    sh_own[...] = jnp.zeros_like(sh_own)
    for i in range(nt):
        sh_own[i : i + 1, :] = share_row[:, 128 * i : 128 * (i + 1)]
    loop(1, slots, lambda k: sh_copy(k).start())
    loop(RELAYED, n, lambda g: loop(0, nb, lambda b: fill(g, b)))
    for g in range(RELAYED):
        relayed_arrive(g)
        if g == 0:
            loop(RELAYED * n, (RELAYED + 1) * n, lambda k: direct_copy(k).start())
    loop(1, slots, lambda k: sh_copy(k).wait_recv())
    shares_in = merge(sh_own[...], sh_recv)
    shares_in = jnp.concatenate([shares_in, jnp.zeros((120, 128), F32)], axis=0).T
    for i in range(nt):
        sh_col[128 * i : 128 * (i + 1), :] = jnp.broadcast_to(shares_in[:, i : i + 1], (128, 128))
    for i in range(3):
        w_copy_local(i).wait()
        w_copy(i).wait()

    def wait_group(g):
        @pl.when(g < RELAYED)
        def _():
            for i in range(5):
                relay_copy(g, i, plane(-turn * ROLE[i])).wait_recv()

        @pl.when(g >= RELAYED)
        def _():
            loop(0, n, lambda i: direct_copy(g * n + i).wait_recv())

        @pl.when(g == RELAYED - 1)
        def _():
            loop((RELAYED + 1) * n, slots, lambda k: direct_copy(k).start())

    def near_sums(g):
        for c in (1, 2, 0):
            total = t_own[g, c]
            for i in range(5):
                if CLASS[i] == c:
                    near_copy(g, i).wait_recv()
                    total = total + t_in[g, i].astype(F32)
            for i in range(n):
                slot = g * n + i
                at = slice(i * CAP, (i + 1) * CAP)
                folded = jnp.concatenate([total[at, :half], total[at, half:]], axis=0)
                folded = folded.astype(BF16)

                @pl.when(slot > 0)
                def _():
                    b_send[slot, c] = folded
                    b_copy(slot, c).start()

                if i == 0:

                    @pl.when(slot == 0)
                    def _():
                        b_recv[0, c] = folded

    def combine(g, c):
        loop(
            0,
            n,
            lambda i: pl.when(g * n + i > 0)(lambda: b_copy(g * n + i, c).wait_recv()),
        )
        rows = pl.ds(pl.multiple_of(g * group, group), group)
        tiles = [b_recv[g * n + i, c].astype(F32) for i in range(n)]
        low = jnp.concatenate([t[:CAP] for t in tiles], axis=0)
        high = jnp.concatenate([t[CAP:] for t in tiles], axis=0)
        back = jnp.concatenate([low, high], axis=1).astype(BF16)
        e_acc[c] += dot(place_t[rows, :], back, TN)

    def send_terms():
        term_own[...] = jnp.zeros_like(term_own)
        for i in range(nt):
            tile = hr[128 * i : 128 * (i + 1), :]
            term_own[i : i + 1, :] = jnp.sum(tile.T, axis=0, keepdims=True)
        loop(1, zn, lambda j: tz_copy(j).start())

    def compute_group(g):
        wait_group(g)
        rows = pl.ds(pl.multiple_of(g * group, group), group)
        share = sh_col[rows, :1]
        gu_acc[...] = jnp.zeros_like(gu_acc)
        r_acc[...] = jnp.zeros_like(r_acc)

        def forward(b):
            cols = pl.ds(pl.multiple_of(b * kb, kb), kb)
            tiles = [recv[g, b, i].astype(F32) for i in range(n)]
            zb = jnp.concatenate([t[:CAP] for t in tiles], axis=0).astype(BF16)
            dyf = jnp.concatenate([t[CAP:] for t in tiles], axis=0)
            rows_z[rows, cols] = zb
            rows_wdy[rows, cols] = (share * dyf).astype(BF16)
            w_gu = [w_gate[0, cols, :], w_gate[1, cols, :], w_up[0, cols, :], w_up[1, cols, :]]
            gu_acc[...] += dot(zb, jnp.concatenate(w_gu, axis=1))
            wd = jnp.concatenate([w_down[0, :, cols], w_down[1, :, cols]], axis=0)
            r_acc[...] += dot(dyf.astype(BF16), wd, NT)

        loop(0, nb, forward)
        gv, uv, rv = gu_acc[:, : 2 * hidden], gu_acc[:, 2 * hidden :], r_acc[...]
        sig = jax.nn.sigmoid(gv)
        act = gv * sig
        hv = act * uv
        prod = hv * rv
        hr[rows, :] = prod[:, :hidden] + prod[:, hidden:]
        scaled = share * rv
        du = (scaled * act).astype(BF16)
        dg = (scaled * uv * sig * (1.0 + gv * (1.0 - sig))).astype(BF16)
        d_gu[rows, :] = jnp.concatenate(
            [dg[:, :hidden], du[:, :hidden], dg[:, hidden:], du[:, hidden:]], axis=1
        )
        hid[rows, :] = hv.astype(BF16)

        @pl.when(g == n - 1)
        def _():
            send_terms()

        def backward(r):
            wrows = pl.ds(pl.multiple_of(r * kb, kb), kb)
            w_gu = [w_gate[0, wrows, :], w_up[0, wrows, :], w_gate[1, wrows, :], w_up[1, wrows, :]]
            return dot(d_gu[rows, :], jnp.concatenate(w_gu, axis=1), NT)

        for i in (2, 3, 4, 0, 1):
            t_send[g, i] = backward(plane(-turn * ROLE[i])).astype(BF16)
            near_copy(g, i).start()
        for c in (1, 2, 0):
            t_own[g, c] = backward(own_class(c))

    def group_step(g):
        compute_group(g)

        @pl.when(g > 0)
        def _():
            near_sums(g - 1)

    loop(0, n, group_step)

    def weight_grads(b):
        cols = pl.ds(pl.multiple_of(b * kb, kb), kb)
        gu = dot(rows_z[:, cols], d_gu[...], TN)
        gu_own[b] = gu[:, : 2 * hidden]
        gu_send[b] = gu[:, 2 * hidden :].astype(BF16)
        gu_copy(b).start()
        dn = dot(hid[...], rows_wdy[:, cols], TN)
        dn_own[b] = dn[:hidden]
        dn_send[b] = dn[hidden:].astype(BF16)
        dn_copy(b).start()

    first, last = nb // 4, nb * 5 // 8
    loop(0, first, weight_grads)
    near_sums(n - 1)
    loop(1, zn, lambda j: tz_copy(j).wait_recv())
    total = term_own[...]
    for j in range(1, zn):
        total = total + term_z[j]
    term_sum[...] = total
    loop(1, slots, lambda k: tb_copy(k).start())
    e_acc[...] = jnp.zeros_like(e_acc)

    def combine_all(g):
        for c in range(3):
            combine(g, c)

    loop(0, n - 1, combine_all)
    loop(first, last, weight_grads)
    for c in (1, 2):
        combine(n - 1, c)
        m_send[c - 1] = e_acc[c].astype(BF16)
        far_copy(c).start()
    combine(n - 1, 0)
    loop(1, slots, lambda k: tb_copy(k).wait_recv())
    terms = merge(term_sum[...], term_b)
    term_row = jnp.concatenate([terms[i : i + 1] for i in range(nt)], axis=1)[:, : slots * CAP]
    choice = [jnp.sum(p * term_row, axis=1, keepdims=True) for p in places]
    mean_grad = shares[0] * choice[0] + shares[1] * choice[1]
    logit_grad = jnp.zeros((toks, 128), F32)
    for k in range(2):
        pick = (choice[k] - mean_grad) / score_sum * picked[k] * (1.0 - picked[k])
        logit_grad = logit_grad + jnp.where(hits[k], pick, 0.0)
    my_cols = pl.ds(pl.multiple_of(z * cols_z, cols_z), cols_z)
    lg_rows = logit_grad.T[:16]
    parts = [p.astype(F32) for p in split3(lg_rows)]
    prod = dot(jnp.concatenate(parts, axis=0).astype(BF16), mod[:, my_cols])
    rc_own[...] = prod[:16] + prod[16:32] + prod[32:]
    rc_copy().start()
    lg_parts = split3(logit_grad)
    mod_grad = sum(dot(p[:, :experts], router[:, my_cols]) for p in lg_parts)
    def gain_normed(r):
        cols = pl.ds(pl.multiple_of(r * kb, kb), kb)
        return 1.0 + scale[:, cols], (tokens[:, cols].astype(F32) - mean) * inv_std

    gain, normed = gain_normed(z)
    sums = [jnp.zeros((toks, 1), F32)] * 2
    for c in range(3):
        gain_c, normed_c = gain_normed(own_class(c))
        part = e_acc[c] if c > 0 else e_acc[0] + mod_grad
        part = part * gain_c
        sums[0] = sums[0] + jnp.sum(part, axis=1, keepdims=True)
        sums[1] = sums[1] + jnp.sum(part * normed_c, axis=1, keepdims=True)
    lane = lax.broadcasted_iota(jnp.int32, (toks, 128), 1)
    sums_t = jnp.where(lane == 0, sums[0], jnp.where(lane == 1, sums[1], 0.0)).T
    ns_own[...] = sums_t[:8]
    loop(1, zn, lambda j: ns_copy(j).start())
    loop(last, nb, weight_grads)

    def finish(b):
        gu_copy(b).wait_recv()
        dn_copy(b).wait_recv()
        cols = pl.ds(pl.multiple_of(b * kb, kb), kb)
        gu = gu_own[b] + gu_recv[b].astype(F32)
        gate_st[cols, :] = gu[:, :hidden].astype(BF16)
        up_st[cols, :] = gu[:, hidden:].astype(BF16)
        down_st[:, cols] = (dn_own[b] + dn_recv[b].astype(F32)).astype(BF16)

    rc_copy().wait_recv()
    rx_sum[...] = rc_own[...] + rc_sib[...]
    rx_buf[cx] = rx_sum[...]
    loop(1, n, lambda j: rx_copy(j, cx).start())
    loop(0, nb // 2, finish)
    loop(1, n, lambda j: rx_copy(j, lax.rem(cx + j, n)).wait_recv())
    total = rx_buf[0]
    for j in range(1, n):
        total = total + rx_buf[j]
    ry_sum[...] = total
    ry_buf[cy] = total
    loop(1, n, lambda j: ry_copy(j, cy).start())
    loop(nb // 2, nb, finish)
    staged = ((gate_st, gate_out), (up_st, up_out), (down_st, down_out))
    stores = [
        pltpu.make_async_copy(src, dst.at[0], out_sem.at[i]) for i, (src, dst) in enumerate(staged)
    ]
    for store in stores:
        store.start()

    for c in (1, 2):
        far_copy(c).wait_recv()
    expert_grad = e_acc[0] + m_in[0].astype(F32) + m_in[1].astype(F32)
    norm_grad = (mod_grad + expert_grad) * gain
    loop(1, n, lambda j: ry_copy(j, lax.rem(cy + j, n)).wait_recv())
    total = ry_buf[0]
    for j in range(1, n):
        total = total + ry_buf[j]
    router_out[...] = total

    loop(1, zn, lambda j: ns_copy(j).wait_recv())
    total = ns_own[...]
    for j in range(1, zn):
        total = total + ns_z[j]
    total = jnp.concatenate([total, jnp.zeros((120, toks), F32)], axis=0).T * (1.0 / width)
    input_out[...] = inv_std * (norm_grad - total[:, 0:1] - normed * total[:, 1:2])

    def drain_slot(k):
        sh_copy(k).wait_send()
        for c in range(3):
            b_copy(k, c).wait_send()
        tb_copy(k).wait_send()

        @pl.when(k < RELAYED * n)
        def _():
            for c in range(3):
                part_copy(k, c).wait_send()

        @pl.when(k >= RELAYED * n)
        def _():
            direct_copy(k).wait_send()

    for store in stores:
        store.wait()
    loop(1, slots, drain_slot)

    def drain_group(g):
        for i in range(5):
            near_copy(g, i).wait_send()

        @pl.when(g < RELAYED)
        def _():
            for i in range(5):
                relay_copy(g, i, own_class(CLASS[i])).wait_send()

    loop(0, n, drain_group)
    for c in (1, 2):
        far_copy(c).wait_send()

    def drain_ring(j):
        rx_copy(j, cx).wait_send()
        ry_copy(j, cy).wait_send()

    rc_copy().wait_send()
    loop(1, n, drain_ring)

    def drain_z(j):
        tz_copy(j).wait_send()
        ns_copy(j).wait_send()

    loop(1, zn, drain_z)

    def drain_b(b):
        gu_copy(b).wait_send()
        dn_copy(b).wait_send()

    loop(0, nb, drain_b)


def copy_kernel(count, *refs):
    sems = refs[-1]
    held = refs[2 * count : 3 * count]
    pieces = []
    for i in range(count):
        cuts = PARTS if len(held[i].shape) == 3 else 1
        step = held[i].shape[-2] // cuts
        for part in range(cuts):
            rows = pl.ds(part * step, step)
            at = (0, rows) if len(held[i].shape) == 3 else (rows,)
            pieces.append((refs[i].at[at], held[i].at[at], refs[count + i].at[at]))
    arrive = [
        pltpu.make_async_copy(src, mid, sems.at[0, p]) for p, (src, mid, dst) in enumerate(pieces)
    ]
    leave = [
        pltpu.make_async_copy(mid, dst, sems.at[1, p]) for p, (src, mid, dst) in enumerate(pieces)
    ]
    for copy in arrive:
        copy.start()
    for p in range(len(pieces)):
        arrive[p].wait()
        leave[p].start()
    for copy in leave:
        copy.wait()


def place_results(arrays):
    count = len(arrays)
    any_spec = pl.BlockSpec(memory_space=pl.ANY)
    return pl.pallas_call(
        functools.partial(copy_kernel, count),
        out_shape=tuple(jax.ShapeDtypeStruct(a.shape, a.dtype) for a in arrays),
        in_specs=[any_spec] * count,
        out_specs=(any_spec,) * count,
        scratch_shapes=[pltpu.VMEM(a.shape, a.dtype) for a in arrays]
        + [pltpu.SemaphoreType.DMA((2, PARTS * count))],
        compiler_params=pltpu.CompilerParams(vmem_limit_bytes=60 * 1024 * 1024),
    )(*arrays)


def shards(
    tokens,
    cotangent,
    expert_ids,
    ada_shift,
    ada_scale,
    ada_gate,
    router_weight,
    gate_blocks,
    up_blocks,
    down_blocks,
):
    zn = lax.axis_size("exp")
    n = math.isqrt(lax.axis_size("seq") // 2)
    slots = n * n
    toks, width = tokens.shape
    experts = router_weight.shape[1]
    hidden = gate_blocks.shape[2]
    rows = slots * CAP
    cols_z = kb = width // zn
    nb = zn
    nt = -(-rows // 128)
    group = n * CAP
    dma = pltpu.SemaphoreType.DMA
    vm = pltpu.VMEM
    scratch = [
        vm((toks, width), BF16),
        vm((toks, width), BF16),
        vm((rows, toks), BF16),
        vm((slots, nb, 2 * CAP, kb), BF16),
        vm((n, nb, n, 2 * CAP, kb), BF16),
        vm((2, width, hidden), BF16),
        vm((2, width, hidden), BF16),
        vm((2, hidden, width), BF16),
        vm((rows, width), BF16),
        vm((rows, width), BF16),
        vm((rows, 4 * hidden), BF16),
        vm((rows, 2 * hidden), BF16),
        vm((nt * 128, hidden), F32),
        vm((group, 4 * hidden), F32),
        vm((group, 2 * hidden), F32),
        vm((n, 5, group, kb), BF16),
        vm((n, 5, group, kb), BF16),
        vm((n, 3, group, kb), F32),
        vm((2, toks, kb), BF16),
        vm((2, toks, kb), BF16),
        vm((slots, 3, 2 * CAP, kb // 2), BF16),
        vm((slots, 3, 2 * CAP, kb // 2), BF16),
        vm((3, toks, kb), F32),
        vm((8, 128), F32),
        vm((zn, 8, 128), F32),
        vm((8, 128), F32),
        vm((slots, 8, 128), F32),
        vm((8, 128), F32),
        vm((slots, 8, 128), F32),
        vm((nt * 128, 128), F32),
        vm((nb, kb, 2 * hidden), F32),
        vm((nb, kb, 2 * hidden), BF16),
        vm((nb, kb, 2 * hidden), BF16),
        vm((nb, hidden, kb), F32),
        vm((nb, hidden, kb), BF16),
        vm((nb, hidden, kb), BF16),
        vm((width, hidden), BF16),
        vm((width, hidden), BF16),
        vm((hidden, width), BF16),
        dma((3,)),
        vm((toks, 128), F32),
        vm((toks, 128), F32),
        vm((16, cols_z), F32),
        vm((16, cols_z), F32),
        vm((16, cols_z), F32),
        vm((n, 16, cols_z), F32),
        vm((16, cols_z), F32),
        vm((n, 16, cols_z), F32),
        vm((8, toks), F32),
        vm((zn, 8, toks), F32),
    ]
    sems = [3, 3, 3, (slots, 3), (slots, 3), (n, 5), (n, 5), (n, 5), (n, 5)]
    sems += [2, 2, (slots, 3), (slots, 3), slots, slots]
    sems += [zn, zn, slots, slots, nb, nb, nb, nb]
    sems += [1, 1, n, n, n, n, zn, zn]
    scratch += [dma(s if isinstance(s, tuple) else (s,)) for s in sems]
    any_spec = pl.BlockSpec(memory_space=pl.ANY)
    vm_spec = pl.BlockSpec(memory_space=pltpu.VMEM)
    row = lambda v: v.reshape(1, width)
    results = pl.pallas_call(
        functools.partial(expert_kernel, n, zn),
        out_shape=(
            jax.ShapeDtypeStruct((toks, cols_z), F32),
            jax.ShapeDtypeStruct((16, cols_z), F32),
            jax.ShapeDtypeStruct((1, width, hidden), BF16),
            jax.ShapeDtypeStruct((1, width, hidden), BF16),
            jax.ShapeDtypeStruct((1, hidden, width), BF16),
        ),
        in_specs=[vm_spec] * 7 + [any_spec] * 3,
        out_specs=(vm_spec,) * 2 + (any_spec,) * 3,
        scratch_shapes=scratch,
        compiler_params=pltpu.CompilerParams(
            collective_id=0, has_side_effects=True, vmem_limit_bytes=60 * 1024 * 1024
        ),
        cost_estimate=pl.CostEstimate(
            flops=16 * rows * width * 2 * hidden, bytes_accessed=16 * 1024 * 1024, transcendentals=0
        ),
    )(
        tokens,
        cotangent,
        expert_ids.T,
        row(ada_shift),
        row(ada_scale),
        row(ada_gate),
        router_weight.T,
        gate_blocks,
        up_blocks,
        down_blocks,
    )
    grad_input, router_t, grad_gate, grad_up, grad_down = place_results(results)
    return (grad_input, router_t[:experts].T, grad_gate, grad_up, grad_down)


def solution(mesh):
    in_specs = (
        P("seq", None),
        P("seq", None),
        P("seq", None),
        P(),
        P(),
        P(),
        P(),
        P(("seq", "exp"), None, None),
        P(("seq", "exp"), None, None),
        P(("seq", "exp"), None, None),
    )
    out_specs = (
        P("seq", "exp"),
        P("exp", None),
        P(("seq", "exp"), None, None),
        P(("seq", "exp"), None, None),
        P(("seq", "exp"), None, None),
    )
    return jax.shard_map(shards, mesh=mesh, in_specs=in_specs, out_specs=out_specs, check_vma=False)
```
